32 devices in a mesh: dp: 8 (over z, x), fsdp: 4 (over y, core).
Axes of the slice: x: 2, y: 2, z: 4, core: 2. Of those that a mesh axis runs over, the one named last changes fastest.
Arguments:
- doc_tokens: bfloat16 [8, 3072, 1024], P('dp', 'fsdp'), may hold values from -6 to 6
- query_tokens: bfloat16 [8, 4, 32, 1024], P('dp', 'fsdp'), may hold values from -6 to 6
- doc_lengths: int32 [8], P('dp'), may hold values from 64 to 3072, as said below
- labels: int32 [8, 4], replicated, may hold values from 0 to 7
- query_weight: bfloat16 [1024, 1024], P(('dp', 'fsdp')), may hold values from -0.1875 to 0.1875
- query_bias: bfloat16 [1024], P(('dp', 'fsdp')), may hold values from -1.75 to 1.75
- key_weight: bfloat16 [1024, 1024], P(('dp', 'fsdp')), may hold values from -0.1875 to 0.1875
- key_bias: bfloat16 [1024], P(('dp', 'fsdp')), may hold values from -1.75 to 1.75
- value_weight: bfloat16 [1024, 1024], P(('dp', 'fsdp')), may hold values from -0.1875 to 0.1875
- value_bias: bfloat16 [1024], P(('dp', 'fsdp')), may hold values from -1.75 to 1.75
- out_weight: bfloat16 [1024, 1024], P(('dp', 'fsdp')), may hold values from -0.75 to 0.75
- out_bias: bfloat16 [1024], P(('dp', 'fsdp')), may hold values from -1.75 to 1.75
- first_gain: bfloat16 [1024], P(('dp', 'fsdp')), may hold values from 0.5 to 1.5
- first_shift: bfloat16 [1024], P(('dp', 'fsdp')), may hold values from -1.75 to 1.75
- inner_weight: bfloat16 [1024, 4096], P(('dp', 'fsdp')), may hold values from -0.1875 to 0.1875
- inner_bias: bfloat16 [4096], P(('dp', 'fsdp')), may hold values from -1.75 to 1.75
- outer_weight: bfloat16 [4096, 1024], P(('dp', 'fsdp')), may hold values from -0.09375 to 0.09375
- outer_bias: bfloat16 [1024], P(('dp', 'fsdp')), may hold values from -1.75 to 1.75
- second_gain: bfloat16 [1024], P(('dp', 'fsdp')), may hold values from 0.5 to 1.5
- second_shift: bfloat16 [1024], P(('dp', 'fsdp')), may hold values from -1.75 to 1.75
- vector_weight: bfloat16 [1024, 128], P(('dp', 'fsdp')), may hold values from -0.1875 to 0.1875
Outputs:
- losses: float32 [3, 32], replicated
- doc_out: bfloat16 [8, 3072, 1024], P('dp', 'fsdp')
- query_out: bfloat16 [8, 4, 32, 1024], P('dp', 'fsdp')
- doc_grad: bfloat16 [8, 3072, 1024], P('dp', 'fsdp')
- query_grad: bfloat16 [8, 4, 32, 1024], P('dp', 'fsdp')
- query_weight_grad: float32 [1024, 1024], P(('dp', 'fsdp'))
- query_bias_grad: float32 [1024], P(('dp', 'fsdp'))
- key_weight_grad: float32 [1024, 1024], P(('dp', 'fsdp'))
- key_bias_grad: float32 [1024], P(('dp', 'fsdp'))
- value_weight_grad: float32 [1024, 1024], P(('dp', 'fsdp'))
- value_bias_grad: float32 [1024], P(('dp', 'fsdp'))
- out_weight_grad: float32 [1024, 1024], P(('dp', 'fsdp'))
- out_bias_grad: float32 [1024], P(('dp', 'fsdp'))
- first_gain_grad: float32 [1024], P(('dp', 'fsdp'))
- first_shift_grad: float32 [1024], P(('dp', 'fsdp'))
- inner_weight_grad: float32 [1024, 4096], P(('dp', 'fsdp'))
- inner_bias_grad: float32 [4096], P(('dp', 'fsdp'))
- outer_weight_grad: float32 [4096, 1024], P(('dp', 'fsdp'))
- outer_bias_grad: float32 [1024], P(('dp', 'fsdp'))
- second_gain_grad: float32 [1024], P(('dp', 'fsdp'))
- second_shift_grad: float32 [1024], P(('dp', 'fsdp'))
- vector_weight_grad: float32 [1024, 128], P(('dp', 'fsdp'))
The draws below stay inside these ranges and needn't reach their ends.
Inputs may be any that keep to these rules, and one draw needn't show every extreme that they name: `doc_lengths`: heavy-tailed lengths; one document of every draw has all 3072 positions valid and another exactly 64.
All inputs are finite; a program needn't handle non-finite values.
Results may differ from the reference program's by a relative error of at most 0.035.
Values may be sent and summed in bfloat16 or wider, within the bound.
A program may use at most 384 MiB of HBM per device.

```python
import jax
import jax.numpy as jnp
from jax import lax

D = 1024
HEADS = 16
HEAD_DIM = 64
FF = 4096
PROJ = 128
QLEN = 32
SEQ = 3072
QUERIES = 32
N_DP = 8
N_FSDP = 4


def draw_doc_lengths(key, part):
    key = jax.random.fold_in(key, 11)
    first_key, second_key, third_key, pick_key = jax.random.split(key, 4)
    span = SEQ - 64
    outer_cap = jax.random.randint(first_key, (N_DP,), 0, span + 1, dtype=jnp.int32)
    middle_cap = jax.random.randint(second_key, (N_DP,), 0, span + 1, dtype=jnp.int32) % (outer_cap + 1)
    extra = jax.random.randint(third_key, (N_DP,), 0, span + 1, dtype=jnp.int32) % (middle_cap + 1)
    drawn = (64 + extra).astype(jnp.int32)
    longest = jax.random.randint(pick_key, (), 0, N_DP, dtype=jnp.int32)
    shortest = (longest + 1) % N_DP
    index_row = jnp.arange(N_DP, dtype=jnp.int32)
    drawn = jnp.where(index_row == shortest, 64, drawn)
    return jnp.where(index_row == longest, SEQ, drawn).astype(jnp.int32)


def plant(result, rng, least, largest):
    shape = result.shape
    spot = [jax.random.randint(jax.random.fold_in(rng, axis), (), 0, shape[axis]) for axis in range(len(shape))]
    result = result.at[tuple(spot)].set(least)
    longest = shape.index(max(shape))
    spot[longest] = (spot[longest] + 1) % shape[longest]
    return result.at[tuple(spot)].set(largest)


def shard_levels(stream_key, extent, pieces, least, top_value):
    level = 1.0
    for axis_at, shards_of in pieces:
        draws = jax.random.uniform(jax.random.fold_in(jax.random.fold_in(stream_key, 6), axis_at), (shards_of,), jnp.float32, least / len(pieces), top_value / len(pieces))
        level = level * jnp.repeat(jnp.exp(draws), extent[axis_at] // shards_of).reshape((-1,) + (1,) * (len(extent) - 1 - axis_at))
    return level


def gaussian(own_key, shape, deviation, bound, shards=(), kind=jnp.bfloat16):
    values = deviation * jax.random.normal(own_key, shape, jnp.float32)
    if shards:
        values = values * shard_levels(own_key, shape, shards, -0.22, 0.18)
    return jnp.clip(values, -bound, bound).astype(kind)


def setup_inputs(seed: int = 0) -> dict:
    splits = jax.random.split(jax.random.key(seed), 22)
    return {
        "doc_tokens": gaussian(splits[0], (N_DP, SEQ, D), 1.0, 6.0, ((0, 8), (1, 4))),
        "query_tokens": gaussian(splits[1], (N_DP, N_FSDP, QLEN, D), 1.0, 6.0, ((0, 8), (1, 4))),
        "doc_lengths": draw_doc_lengths(jax.random.fold_in(splits[21], 71), 0),
        "labels": plant(jax.random.randint(splits[3], (N_DP, N_FSDP), 0, N_DP), jax.random.fold_in(splits[3], 1), 0, N_DP - 1).astype(jnp.int32),
        "query_weight": gaussian(splits[4], (D, D), D ** -0.5, 0.1875, ((0, 32),)),
        "query_bias": gaussian(splits[5], (D,), 0.3, 1.75, ((0, 32),)),
        "key_weight": gaussian(splits[6], (D, D), D ** -0.5, 0.1875, ((0, 32),)),
        "key_bias": gaussian(splits[7], (D,), 0.3, 1.75, ((0, 32),)),
        "value_weight": gaussian(splits[8], (D, D), D ** -0.5, 0.1875, ((0, 32),)),
        "value_bias": gaussian(splits[9], (D,), 0.3, 1.75, ((0, 32),)),
        "out_weight": gaussian(splits[10], (D, D), (D // 16) ** -0.5, 0.75, ((0, 32),)),
        "out_bias": gaussian(splits[11], (D,), 0.3, 1.75, ((0, 32),)),
        "first_gain": jnp.clip(1.0 + 0.1 * jax.random.normal(splits[12], (D,), jnp.float32), 0.5, 1.5).astype(jnp.bfloat16),
        "first_shift": gaussian(splits[13], (D,), 0.3, 1.75, ((0, 32),)),
        "inner_weight": gaussian(splits[14], (D, FF), D ** -0.5, 0.1875, ((0, 32),)),
        "inner_bias": gaussian(splits[15], (FF,), 0.3, 1.75, ((0, 32),)),
        "outer_weight": gaussian(splits[16], (FF, D), FF ** -0.5, 0.09375, ((0, 32),)),
        "outer_bias": gaussian(splits[17], (D,), 0.3, 1.75, ((0, 32),)),
        "second_gain": jnp.clip(1.0 + 0.1 * jax.random.normal(splits[18], (D,), jnp.float32), 0.5, 1.5).astype(jnp.bfloat16),
        "second_shift": gaussian(splits[19], (D,), 0.3, 1.75, ((0, 32),)),
        "vector_weight": gaussian(splits[20], (D, PROJ), D ** -0.5, 0.1875, ((0, 32),)),
    }


@jax.custom_vjp
def low(v):
    return lax.optimization_barrier(v.astype(jnp.bfloat16)).astype(jnp.float32)

@jax.custom_vjp
def low_back(v):
    return v

def low_keep(v):
    return (low(v), None)

def low_pass(kept, grad):
    return (grad,)

def back_keep(v):
    return (v, None)

def back_low(kept, grad):
    return (low(grad),)
low.defvjp(low_keep, low_pass)
low_back.defvjp(back_keep, back_low)
norm_eps = 1e-05
vector_eps = 1e-06
rope_base = 10000.0
smooth_temp = 0.05
loss_temp = 0.02
masked_score = -1e+30

def matmul(left, right):
    return jnp.dot(left, right, precision=lax.Precision.HIGHEST)

def rotate(flat_rows, positions):
    row_count = flat_rows.shape[0]
    by_head = flat_rows.reshape(row_count, -1, HEAD_DIM)
    half_dim = HEAD_DIM // 2
    frequency = rope_base ** (-jnp.arange(half_dim, dtype=jnp.float32) / half_dim)
    angles = positions.astype(jnp.float32)[:, None] * frequency[None, :]
    cosine = jnp.cos(angles)[:, None, :]
    sine_part = jnp.sin(angles)[:, None, :]
    leading = by_head[..., :half_dim]
    trailing = by_head[..., half_dim:]
    turned = jnp.concatenate([leading * cosine - trailing * sine_part, trailing * cosine + leading * sine_part], axis=-1)
    return turned.reshape(row_count, -1)

def layer_norm(summed, gain_row, shift_row):
    centered = summed - lax.optimization_barrier(jnp.mean(summed, axis=-1, keepdims=True))
    variance = lax.optimization_barrier(jnp.mean(centered * centered, axis=-1, keepdims=True))
    return centered * lax.rsqrt(variance + norm_eps) * gain_row + shift_row

def attend(query_rows, key_rows, value_rows, allowed):
    row_count = query_rows.shape[0]
    key_count = key_rows.shape[0]
    query_heads = query_rows.reshape(row_count, HEADS, HEAD_DIM)
    key_heads = key_rows.reshape(key_count, HEADS, HEAD_DIM)
    value_heads = value_rows.reshape(key_count, HEADS, HEAD_DIM)
    raw_scores = jnp.einsum('rhd,khd->hrk', query_heads, key_heads, precision=lax.Precision.HIGHEST)
    scaled = jnp.where(allowed[None, None, :], low_back(raw_scores) * HEAD_DIM ** (-0.5), masked_score)
    softmax_rows = jax.nn.softmax(scaled, axis=-1)
    mixed_heads = jnp.einsum('hrk,khd->rhd', low(softmax_rows), value_heads, precision=lax.Precision.HIGHEST)
    return mixed_heads.reshape(row_count, HEADS * HEAD_DIM)

def layer(params, rows_in, positions, attend_rows):
    query_mat, query_vec, key_mat, key_vec, value_mat, value_vec, out_mat, out_vec, gain_one, shift_one, inner_mat, inner_vec, outer_mat, outer_vec, gain_two, shift_two, vector_mat = params
    query_low = low(rotate(low_back(matmul(rows_in, query_mat) + query_vec), positions))
    key_low = low(rotate(low_back(matmul(rows_in, key_mat) + key_vec), positions))
    value_low = low(low_back(matmul(rows_in, value_mat) + value_vec))
    attended = low(low_back(attend_rows(query_low, key_low, value_low)))
    normed_one = layer_norm(rows_in + low_back(matmul(attended, out_mat) + out_vec), gain_one, shift_one)
    inner = low_back(matmul(low(normed_one), inner_mat) + inner_vec)
    activ = low(jax.nn.gelu(inner, approximate=False))
    normed_two = layer_norm(normed_one + low_back(matmul(activ, outer_mat) + outer_vec), gain_two, shift_two)
    encoded = low(normed_two)
    projected = low_back(matmul(encoded, vector_mat))
    return (encoded, projected)

def normalize(projected):
    result_list = []
    for columns in (PROJ, PROJ * 3 // 4, PROJ // 2):
        leading = projected[:, :columns]
        result_list.append(leading * lax.rsqrt(lax.optimization_barrier(jnp.sum(leading * leading, axis=-1, keepdims=True)) + vector_eps))
    return result_list

def maxsim(query_vec, doc_vec, allowed):
    similar = low_back(matmul(query_vec, doc_vec.T))
    smooth = jnp.where(allowed[None, :], similar / smooth_temp, masked_score)
    token_max = jax.nn.logsumexp(smooth, axis=-1)
    return smooth_temp * lax.optimization_barrier(jnp.mean(token_max.reshape(QUERIES, QLEN), axis=-1))

def document_pass(params, query_vectors, doc_rows, length):
    positions = jnp.arange(SEQ, dtype=jnp.int32)
    allowed = positions < length
    block_rows = min(512, SEQ)

    def attend_rows(query_low, key_low, value_low):
        blocked = query_low.reshape(SEQ // block_rows, block_rows, HEADS * HEAD_DIM)
        one_block = jax.checkpoint(lambda rows_here: attend(rows_here, key_low, value_low, allowed))
        return lax.map(one_block, blocked).reshape(SEQ, HEADS * HEAD_DIM)
    encoded, projected = layer(params, doc_rows, positions, attend_rows)
    doc_vectors = [low(entry) for entry in normalize(projected)]
    scores = jnp.stack([maxsim(query_vec, doc_vec, allowed) for query_vec, doc_vec in zip(query_vectors, doc_vectors)])
    return (scores, encoded)

def forward(params, doc_rows, query_rows, lengths, labels):
    query_flat = query_rows.reshape(QUERIES * QLEN, D)
    query_pos = jnp.tile(jnp.arange(QLEN, dtype=jnp.int32), QUERIES)
    every_key = jnp.ones((QLEN,), dtype=jnp.bool_)

    def attend_queries(query_low, key_low, value_low):
        shaped_q = query_low.reshape(QUERIES, QLEN, D)
        shaped_k = key_low.reshape(QUERIES, QLEN, D)
        shaped_v = value_low.reshape(QUERIES, QLEN, D)
        joined = jax.vmap(lambda a, b, c: attend(a, b, c, every_key))(shaped_q, shaped_k, shaped_v)
        return joined.reshape(QUERIES * QLEN, D)
    query_out, query_proj = layer(params, query_flat, query_pos, attend_queries)
    query_vectors = [low(entry) for entry in normalize(query_proj)]
    step_fn = jax.checkpoint(lambda doc_item: document_pass(params, query_vectors, doc_item[0], doc_item[1]))
    scores, doc_out = lax.map(step_fn, (doc_rows, lengths))
    logits = jnp.transpose(scores, (1, 2, 0)) / loss_temp
    chosen = labels.reshape(-1)[:, None] == jnp.arange(N_DP, dtype=jnp.int32)[None, :]
    picked = lax.optimization_barrier(jnp.sum(jnp.where(chosen[None], logits, 0.0), axis=-1))
    losses = jax.nn.logsumexp(logits, axis=-1) - picked
    return (losses, (doc_out, query_out.reshape(N_DP, N_FSDP, QLEN, D)))

def reference(doc_tokens, query_tokens, doc_lengths, labels, query_weight, query_bias, key_weight, key_bias, value_weight, value_bias, out_weight, out_bias, first_gain, first_shift, inner_weight, inner_bias, outer_weight, outer_bias, second_gain, second_shift, vector_weight):
    params = tuple((entry.astype(jnp.float32) for entry in (query_weight, query_bias, key_weight, key_bias, value_weight, value_bias, out_weight, out_bias, first_gain, first_shift, inner_weight, inner_bias, outer_weight, outer_bias, second_gain, second_shift, vector_weight)))

    def wrapped(weights, doc_rows, query_rows):
        return forward(weights, doc_rows, query_rows, doc_lengths, labels)
    losses, backward_fn, outputs = jax.vjp(wrapped, params, doc_tokens.astype(jnp.float32), query_tokens.astype(jnp.float32), has_aux=True)
    weight_grads, doc_grad, query_grad = backward_fn(jnp.ones_like(losses))
    doc_out, query_out = outputs
    return (losses, doc_out.astype(jnp.bfloat16), query_out.astype(jnp.bfloat16), doc_grad.astype(jnp.bfloat16), query_grad.astype(jnp.bfloat16), weight_grads[0], weight_grads[1], weight_grads[2], weight_grads[3], weight_grads[4], weight_grads[5], weight_grads[6], weight_grads[7], weight_grads[8], weight_grads[9], weight_grads[10], weight_grads[11], weight_grads[12], weight_grads[13], weight_grads[14], weight_grads[15], weight_grads[16])
```

```python
import functools
import math

import jax
import jax.numpy as jnp
import numpy as np
from jax import lax
from jax.experimental import pallas as pl
from jax.experimental.pallas import tpu as pltpu
from jax.sharding import PartitionSpec as P

D = 1024
HEAD_DIM = 64
PROJ = 128
QLEN = 32
LANES = 128

norm_eps = 1e-05
vector_eps = 1e-06
rope_base = 10000.0
smooth_temp = 0.05
loss_temp = 0.02
masked_score = -1e30
log2e = math.log2(math.e)
AXES = ("dp", "fsdp")
BF = jnp.bfloat16
F32 = jnp.float32
VMEM_MOST = 60 << 20


def dot_nn(left, right):
    return lax.dot_general(left, right, (((1,), (0,)), ((), ())), preferred_element_type=F32)


def dot_nt(left, right):
    return lax.dot_general(left, right, (((1,), (1,)), ((), ())), preferred_element_type=F32)


def dot_tn(left, right):
    return lax.dot_general(left, right, (((0,), (0,)), ((), ())), preferred_element_type=F32)


def lanes_of(shape):
    return lax.broadcasted_iota(jnp.int32, shape, len(shape) - 1)


def split_three(value):
    high = value.astype(BF)
    rest = value - high.astype(F32)
    middle = rest.astype(BF)
    return high, middle, (rest - middle.astype(F32)).astype(BF)


def params(**more):
    return pltpu.CompilerParams(vmem_limit_bytes=VMEM_MOST, **more)


def rope_tables(parts, doc_rows):
    half_dim = HEAD_DIM // 2
    frequency = rope_base ** (-np.arange(half_dim, dtype=np.float64) / half_dim)
    own = [
        np.concatenate([part * doc_rows + np.arange(doc_rows), np.arange(QLEN)])
        for part in range(parts)
    ]
    angles = np.concatenate(own)[:, None] * frequency[None, :]
    cosine, sine = np.cos(angles), np.sin(angles)
    shape = (parts, doc_rows + QLEN, LANES)
    return (
        np.concatenate([cosine] * 4, axis=1).astype(np.float32).reshape(shape),
        np.concatenate([-sine, sine, -sine, sine], axis=1).astype(np.float32).reshape(shape),
    )


def turn(tile, cosine, sine):
    first = lanes_of(tile.shape) % HEAD_DIM < HEAD_DIM // 2
    partner = jnp.where(first, pltpu.roll(tile, LANES - 32, 1), pltpu.roll(tile, 32, 1))
    return tile * cosine + partner * sine


def heads_kernel(doc_rows, len_ref, x_ref, w_ref, b_ref, cos_ref, sin_ref, q_ref, k_ref, v_ref):
    part = pl.program_id(0)
    rows = x_ref.shape[1]
    cosine, sine = cos_ref[0], sin_ref[0]
    lane = lanes_of((rows, LANES))
    row = lax.broadcasted_iota(jnp.int32, (rows, LANES), 0)
    allowed = (row >= doc_rows) | (part * doc_rows + row < len_ref[0])
    mask = jnp.where(allowed, 0.0, masked_score)
    width = w_ref.shape[1] // 3
    line = dot_nn(x_ref[0], w_ref[...]) + b_ref[...]
    for pair in range(width // LANES):
        here = pair * LANES
        query = turn(line[:, here : here + LANES], cosine, sine) * (log2e * HEAD_DIM**-0.5)
        key = turn(line[:, width + here : width + here + LANES], cosine, sine)
        value = line[:, 2 * width + here : 2 * width + here + LANES]
        for half in range(2):
            if half:
                query, key, value = (pltpu.roll(entry, 64, 1) for entry in (query, key, value))
            q_ref[2 * pair + half] = jnp.where(
                lane < 64, query, jnp.where(lane == 64, 1.0, 0.0)
            ).astype(BF)
            k_ref[2 * pair + half] = jnp.where(
                lane < 64, key, jnp.where(lane == 64, mask, jnp.where(lane < 68, 1.0, 0.0))
            ).astype(BF)
            v_ref[2 * pair + half] = jnp.where(
                lane < 64, value, jnp.where(lane < 67, 1.0, 0.0)
            ).astype(BF)


def project_heads(length, x_all, w_heads, b_heads, cosine, sine, doc_rows):
    parts, rows, _ = x_all.shape
    heads = w_heads.shape[1] // 3 // HEAD_DIM
    block = pl.BlockSpec((heads, rows, LANES), lambda part: (0, part, 0))
    shape = jax.ShapeDtypeStruct((heads, parts * rows, LANES), BF)
    table = pl.BlockSpec((1, rows, LANES), lambda part: (part, 0, 0))
    return pl.pallas_call(
        functools.partial(heads_kernel, doc_rows),
        grid=(parts,),
        in_specs=[
            pl.BlockSpec(memory_space=pltpu.SMEM),
            pl.BlockSpec((1, rows, D), lambda part: (part, 0, 0)),
            pl.BlockSpec(w_heads.shape, lambda part: (0, 0)),
            pl.BlockSpec(b_heads.shape, lambda part: (0, 0)),
            table,
            table,
        ],
        out_specs=[block] * 3,
        out_shape=[shape] * 3,
        compiler_params=params(),
        name="project_heads",
    )(length, x_all, w_heads, b_heads, cosine, sine)


def attend_rows(query, chunks):
    largest = jnp.full((query.shape[0], 1), -1e38, F32)
    total = jnp.zeros((query.shape[0], LANES), F32)
    for key, value in chunks:
        scores = dot_nt(query, key())
        newest = jnp.maximum(largest, jnp.max(scores, axis=1, keepdims=True))
        powers = jnp.exp2(scores - newest).astype(BF)
        total = total * jnp.exp2(largest - newest) + dot_nn(powers, value())
        largest = newest
    row_sum = total[:, 64:65]
    return total / row_sum, largest + jnp.log2(row_sum)


def attend_kernel(
    doc_rows, parts, q_ref, k_ref, v_ref, ko_ref, vo_ref, o_ref, full_ref, qa_ref
):
    rows = doc_rows + QLEN
    for span, own in ((slice(0, doc_rows), False), (slice(doc_rows, rows), True)):
        mixed = []
        for head in range(2):
            query = q_ref[head, span, :]
            lane = lanes_of(query.shape)
            if own:
                chunks = [(lambda: ko_ref[head], lambda: vo_ref[head])]
            else:
                chunks = [
                    (
                        lambda part=part: k_ref[head, part * rows : part * rows + doc_rows, :],
                        lambda part=part: v_ref[head, part * rows : part * rows + doc_rows, :],
                    )
                    for part in range(parts)
                ]
            out, log_sum = attend_rows(query, chunks)
            mixed.append(out)
            high, middle, low = split_three(-log_sum)
            qa_ref[head, span, :] = jnp.where(
                lane == 65,
                high,
                jnp.where(lane == 66, middle, jnp.where(lane == 67, low, query)),
            )
        joined = jnp.where(lanes_of(mixed[0].shape) < 64, mixed[0], pltpu.roll(mixed[1], 64, 1))
        full_ref[0, span, :] = joined
        o_ref[0, span, :] = joined.astype(BF)


def attend(query, key, value, parts, doc_rows):
    heads, total, _ = query.shape
    rows = total // parts
    own_at = rows // QLEN
    mine = pl.BlockSpec((2, rows, LANES), lambda pair, part: (pair, part, 0))
    whole = pl.BlockSpec((2, total, LANES), lambda pair, part: (pair, 0, 0))
    own = pl.BlockSpec((2, QLEN, LANES), lambda pair, part: (pair, part * own_at + own_at - 1, 0))
    flat = pl.BlockSpec((1, rows, LANES), lambda pair, part: (part, 0, pair))
    flops = 4 * heads * total * total * 256
    return pl.pallas_call(
        functools.partial(attend_kernel, doc_rows, parts),
        grid=(heads // 2, parts),
        in_specs=[mine, whole, whole, own, own],
        out_specs=[flat, flat, mine],
        out_shape=[
            jax.ShapeDtypeStruct((parts, rows, heads * HEAD_DIM), BF),
            jax.ShapeDtypeStruct((parts, rows, heads * HEAD_DIM), F32),
            jax.ShapeDtypeStruct(query.shape, BF),
        ],
        compiler_params=params(),
        cost_estimate=pl.CostEstimate(flops=flops, bytes_accessed=1 << 24, transcendentals=0),
        name="attend",
    )(query, key, value, key, value)


def attend_back_kernel(
    doc_rows,
    parts,
    q_ref,
    k_ref,
    v_ref,
    ko_ref,
    vo_ref,
    do_ref,
    o_ref,
    cos_ref,
    sin_ref,
    dq_ref,
    dk_ref,
    dv_ref,
    dk_doc,
    dv_doc,
    dk_own,
    dv_own,
):
    rows = doc_rows + QLEN
    at = pl.program_id(1)

    @pl.when(at == 0)
    def _():
        dk_doc[...] = jnp.zeros_like(dk_doc)
        dv_doc[...] = jnp.zeros_like(dv_doc)

    for span, own in ((slice(0, doc_rows), False), (slice(doc_rows, rows), True)):
        grad_pair = do_ref[0, span, :]
        lane = lanes_of(grad_pair.shape)
        product = grad_pair.astype(F32) * o_ref[0, span, :]
        turned = pltpu.roll(grad_pair.astype(F32), 64, 1).astype(BF)
        pieces = []
        for head in range(2):
            query = q_ref[head, span, :]
            inside = lane < 64 if head == 0 else lane >= 64
            row_dot = jnp.sum(jnp.where(inside, product, 0.0), axis=1, keepdims=True)
            high, middle, low = split_three(-row_dot)
            grad = jnp.where(
                lane < 64,
                turned if head else grad_pair,
                jnp.where(
                    lane == 64,
                    high,
                    jnp.where(
                        lane == 65, middle, jnp.where(lane == 66, low, jnp.zeros_like(grad_pair))
                    ),
                ),
            )
            query_t, grad_t = query.T, grad.T
            grad_query = jnp.zeros(query.shape, F32)
            for part in range(1 if own else parts):
                if own:
                    key, value = ko_ref[head], vo_ref[head]
                else:
                    key = k_ref[head, part * rows : part * rows + doc_rows, :]
                    value = v_ref[head, part * rows : part * rows + doc_rows, :]
                powers = jnp.exp2(dot_nt(query, key))
                grad_scores = (powers * dot_nt(grad, value)).astype(BF)
                if own:
                    dv_own[head, at] = dot_nn(grad_t, powers.astype(BF))
                    dk_own[head, at] = dot_nn(query_t, grad_scores)
                else:
                    dv_doc[head, part] += dot_nn(grad_t, powers.astype(BF))
                    dk_doc[head, part] += dot_nn(query_t, grad_scores)
                grad_query += dot_nn(grad_scores, key)
            pieces.append(grad_query)
        joined = jnp.where(lane < 64, pieces[0], pltpu.roll(pieces[1], 64, 1)) * HEAD_DIM**-0.5
        dq_ref[0, span, :] = turn(joined, cos_ref[at, span, :], -sin_ref[at, span, :]).astype(BF)

    @pl.when(at == parts - 1)
    def _():
        def both(kept, part):
            first, second = kept[0, part].T, kept[1, part].T
            return jnp.where(lanes_of(first.shape) < 64, first, pltpu.roll(second, 64, 1))

        for part in range(parts):
            for span, keys, values in (
                (slice(0, doc_rows), dk_doc, dv_doc),
                (slice(doc_rows, rows), dk_own, dv_own),
            ):
                grad_key = both(keys, part) * (1.0 / log2e)
                dk_ref[part, span, :] = turn(
                    grad_key, cos_ref[part, span, :], -sin_ref[part, span, :]
                ).astype(BF)
                dv_ref[part, span, :] = both(values, part).astype(BF)


def attend_back(query, key, value, grad, mixed, cosine, sine, doc_rows):
    heads, total, _ = query.shape
    parts, rows, width = grad.shape
    own_at = rows // QLEN
    mine = pl.BlockSpec((2, rows, LANES), lambda pair, part: (pair, part, 0))
    whole = pl.BlockSpec((2, total, LANES), lambda pair, part: (pair, 0, 0))
    own = pl.BlockSpec((2, QLEN, LANES), lambda pair, part: (pair, part * own_at + own_at - 1, 0))
    flat = pl.BlockSpec((1, rows, LANES), lambda pair, part: (part, 0, pair))
    full = pl.BlockSpec((parts, rows, LANES), lambda pair, part: (0, 0, pair))
    table = pl.BlockSpec((parts, rows, LANES), lambda pair, part: (0, 0, 0))
    shape = jax.ShapeDtypeStruct(grad.shape, BF)
    return pl.pallas_call(
        functools.partial(attend_back_kernel, doc_rows, parts),
        grid=(heads // 2, parts),
        in_specs=[mine, whole, whole, own, own, flat, flat, table, table],
        out_specs=[flat, full, full],
        out_shape=[shape] * 3,
        scratch_shapes=[
            pltpu.VMEM((2, parts, LANES, doc_rows), F32),
            pltpu.VMEM((2, parts, LANES, doc_rows), F32),
            pltpu.VMEM((2, parts, LANES, QLEN), F32),
            pltpu.VMEM((2, parts, LANES, QLEN), F32),
        ],
        compiler_params=params(),
        cost_estimate=pl.CostEstimate(
            flops=10 * heads * total * total * 256, bytes_accessed=1 << 24, transcendentals=0
        ),
        name="attend_back",
    )(query, key, value, key, value, grad, mixed, cosine, sine)


def normed(summed):
    centered = summed - jnp.mean(summed, axis=-1, keepdims=True)
    variance = jnp.mean(centered * centered, axis=-1, keepdims=True)
    inverse = lax.rsqrt(variance + norm_eps)
    return centered * inverse, inverse


def rows_kernel(
    att_ref,
    x_ref,
    wo_ref,
    wi_ref,
    wu_ref,
    wv_ref,
    bi_ref,
    vec_ref,
    hat1_ref,
    inv1_ref,
    low1_ref,
    act_ref,
    slope_ref,
    hat2_ref,
    inv2_ref,
    enc_ref,
    proj_ref,
    sum_ref,
):
    step = pl.program_id(0)
    parts, _, width = att_ref.shape

    @pl.when(step == 0)
    def _():
        summed = x_ref[...].astype(F32) + vec_ref[0:1, :]
        for part in range(parts):
            summed += dot_nn(att_ref[part], wo_ref[part * width : (part + 1) * width, :])
        hat, inverse = normed(summed)
        hat1_ref[...] = hat.astype(BF)
        inv1_ref[...] = jnp.broadcast_to(inverse, inv1_ref.shape)
        out = hat * vec_ref[1:2, :] + vec_ref[2:3, :]
        low1_ref[...] = out.astype(BF)
        sum_ref[...] = out + vec_ref[3:4, :]

    inner = dot_nn(low1_ref[...], wi_ref[...]) + bi_ref[...]
    share = 0.5 * lax.erf(inner * math.sqrt(0.5)) + 0.5
    act = (inner * share).astype(BF)
    act_ref[...] = act
    density = jnp.exp(inner * inner * -0.5) * (1.0 / math.sqrt(2.0 * math.pi))
    slope_ref[...] = (share + inner * density).astype(BF)
    sum_ref[...] += dot_nn(act, wu_ref[...])

    @pl.when(step == pl.num_programs(0) - 1)
    def _():
        hat, inverse = normed(sum_ref[...])
        hat2_ref[...] = hat.astype(BF)
        inv2_ref[...] = jnp.broadcast_to(inverse, inv2_ref.shape)
        low = (hat * vec_ref[4:5, :] + vec_ref[5:6, :]).astype(BF)
        enc_ref[...] = low
        proj_ref[...] = dot_nn(low, wv_ref[...])


def rows_forward(att, rows_in, wo, wi, wu, wv, inner_bias, vectors):
    rows = rows_in.shape[0]
    hidden = wi.shape[1]
    chunk = 512
    keep = lambda shape: pl.BlockSpec(shape, lambda step: (0,) * len(shape))
    columns = pl.BlockSpec((rows, chunk), lambda step: (0, step))
    wide = jax.ShapeDtypeStruct((rows, D), BF)
    thin = jax.ShapeDtypeStruct((rows, LANES), F32)
    big = jax.ShapeDtypeStruct((rows, hidden), BF)
    return pl.pallas_call(
        rows_kernel,
        grid=(hidden // chunk,),
        in_specs=[
            keep(att.shape),
            keep(rows_in.shape),
            keep(wo.shape),
            pl.BlockSpec((D, chunk), lambda step: (0, step)),
            pl.BlockSpec((chunk, D), lambda step: (step, 0)),
            keep(wv.shape),
            pl.BlockSpec((1, chunk), lambda step: (0, step)),
            keep(vectors.shape),
        ],
        out_specs=[
            keep((rows, D)),
            keep((rows, LANES)),
            keep((rows, D)),
            columns,
            columns,
            keep((rows, D)),
            keep((rows, LANES)),
            keep((rows, D)),
            keep((rows, LANES)),
        ],
        out_shape=[wide, thin, wide, big, big, wide, thin, wide, thin],
        scratch_shapes=[pltpu.VMEM((rows, D), F32)],
        compiler_params=params(),
        cost_estimate=pl.CostEstimate(
            flops=2 * rows * D * (D + 2 * hidden), bytes_accessed=1 << 25, transcendentals=0
        ),
        name="rows_forward",
    )(att, rows_in, wo, wi, wu, wv, inner_bias, vectors)


def norm_back(grad, hat, inverse, gain):
    scaled = grad * gain
    first = jnp.mean(scaled, axis=-1, keepdims=True)
    second = jnp.mean(scaled * hat, axis=-1, keepdims=True)
    return (scaled - first - hat * second) * inverse


def column_sum(value):
    return jnp.sum(value, axis=0, keepdims=True)


def rows_back_kernel(
    dproj_ref,
    enc_ref,
    hat2_ref,
    inv2_ref,
    wv_ref,
    act_ref,
    slope_ref,
    wu_ref,
    wi_ref,
    low1_ref,
    hat1_ref,
    inv1_ref,
    att_ref,
    wo_ref,
    vec_ref,
    dwv_ref,
    dwu_ref,
    dwi_ref,
    dbi_ref,
    dwo_ref,
    datt_ref,
    dsum_ref,
    dvec_ref,
    low_ref,
    total_ref,
):
    step = pl.program_id(0)
    parts, _, width = att_ref.shape

    @pl.when(step == 0)
    def _():
        dproj = dproj_ref[...]
        dwv_ref[...] = dot_tn(enc_ref[...], dproj).astype(BF)
        grad = dot_nt(dproj, wv_ref[...])
        hat = hat2_ref[...].astype(F32)
        dvec_ref[4:5, :] = column_sum(grad * hat)
        dvec_ref[5:6, :] = column_sum(grad)
        back = norm_back(grad, hat, inv2_ref[:, :1], vec_ref[4:5, :])
        low = back.astype(BF)
        low_ref[...] = low
        total_ref[...] = back
        dvec_ref[3:4, :] = column_sum(low.astype(F32))

    low = low_ref[...]
    dinner = (dot_nt(low, wu_ref[...]) * slope_ref[...].astype(F32)).astype(BF)
    dbi_ref[...] = column_sum(dinner.astype(F32))
    dwu_ref[...] = dot_tn(act_ref[...], low).astype(BF)
    dwi_ref[...] = dot_tn(low1_ref[...], dinner).astype(BF)
    total_ref[...] += dot_nt(dinner, wi_ref[...])

    @pl.when(step == pl.num_programs(0) - 1)
    def _():
        grad = total_ref[...]
        hat = hat1_ref[...].astype(F32)
        dvec_ref[1:2, :] = column_sum(grad * hat)
        dvec_ref[2:3, :] = column_sum(grad)
        back = norm_back(grad, hat, inv1_ref[:, :1], vec_ref[1:2, :])
        dsum_ref[...] = back
        attn_low = back.astype(BF)
        dvec_ref[0:1, :] = column_sum(attn_low.astype(F32))
        for part in range(parts):
            here = slice(part * width, (part + 1) * width)
            dwo_ref[here, :] = dot_tn(att_ref[part], attn_low).astype(BF)
            datt_ref[part] = dot_nt(attn_low, wo_ref[here, :]).astype(BF)


def rows_backward(
    dproj, enc, hat2, inv2, wv, act, slope, wu, wi, low1, hat1, inv1, att, wo, vectors
):
    rows, hidden = act.shape
    chunk = 512
    keep = lambda shape: pl.BlockSpec(shape, lambda step: (0,) * len(shape))
    columns = pl.BlockSpec((rows, chunk), lambda step: (0, step))
    up = pl.BlockSpec((chunk, D), lambda step: (step, 0))
    down = pl.BlockSpec((D, chunk), lambda step: (0, step))
    bias = pl.BlockSpec((1, chunk), lambda step: (0, step))
    operands = (dproj, enc, hat2, inv2, wv, act, slope, wu, wi, low1, hat1, inv1, att, wo, vectors)
    special = {5: columns, 6: columns, 7: up, 8: down}
    return pl.pallas_call(
        rows_back_kernel,
        grid=(hidden // chunk,),
        in_specs=[special.get(i, keep(entry.shape)) for i, entry in enumerate(operands)],
        out_specs=[
            keep(wv.shape),
            up,
            down,
            bias,
            keep(wo.shape),
            keep(att.shape),
            keep((rows, D)),
            keep((8, D)),
        ],
        out_shape=[
            jax.ShapeDtypeStruct(wv.shape, BF),
            jax.ShapeDtypeStruct(wu.shape, BF),
            jax.ShapeDtypeStruct(wi.shape, BF),
            jax.ShapeDtypeStruct((1, hidden), F32),
            jax.ShapeDtypeStruct(wo.shape, BF),
            jax.ShapeDtypeStruct(att.shape, BF),
            jax.ShapeDtypeStruct((rows, D), F32),
            jax.ShapeDtypeStruct((8, D), F32),
        ],
        scratch_shapes=[pltpu.VMEM((rows, D), BF), pltpu.VMEM((rows, D), F32)],
        compiler_params=params(),
        cost_estimate=pl.CostEstimate(
            flops=4 * rows * D * (D + 2 * hidden), bytes_accessed=1 << 26, transcendentals=0
        ),
        name="rows_backward",
    )(*operands)


def heads_back_kernel(x_ref, dq_ref, dk_ref, dv_ref, w_ref, dx_ref, dw_ref, db_ref, acc_ref):
    part = pl.program_id(0)
    width = dq_ref.shape[2]

    @pl.when(part == 0)
    def _():
        acc_ref[...] = jnp.zeros_like(acc_ref)
        db_ref[...] = jnp.zeros_like(db_ref)

    total = None
    for index, ref in enumerate((dq_ref, dk_ref, dv_ref)):
        here = slice(index * width, (index + 1) * width)
        grad = ref[0]
        term = dot_nt(grad, w_ref[:, here])
        total = term if total is None else total + term
        acc_ref[:, here] += dot_tn(x_ref[0], grad)
        db_ref[:, here] += column_sum(grad.astype(F32))
    dx_ref[0] = total.astype(BF)

    @pl.when(part == pl.num_programs(0) - 1)
    def _():
        dw_ref[...] = acc_ref[...].astype(BF)


def heads_backward(x_all, dq, dk, dv, w_heads):
    parts, rows, width = dq.shape
    flat = pl.BlockSpec((1, rows, width), lambda part: (part, 0, 0))
    wide = pl.BlockSpec((1, rows, D), lambda part: (part, 0, 0))
    return pl.pallas_call(
        heads_back_kernel,
        grid=(parts,),
        in_specs=[wide, flat, flat, flat, pl.BlockSpec(w_heads.shape, lambda part: (0, 0))],
        out_specs=[
            wide,
            pl.BlockSpec(w_heads.shape, lambda part: (0, 0)),
            pl.BlockSpec((1, 3 * width), lambda part: (0, 0)),
        ],
        out_shape=[
            jax.ShapeDtypeStruct(x_all.shape, BF),
            jax.ShapeDtypeStruct(w_heads.shape, BF),
            jax.ShapeDtypeStruct((1, 3 * width), F32),
        ],
        scratch_shapes=[pltpu.VMEM(w_heads.shape, F32)],
        compiler_params=params(),
        name="heads_backward",
    )(x_all, dq, dk, dv, w_heads)


class Exchange:
    def __init__(self, axis, size, send, recv):
        self.axis, self.size, self.send, self.recv = axis, size, send, recv
        self.me = lax.axis_index(axis)
        self.going = []

    def to(self, offset):
        return lax.rem(self.me + offset, self.size)

    def source(self, offset):
        return lax.rem(self.me - offset + self.size, self.size)

    def start(self, source_of, target_of):
        for offset in range(1, self.size):
            partner = self.to(offset)
            copy = pltpu.make_async_remote_copy(
                src_ref=source_of(partner),
                dst_ref=target_of(offset),
                send_sem=self.send.at[offset - 1],
                recv_sem=self.recv.at[offset - 1],
                device_id={self.axis: partner},
                device_id_type=pl.DeviceIdType.MESH,
            )
            copy.start()
            self.going.append(copy)

    def arrived(self):
        for copy in self.going:
            copy.wait_recv()

    def sent(self):
        for copy in self.going:
            copy.wait_send()


def greet(sizes):
    barrier = pltpu.get_barrier_semaphore()
    for axis, size in sizes.items():
        for offset in range(1, size):
            partner = lax.rem(lax.axis_index(axis) + offset, size)
            pl.semaphore_signal(
                barrier,
                inc=1,
                device_id={axis: partner},
                device_id_type=pl.DeviceIdType.MESH,
            )
    pl.semaphore_wait(barrier, sum(size - 1 for size in sizes.values()))


widths = (PROJ, PROJ * 3 // 4, PROJ // 2)
token_block = 1024


def unit(projected, columns):
    leading = jnp.where(lanes_of(projected.shape) < columns, projected, 0.0)
    inverse = lax.rsqrt(jnp.sum(leading * leading, axis=-1, keepdims=True) + vector_eps)
    return leading, inverse, (leading * inverse).astype(BF)


def unit_back(leading, inverse, grad):
    along = jnp.sum(leading * grad, axis=-1, keepdims=True)
    return grad * inverse - leading * (along * (inverse * inverse * inverse))


def exact(left, right):
    return lax.dot_general(
        left,
        right,
        (((1,), (0,)), ((), ())),
        precision=lax.Precision.HIGHEST,
        preferred_element_type=F32,
    )


def maxsim_kernel(
    n_dp,
    n_fs,
    pq_ref,
    pd_ref,
    mask_ref,
    label_ref,
    loss_ref,
    dq_ref,
    dd_ref,
    all_ref,
    power_ref,
    part_ref,
    score_ref,
    grad_ref,
    first_ref,
    total_ref,
    second_ref,
    *sems,
):
    tokens = n_dp * n_fs * QLEN
    blocks = tokens // token_block
    spots = label_ref.shape[1]
    my_dp, my_fs = lax.axis_index("dp"), lax.axis_index("fsdp")
    over = [
        Exchange(axis, n_dp if axis == "dp" else n_fs, sems[2 * i], sems[2 * i + 1])
        for i, axis in enumerate(("dp", "fsdp", "fsdp", "dp", "fsdp", "dp"))
    ]
    greet({"dp": n_dp, "fsdp": n_fs})

    own = all_ref.at[my_fs, my_dp]
    all_ref[my_fs, my_dp] = pq_ref[...]
    over[0].start(lambda partner: own, lambda offset: own)
    docs = [unit(pd_ref[...], columns) for columns in widths]
    over[0].arrived()
    over[1].start(lambda partner: all_ref.at[my_fs], lambda offset: all_ref.at[my_fs])
    over[1].arrived()

    def queries(block):
        every = all_ref[...].reshape(tokens, PROJ)
        return every[block * token_block : (block + 1) * token_block]

    def powers(index, block):
        similar = dot_nt(docs[index][2], unit(queries(block), widths[index])[2])
        return jnp.exp2(similar * (log2e / smooth_temp)) * mask_ref[:, :1]

    mine = part_ref.at[my_fs]
    part_ref[my_fs] = jnp.ones((8, tokens), F32)
    for block in range(blocks):
        here = slice(block * token_block, (block + 1) * token_block)
        for index in range(3):
            power = powers(index, block)
            if blocks == 1:
                power_ref[index] = power
            part_ref[my_fs, index : index + 1, here] = column_sum(power)
    over[2].start(lambda partner: mine, lambda offset: mine)
    over[2].arrived()
    total = part_ref[0]
    for source in range(1, n_fs):
        total = total + part_ref[source]

    token_of = lax.broadcasted_iota(jnp.int32, (tokens, spots), 0) // QLEN
    pool = jnp.where(token_of == lanes_of((tokens, spots)), 1.0, 0.0)
    score = exact(jnp.log(total), pool) * (smooth_temp / QLEN)
    score_ref[my_dp] = score
    row = score_ref.at[my_dp]
    over[3].start(lambda partner: row, lambda offset: row)
    over[3].arrived()
    logits = score_ref[...] * (1.0 / loss_temp)
    largest = jnp.max(logits, axis=0)
    log_sum = largest + jnp.log(jnp.sum(jnp.exp(logits - largest[None]), axis=0))
    label = label_ref[...]
    picked = jnp.zeros_like(log_sum)
    for index in range(n_dp):
        picked += jnp.where(label == index, logits[index], 0.0)
    loss_ref[...] = log_sum - picked
    dscore = jnp.exp(score * (1.0 / loss_temp) - log_sum) - jnp.where(label == my_dp, 1.0, 0.0)
    query_of = lax.broadcasted_iota(jnp.int32, (spots, tokens), 0)
    spread = jnp.where(lanes_of((spots, tokens)) // QLEN == query_of, 1.0, 0.0)
    factor = exact(dscore * (1.0 / (loss_temp * QLEN)), spread) / total

    grad_doc = [jnp.zeros(pd_ref.shape, F32)] * 3
    for block in range(blocks):
        here = slice(block * token_block, (block + 1) * token_block)
        grad_query = jnp.zeros((token_block, PROJ), F32)
        for index, columns in enumerate(widths):
            leading, inverse, vector = unit(queries(block), columns)
            power = power_ref[index] if blocks == 1 else powers(index, block)
            dsim = (power * factor[index : index + 1, here]).astype(BF)
            grad_query += unit_back(leading, inverse, dot_tn(dsim, docs[index][2]))
            grad_doc[index] += dot_nn(dsim, vector)
        if blocks == 1:
            grad_ref[...] = grad_query.reshape(grad_ref.shape)
        else:
            flat = block * token_block // QLEN
            count = token_block // QLEN
            grad_ref[flat // n_dp, flat % n_dp : flat % n_dp + count] = grad_query.reshape(
                count, QLEN, PROJ
            )
    over[4].start(lambda partner: grad_ref.at[partner], lambda offset: first_ref.at[offset - 1])
    dd = jnp.zeros(pd_ref.shape, F32)
    for index in range(3):
        dd += unit_back(docs[index][0], docs[index][1], grad_doc[index])
    dd_ref[...] = dd.astype(BF)
    over[4].arrived()
    summed = grad_ref[my_fs]
    for offset in range(n_fs - 1):
        summed = summed + first_ref[offset]
    total_ref[...] = summed
    over[5].start(lambda partner: total_ref.at[partner], lambda offset: second_ref.at[offset - 1])
    over[5].arrived()
    dq = total_ref[my_dp]
    for offset in range(n_dp - 1):
        dq = dq + second_ref[offset]
    dq_ref[...] = dq.astype(BF)
    for exchange in over:
        exchange.sent()


def maxsim(proj_query, proj_doc, doc_allowed, labels):
    n_dp, n_fs = lax.axis_size("dp"), lax.axis_size("fsdp")
    query_total = n_dp * n_fs
    tokens = query_total * QLEN
    blocks = tokens // token_block
    spots = -(-query_total // LANES) * LANES
    doc_rows = proj_doc.shape[0]
    ordered = jnp.transpose(labels).reshape(1, query_total)
    ordered = jnp.pad(ordered, ((0, 0), (0, spots - query_total)), constant_values=-1)
    mask = jnp.broadcast_to(doc_allowed[:, None], (doc_rows, LANES)).astype(F32)
    dma = lambda axis: [pltpu.SemaphoreType.DMA(((n_dp if axis == "dp" else n_fs) - 1,))] * 2
    whole = pl.BlockSpec(memory_space=pltpu.VMEM)
    loss, grad_query, grad_doc = pl.pallas_call(
        functools.partial(maxsim_kernel, n_dp, n_fs),
        in_specs=[whole] * 4,
        out_specs=[whole] * 3,
        out_shape=[
            jax.ShapeDtypeStruct((8, spots), F32),
            jax.ShapeDtypeStruct((QLEN, PROJ), BF),
            jax.ShapeDtypeStruct((doc_rows, PROJ), BF),
        ],
        scratch_shapes=[
            pltpu.VMEM((n_fs, n_dp, QLEN, PROJ), F32),
            pltpu.VMEM((3, doc_rows, token_block) if blocks == 1 else (3, 8, LANES), F32),
            pltpu.VMEM((n_fs, 8, tokens), F32),
            pltpu.VMEM((n_dp, 8, spots), F32),
            pltpu.VMEM((n_fs, n_dp, QLEN, PROJ), F32),
            pltpu.VMEM((n_fs - 1, n_dp, QLEN, PROJ), F32),
            pltpu.VMEM((n_dp, QLEN, PROJ), F32),
            pltpu.VMEM((n_dp - 1, QLEN, PROJ), F32),
        ]
        + [sem for axis in ("dp", "fsdp", "fsdp", "dp", "fsdp", "dp") for sem in dma(axis)],
        compiler_params=params(collective_id=1, has_side_effects=True),
        name="maxsim",
    )(proj_query, proj_doc, mask, jnp.broadcast_to(ordered, (8, spots)))
    losses = loss[:3, :query_total].reshape(3, n_fs, n_dp).transpose(0, 2, 1)
    return losses.reshape(3, query_total), grad_query, grad_doc


def other_core(parts):
    return [(part, part ^ 1) for part in range(parts)]


def other_chip(parts):
    return [(part, part ^ 2) for part in range(parts)]


def shards(
    doc_tokens,
    query_tokens,
    doc_lengths,
    labels,
    query_weight,
    query_bias,
    key_weight,
    key_bias,
    value_weight,
    value_bias,
    out_weight,
    out_bias,
    first_gain,
    first_shift,
    inner_weight,
    inner_bias,
    outer_weight,
    outer_bias,
    second_gain,
    second_shift,
    vector_weight,
):
    parts = lax.axis_size("fsdp")
    mine = lax.axis_index("fsdp")
    doc_rows = doc_tokens.shape[1]
    rows = doc_rows + QLEN
    width = D // parts
    split = query_weight.shape[0]

    w_split = jnp.concatenate(
        [
            entry[:, part * width : (part + 1) * width]
            for part in range(parts)
            for entry in (query_weight, key_weight, value_weight)
        ],
        axis=1,
    )
    w_split = lax.all_to_all(w_split, "fsdp", 1, 0, tiled=True)
    w_heads = lax.all_gather(w_split, "dp", axis=0, tiled=True)
    small = [
        query_bias,
        key_bias,
        value_bias,
        out_bias,
        first_gain,
        first_shift,
        outer_bias,
        second_gain,
        second_shift,
    ]
    hidden_split = inner_bias.shape[0]
    packed = lax.all_gather(jnp.concatenate(small + [inner_bias]), AXES, axis=0, tiled=False)
    packed = packed.astype(F32)

    def vector(index):
        return packed[:, index * split : (index + 1) * split].reshape(-1)

    inner_vec = packed[:, len(small) * split :].reshape(1, -1)
    vectors = jnp.stack([vector(i) for i in (3, 4, 5, 6, 7, 8)] + [jnp.zeros((D,), F32)] * 2)
    b_heads = jnp.concatenate(
        [lax.dynamic_slice(vector(i), (mine * width,), (width,)) for i in range(3)]
    ).reshape(1, -1)

    rows_in = jnp.concatenate([doc_tokens.reshape(doc_rows, D), query_tokens.reshape(QLEN, D)])
    x_all = lax.all_gather(rows_in, "fsdp")
    wo = lax.all_gather(out_weight, AXES, axis=0, tiled=True)
    wi = lax.all_gather(inner_weight, AXES, axis=0, tiled=True)
    wu = lax.all_gather(outer_weight, AXES, axis=0, tiled=True)
    wv = lax.all_gather(vector_weight, AXES, axis=0, tiled=True)

    tables = rope_tables(parts, doc_rows)
    cosine, sine = jnp.asarray(tables[0]), jnp.asarray(tables[1])
    query, key, value = project_heads(
        doc_lengths, x_all, w_heads, b_heads, cosine, sine, doc_rows
    )
    mixed, mixed_full, query_log = attend(query, key, value, parts, doc_rows)
    att = lax.all_to_all(mixed, "fsdp", 0, 0, tiled=True)
    hat1, inv1, low1, act, slope, hat2, inv2, enc, proj = rows_forward(
        att, rows_in, wo, wi, wu, wv, inner_vec, vectors
    )

    positions = mine * doc_rows + jnp.arange(doc_rows, dtype=jnp.int32)
    losses, grad_query, grad_doc = maxsim(
        proj[doc_rows:], proj[:doc_rows], positions < doc_lengths[0], labels
    )
    dproj = jnp.concatenate([grad_doc, grad_query])

    dwv, dwu, dwi, dbi, dwo, datt, dsum, dvec = rows_backward(
        dproj, enc, hat2, inv2, wv, act, slope, wu, wi, low1, hat1, inv1, att, wo, vectors
    )
    grad_mixed = lax.all_to_all(datt, "fsdp", 0, 0, tiled=True)
    dq, dk, dv = attend_back(query_log, key, value, grad_mixed, mixed_full, cosine, sine, doc_rows)
    dx, dw, db = heads_backward(x_all, dq, dk, dv, w_heads)

    core, chip = mine % 2, mine // 2
    by_core = dx.reshape(parts // 2, 2, rows, D)
    kept = lax.dynamic_index_in_dim(by_core, core, 1, False)
    sent = lax.dynamic_index_in_dim(by_core, 1 - core, 1, False)
    half = kept.astype(F32) + lax.ppermute(sent, "fsdp", other_core(parts)).astype(F32)
    away = lax.dynamic_index_in_dim(half, 1 - chip, 0, False).astype(BF)
    grad_rows = (
        dsum
        + lax.dynamic_index_in_dim(half, chip, 0, False)
        + lax.ppermute(away, "fsdp", other_chip(parts)).astype(F32)
    )
    grad_low = grad_rows.astype(BF)

    dw_dp = lax.psum_scatter(dw, "dp", scatter_dimension=0, tiled=True)
    dw_own = lax.all_to_all(dw_dp, "fsdp", 0, 1, tiled=True).astype(F32)
    dw_own = dw_own.reshape(split, parts, 3, width).transpose(2, 0, 1, 3).reshape(3, split, D)
    dwo_own = lax.psum_scatter(dwo, "dp", scatter_dimension=0, tiled=True)
    dwo_own = lax.psum_scatter(dwo_own, "fsdp", scatter_dimension=0, tiled=True).astype(F32)
    dwi_own = lax.psum_scatter(dwi, "dp", scatter_dimension=0, tiled=True)
    dwi_own = lax.psum_scatter(dwi_own, "fsdp", scatter_dimension=0, tiled=True).astype(F32)
    dwu_own = lax.psum_scatter(dwu, "dp", scatter_dimension=0, tiled=True)
    dwu_own = lax.psum_scatter(dwu_own, "fsdp", scatter_dimension=0, tiled=True).astype(F32)
    dwv_own = lax.psum_scatter(dwv, "dp", scatter_dimension=0, tiled=True)
    dwv_own = lax.psum_scatter(dwv_own, "fsdp", scatter_dimension=0, tiled=True).astype(F32)
    place = jnp.arange(parts, dtype=jnp.int32)[None, :, None] == mine
    db_all = jnp.where(place, db.reshape(3, 1, width), 0.0).reshape(3, D)
    vector_grads = jnp.concatenate([db_all, dvec[:6]]).reshape(9, -1, split).transpose(1, 0, 2)
    vector_grads = jnp.concatenate(
        [vector_grads.reshape(-1, 9 * split), dbi.reshape(-1, hidden_split)], axis=1
    )
    summed = lax.psum_scatter(vector_grads, AXES, scatter_dimension=0, tiled=False)
    vec_own = [summed[index * split : (index + 1) * split] for index in range(9)]
    dbi_own = summed[9 * split :]
    return (
        losses,
        enc[:doc_rows].reshape(1, doc_rows, D),
        enc[doc_rows:].reshape(1, 1, QLEN, D),
        grad_low[:doc_rows].reshape(1, doc_rows, D),
        grad_low[doc_rows:].reshape(1, 1, QLEN, D),
        dw_own[0],
        vec_own[0],
        dw_own[1],
        vec_own[1],
        dw_own[2],
        vec_own[2],
        dwo_own,
        vec_own[3],
        vec_own[4],
        vec_own[5],
        dwi_own,
        dbi_own,
        dwu_own,
        vec_own[6],
        vec_own[7],
        vec_own[8],
        dwv_own,
    )


def solution(mesh):
    rows = P(AXES, None)
    line = P(AXES)
    doc = P("dp", "fsdp", None)
    query = P("dp", "fsdp", None, None)
    weights = (rows, line) * 4 + (line, line, rows, line, rows, line, line, line, rows)
    return jax.shard_map(
        shards,
        mesh=mesh,
        in_specs=(doc, query, P("dp"), P()) + weights,
        out_specs=(P(), doc, query, doc, query) + weights,
        check_vma=False,
    )
```

```python
import functools
import math

import jax
import jax.numpy as jnp
import numpy as np
from jax import lax
from jax.experimental import pallas as pl
from jax.experimental.pallas import tpu as pltpu
from jax.sharding import PartitionSpec as P

D = 1024
HEAD_DIM = 64
PROJ = 128
QLEN = 32
LANES = 128

norm_eps = 1e-05
vector_eps = 1e-06
rope_base = 10000.0
smooth_temp = 0.05
loss_temp = 0.02
masked_score = -1e30
log2e = math.log2(math.e)
AXES = ("dp", "fsdp")
BF = jnp.bfloat16
F32 = jnp.float32
VMEM_MOST = 60 << 20


def dot_nn(left, right):
    return lax.dot_general(left, right, (((1,), (0,)), ((), ())), preferred_element_type=F32)


def dot_nt(left, right):
    return lax.dot_general(left, right, (((1,), (1,)), ((), ())), preferred_element_type=F32)


def dot_tn(left, right):
    return lax.dot_general(left, right, (((0,), (0,)), ((), ())), preferred_element_type=F32)


def lanes_of(shape):
    return lax.broadcasted_iota(jnp.int32, shape, len(shape) - 1)


def split_three(value):
    high = value.astype(BF)
    rest = value - high.astype(F32)
    middle = rest.astype(BF)
    return high, middle, (rest - middle.astype(F32)).astype(BF)


def params(**more):
    return pltpu.CompilerParams(vmem_limit_bytes=VMEM_MOST, **more)


def rope_tables(parts, doc_rows):
    half_dim = HEAD_DIM // 2
    frequency = rope_base ** (-np.arange(half_dim, dtype=np.float64) / half_dim)
    own = [
        np.concatenate([part * doc_rows + np.arange(doc_rows), np.arange(QLEN)])
        for part in range(parts)
    ]
    angles = np.concatenate(own)[:, None] * frequency[None, :]
    cosine, sine = np.cos(angles), np.sin(angles)
    shape = (parts, doc_rows + QLEN, LANES)
    return (
        np.concatenate([cosine] * 4, axis=1).astype(np.float32).reshape(shape),
        np.concatenate([-sine, sine, -sine, sine], axis=1).astype(np.float32).reshape(shape),
    )


def turn(tile, cosine, sine):
    first = lanes_of(tile.shape) % HEAD_DIM < HEAD_DIM // 2
    partner = jnp.where(first, pltpu.roll(tile, LANES - 32, 1), pltpu.roll(tile, 32, 1))
    return tile * cosine + partner * sine


def heads_kernel(doc_rows, len_ref, x_ref, w_ref, b_ref, cos_ref, sin_ref, q_ref, k_ref, v_ref):
    part = pl.program_id(0)
    rows = x_ref.shape[1]
    cosine, sine = cos_ref[0], sin_ref[0]
    lane = lanes_of((rows, LANES))
    row = lax.broadcasted_iota(jnp.int32, (rows, LANES), 0)
    allowed = (row >= doc_rows) | (part * doc_rows + row < len_ref[0])
    mask = jnp.where(allowed, 0.0, masked_score)
    width = w_ref.shape[1] // 3
    line = dot_nn(x_ref[0], w_ref[...]) + b_ref[...]
    for pair in range(width // LANES):
        here = pair * LANES
        query = turn(line[:, here : here + LANES], cosine, sine) * (log2e * HEAD_DIM**-0.5)
        key = turn(line[:, width + here : width + here + LANES], cosine, sine)
        value = line[:, 2 * width + here : 2 * width + here + LANES]
        for half in range(2):
            if half:
                query, key, value = (pltpu.roll(entry, 64, 1) for entry in (query, key, value))
            q_ref[2 * pair + half] = jnp.where(
                lane < 64, query, jnp.where(lane == 64, 1.0, 0.0)
            ).astype(BF)
            k_ref[2 * pair + half] = jnp.where(
                lane < 64, key, jnp.where(lane == 64, mask, jnp.where(lane < 68, 1.0, 0.0))
            ).astype(BF)
            v_ref[2 * pair + half] = jnp.where(
                lane < 64, value, jnp.where(lane < 67, 1.0, 0.0)
            ).astype(BF)


def project_heads(length, x_all, w_heads, b_heads, cosine, sine, doc_rows):
    parts, rows, _ = x_all.shape
    heads = w_heads.shape[1] // 3 // HEAD_DIM
    block = pl.BlockSpec((heads, rows, LANES), lambda part: (0, part, 0))
    shape = jax.ShapeDtypeStruct((heads, parts * rows, LANES), BF)
    table = pl.BlockSpec((1, rows, LANES), lambda part: (part, 0, 0))
    return pl.pallas_call(
        functools.partial(heads_kernel, doc_rows),
        grid=(parts,),
        in_specs=[
            pl.BlockSpec(memory_space=pltpu.SMEM),
            pl.BlockSpec((1, rows, D), lambda part: (part, 0, 0)),
            pl.BlockSpec(w_heads.shape, lambda part: (0, 0)),
            pl.BlockSpec(b_heads.shape, lambda part: (0, 0)),
            table,
            table,
        ],
        out_specs=[block] * 3,
        out_shape=[shape] * 3,
        compiler_params=params(),
        name="project_heads",
    )(length, x_all, w_heads, b_heads, cosine, sine)


def attend_rows(query, chunks):
    largest = jnp.full((query.shape[0], 1), -1e38, F32)
    total = jnp.zeros((query.shape[0], LANES), F32)
    for key, value in chunks:
        scores = dot_nt(query, key())
        newest = jnp.maximum(largest, jnp.max(scores, axis=1, keepdims=True))
        powers = jnp.exp2(scores - newest).astype(BF)
        total = total * jnp.exp2(largest - newest) + dot_nn(powers, value())
        largest = newest
    row_sum = total[:, 64:65]
    return total / row_sum, largest + jnp.log2(row_sum)


def attend_kernel(
    doc_rows, parts, q_ref, k_ref, v_ref, ko_ref, vo_ref, o_ref, full_ref, qa_ref
):
    rows = doc_rows + QLEN
    for span, own in ((slice(0, doc_rows), False), (slice(doc_rows, rows), True)):
        mixed = []
        for head in range(2):
            query = q_ref[head, span, :]
            lane = lanes_of(query.shape)
            if own:
                chunks = [(lambda: ko_ref[head], lambda: vo_ref[head])]
            else:
                chunks = [
                    (
                        lambda part=part: k_ref[head, part * rows : part * rows + doc_rows, :],
                        lambda part=part: v_ref[head, part * rows : part * rows + doc_rows, :],
                    )
                    for part in range(parts)
                ]
            out, log_sum = attend_rows(query, chunks)
            mixed.append(out)
            high, middle, low = split_three(-log_sum)
            qa_ref[head, span, :] = jnp.where(
                lane == 65,
                high,
                jnp.where(lane == 66, middle, jnp.where(lane == 67, low, query)),
            )
        joined = jnp.where(lanes_of(mixed[0].shape) < 64, mixed[0], pltpu.roll(mixed[1], 64, 1))
        full_ref[0, span, :] = joined
        o_ref[0, span, :] = joined.astype(BF)


def attend(query, key, value, parts, doc_rows):
    heads, total, _ = query.shape
    rows = total // parts
    own_at = rows // QLEN
    mine = pl.BlockSpec((2, rows, LANES), lambda pair, part: (pair, part, 0))
    whole = pl.BlockSpec((2, total, LANES), lambda pair, part: (pair, 0, 0))
    own = pl.BlockSpec((2, QLEN, LANES), lambda pair, part: (pair, part * own_at + own_at - 1, 0))
    flat = pl.BlockSpec((1, rows, LANES), lambda pair, part: (part, 0, pair))
    flops = 4 * heads * total * total * 256
    return pl.pallas_call(
        functools.partial(attend_kernel, doc_rows, parts),
        grid=(heads // 2, parts),
        in_specs=[mine, whole, whole, own, own],
        out_specs=[flat, flat, mine],
        out_shape=[
            jax.ShapeDtypeStruct((parts, rows, heads * HEAD_DIM), BF),
            jax.ShapeDtypeStruct((parts, rows, heads * HEAD_DIM), F32),
            jax.ShapeDtypeStruct(query.shape, BF),
        ],
        compiler_params=params(),
        cost_estimate=pl.CostEstimate(flops=flops, bytes_accessed=1 << 24, transcendentals=0),
        name="attend",
    )(query, key, value, key, value)


def attend_back_kernel(
    doc_rows,
    parts,
    q_ref,
    k_ref,
    v_ref,
    ko_ref,
    vo_ref,
    do_ref,
    o_ref,
    cos_ref,
    sin_ref,
    dq_ref,
    dk_ref,
    dv_ref,
    sums_ref,
    dk_doc,
    dv_doc,
    dk_own,
    dv_own,
):
    rows = doc_rows + QLEN
    at = pl.program_id(0)

    @pl.when(at == 0)
    def _():
        dk_doc[...] = jnp.zeros_like(dk_doc)
        dv_doc[...] = jnp.zeros_like(dv_doc)
        sums_ref[...] = jnp.zeros_like(sums_ref)

    for span, own in ((slice(0, doc_rows), False), (slice(doc_rows, rows), True)):
        grad_pair = do_ref[0, span, :]
        lane = lanes_of(grad_pair.shape)
        product = grad_pair.astype(F32) * o_ref[0, span, :]
        turned = pltpu.roll(grad_pair.astype(F32), 64, 1).astype(BF)
        pieces = []
        for head in range(2):
            query = q_ref[head, span, :]
            inside = lane < 64 if head == 0 else lane >= 64
            row_dot = jnp.sum(jnp.where(inside, product, 0.0), axis=1, keepdims=True)
            high, middle, low = split_three(-row_dot)
            grad = jnp.where(
                lane < 64,
                turned if head else grad_pair,
                jnp.where(
                    lane == 64,
                    high,
                    jnp.where(
                        lane == 65, middle, jnp.where(lane == 66, low, jnp.zeros_like(grad_pair))
                    ),
                ),
            )
            query_t, grad_t = query.T, grad.T
            grad_query = jnp.zeros(query.shape, F32)
            for part in range(1 if own else parts):
                if own:
                    key, value = ko_ref[head], vo_ref[head]
                else:
                    key = k_ref[head, part * rows : part * rows + doc_rows, :]
                    value = v_ref[head, part * rows : part * rows + doc_rows, :]
                powers = jnp.exp2(dot_nt(query, key))
                grad_scores = (powers * dot_nt(grad, value)).astype(BF)
                if own:
                    dv_own[head, at] = dot_nn(grad_t, powers.astype(BF))
                    dk_own[head, at] = dot_nn(query_t, grad_scores)
                else:
                    dv_doc[head, part] += dot_nn(grad_t, powers.astype(BF))
                    dk_doc[head, part] += dot_nn(query_t, grad_scores)
                grad_query += dot_nn(grad_scores, key)
            pieces.append(grad_query)
        joined = jnp.where(lane < 64, pieces[0], pltpu.roll(pieces[1], 64, 1)) * HEAD_DIM**-0.5
        low = turn(joined, cos_ref[at, span, :], -sin_ref[at, span, :]).astype(BF)
        dq_ref[0, span, :] = low
        sums_ref[0:1, :] += column_sum(low.astype(F32))

    @pl.when(at == parts - 1)
    def _():
        def both(kept, part):
            first, second = kept[0, part].T, kept[1, part].T
            return jnp.where(lanes_of(first.shape) < 64, first, pltpu.roll(second, 64, 1))

        for part in range(parts):
            for span, keys, values in (
                (slice(0, doc_rows), dk_doc, dv_doc),
                (slice(doc_rows, rows), dk_own, dv_own),
            ):
                grad_key = both(keys, part) * (1.0 / log2e)
                low = turn(grad_key, cos_ref[part, span, :], -sin_ref[part, span, :]).astype(BF)
                dk_ref[part, span, :] = low
                sums_ref[1:2, :] += column_sum(low.astype(F32))
                low = both(values, part).astype(BF)
                dv_ref[part, span, :] = low
                sums_ref[2:3, :] += column_sum(low.astype(F32))


def attend_back(pair, query, key, value, grad, mixed, cosine, sine, doc_rows):
    heads, total, _ = query.shape
    parts, rows, width = grad.shape
    own_at = rows // QLEN
    mine = pl.BlockSpec((2, rows, LANES), lambda part: (pair, part, 0))
    whole = pl.BlockSpec((2, total, LANES), lambda part: (pair, 0, 0))
    own = pl.BlockSpec((2, QLEN, LANES), lambda part: (pair, part * own_at + own_at - 1, 0))
    flat = pl.BlockSpec((1, rows, LANES), lambda part: (part, 0, pair))
    table = pl.BlockSpec((parts, rows, LANES), lambda part: (0, 0, 0))
    full = pl.BlockSpec((parts, rows, LANES), lambda part: (0, 0, 0))
    shape = jax.ShapeDtypeStruct((parts, rows, LANES), BF)
    return pl.pallas_call(
        functools.partial(attend_back_kernel, doc_rows, parts),
        grid=(parts,),
        in_specs=[mine, whole, whole, own, own, flat, flat, table, table],
        out_specs=[
            pl.BlockSpec((1, rows, LANES), lambda part: (part, 0, 0)),
            full,
            full,
            pl.BlockSpec((8, LANES), lambda part: (0, 0)),
        ],
        out_shape=[shape] * 3 + [jax.ShapeDtypeStruct((8, LANES), F32)],
        scratch_shapes=[
            pltpu.VMEM((2, parts, LANES, doc_rows), F32),
            pltpu.VMEM((2, parts, LANES, doc_rows), F32),
            pltpu.VMEM((2, parts, LANES, QLEN), F32),
            pltpu.VMEM((2, parts, LANES, QLEN), F32),
        ],
        compiler_params=params(),
        cost_estimate=pl.CostEstimate(
            flops=10 * 2 * total * total * 256, bytes_accessed=1 << 24, transcendentals=0
        ),
        name="attend_back",
    )(query, key, value, key, value, grad, mixed, cosine, sine)


def normed(summed):
    centered = summed - jnp.mean(summed, axis=-1, keepdims=True)
    variance = jnp.mean(centered * centered, axis=-1, keepdims=True)
    inverse = lax.rsqrt(variance + norm_eps)
    return centered * inverse, inverse


GROUPS = 4
CHUNK = 512


def joined_up(up_ref):
    size = up_ref.shape[0] // (CHUNK // (QLEN * GROUPS))
    pieces = [
        up_ref[at : at + size, group * D : (group + 1) * D]
        for at in range(0, up_ref.shape[0], size)
        for group in range(GROUPS)
    ]
    return jnp.concatenate(pieces, axis=0)


def packed_specs():
    hidden = GROUPS * D
    return {
        "up": pl.BlockSpec((CHUNK // GROUPS, hidden), lambda step: (step, 0)),
        "down": pl.BlockSpec((D, CHUNK), lambda step: (0, hidden // CHUNK + step)),
        "out": pl.BlockSpec((D, D), lambda step: (0, 2 * hidden // D)),
        "vector": pl.BlockSpec((D, LANES), lambda step: (0, (2 * hidden + D) // LANES)),
    }


def rows_kernel(
    att_ref,
    x_ref,
    wo_ref,
    wi_ref,
    wu_ref,
    wv_ref,
    bi_ref,
    vec_ref,
    hat1_ref,
    inv1_ref,
    low1_ref,
    act_ref,
    slope_ref,
    hat2_ref,
    inv2_ref,
    enc_ref,
    proj_ref,
    sum_ref,
):
    step = pl.program_id(0)
    parts, _, width = att_ref.shape

    @pl.when(step == 0)
    def _():
        summed = x_ref[...].astype(F32) + vec_ref[0:1, :]
        for part in range(parts):
            summed += dot_nn(att_ref[part], wo_ref[part * width : (part + 1) * width, :])
        hat, inverse = normed(summed)
        hat1_ref[...] = hat.astype(BF)
        inv1_ref[...] = jnp.broadcast_to(inverse, inv1_ref.shape)
        out = hat * vec_ref[1:2, :] + vec_ref[2:3, :]
        low1_ref[...] = out.astype(BF)
        sum_ref[...] = out + vec_ref[3:4, :]

    up = joined_up(wu_ref)
    inner = dot_nn(low1_ref[...], wi_ref[...]) + bi_ref[...]
    share = 0.5 * lax.erf(inner * math.sqrt(0.5)) + 0.5
    act = (inner * share).astype(BF)
    act_ref[...] = act
    density = jnp.exp(inner * inner * -0.5) * (1.0 / math.sqrt(2.0 * math.pi))
    slope_ref[...] = (share + inner * density).astype(BF)
    sum_ref[...] += dot_nn(act, up)

    @pl.when(step == pl.num_programs(0) - 1)
    def _():
        hat, inverse = normed(sum_ref[...])
        hat2_ref[...] = hat.astype(BF)
        inv2_ref[...] = jnp.broadcast_to(inverse, inv2_ref.shape)
        low = (hat * vec_ref[4:5, :] + vec_ref[5:6, :]).astype(BF)
        enc_ref[...] = low
        proj_ref[...] = dot_nn(low, wv_ref[...])


def rows_forward(att, rows_in, packed, inner_bias, vectors):
    rows = rows_in.shape[0]
    hidden = inner_bias.shape[1]
    chunk = CHUNK
    weights = packed_specs()
    keep = lambda shape: pl.BlockSpec(shape, lambda step: (0,) * len(shape))
    columns = pl.BlockSpec((rows, chunk), lambda step: (0, step))
    wide = jax.ShapeDtypeStruct((rows, D), BF)
    thin = jax.ShapeDtypeStruct((rows, LANES), F32)
    big = jax.ShapeDtypeStruct((rows, hidden), BF)
    return pl.pallas_call(
        rows_kernel,
        grid=(hidden // chunk,),
        in_specs=[
            keep(att.shape),
            keep(rows_in.shape),
            weights["out"],
            weights["down"],
            weights["up"],
            weights["vector"],
            pl.BlockSpec((1, chunk), lambda step: (0, step)),
            keep(vectors.shape),
        ],
        out_specs=[
            keep((rows, D)),
            keep((rows, LANES)),
            keep((rows, D)),
            columns,
            columns,
            keep((rows, D)),
            keep((rows, LANES)),
            keep((rows, D)),
            keep((rows, LANES)),
        ],
        out_shape=[wide, thin, wide, big, big, wide, thin, wide, thin],
        scratch_shapes=[pltpu.VMEM((rows, D), F32)],
        compiler_params=params(),
        cost_estimate=pl.CostEstimate(
            flops=2 * rows * D * (D + 2 * hidden), bytes_accessed=1 << 25, transcendentals=0
        ),
        name="rows_forward",
    )(att, rows_in, packed, packed, packed, packed, inner_bias, vectors)


def norm_back(grad, hat, inverse, gain):
    scaled = grad * gain
    first = jnp.mean(scaled, axis=-1, keepdims=True)
    second = jnp.mean(scaled * hat, axis=-1, keepdims=True)
    return (scaled - first - hat * second) * inverse


def column_sum(value):
    return jnp.sum(value, axis=0, keepdims=True)


def rows_back_kernel(
    dproj_ref,
    enc_ref,
    hat2_ref,
    inv2_ref,
    wv_ref,
    act_ref,
    slope_ref,
    wu_ref,
    wi_ref,
    low1_ref,
    hat1_ref,
    inv1_ref,
    att_ref,
    wo_ref,
    vec_ref,
    grads_ref,
    dbi_ref,
    datt_ref,
    dsum_ref,
    dvec_ref,
    low_ref,
    total_ref,
    dwv_ref,
    dwo_ref,
    dwu_ref,
    dwi_ref,
    once_sem,
    up_sem,
    down_sem,
):
    step = pl.program_id(0)
    steps = pl.num_programs(0)
    parts, _, width = att_ref.shape
    hidden = GROUPS * D
    slot = lax.rem(step, 2)

    def up_copy(at, place):
        here = pl.ds(pl.multiple_of(at * (CHUNK // GROUPS), CHUNK // GROUPS), CHUNK // GROUPS)
        return pltpu.make_async_copy(
            dwu_ref.at[place], grads_ref.at[here, pl.ds(0, hidden)], up_sem.at[place]
        )

    def down_copy(at, place):
        here = pl.ds(pl.multiple_of(hidden + at * CHUNK, CHUNK), CHUNK)
        return pltpu.make_async_copy(
            dwi_ref.at[place], grads_ref.at[:, here], down_sem.at[place]
        )

    vector_copy = pltpu.make_async_copy(
        dwv_ref, grads_ref.at[:, pl.ds(2 * hidden + D, LANES)], once_sem.at[0]
    )
    out_copy = pltpu.make_async_copy(
        dwo_ref, grads_ref.at[:, pl.ds(2 * hidden, D)], once_sem.at[1]
    )

    @pl.when(step == 0)
    def _():
        dproj = dproj_ref[...]
        dwv_ref[...] = dot_tn(enc_ref[...], dproj).astype(BF)
        vector_copy.start()
        grad = dot_nt(dproj, wv_ref[...])
        hat = hat2_ref[...].astype(F32)
        dvec_ref[4:5, :] = column_sum(grad * hat)
        dvec_ref[5:6, :] = column_sum(grad)
        back = norm_back(grad, hat, inv2_ref[:, :1], vec_ref[4:5, :])
        low = back.astype(BF)
        low_ref[...] = low
        total_ref[...] = back
        dvec_ref[3:4, :] = column_sum(low.astype(F32))

    @pl.when(step >= 2)
    def _():
        up_copy(step - 2, slot).wait()
        down_copy(step - 2, slot).wait()

    low = low_ref[...]
    dinner = (dot_nt(low, joined_up(wu_ref)) * slope_ref[...].astype(F32)).astype(BF)
    dbi_ref[...] = column_sum(dinner.astype(F32))
    up_grad = dot_tn(act_ref[...], low).astype(BF)
    for at in range(0, CHUNK, QLEN):
        own, group = at // (QLEN * GROUPS), at // QLEN % GROUPS
        dwu_ref[slot, own * QLEN : (own + 1) * QLEN, group * D : (group + 1) * D] = up_grad[
            at : at + QLEN
        ]
    up_copy(step, slot).start()
    dwi_ref[slot] = dot_tn(low1_ref[...], dinner).astype(BF)
    down_copy(step, slot).start()
    total_ref[...] += dot_nt(dinner, wi_ref[...])

    @pl.when(step == pl.num_programs(0) - 1)
    def _():
        grad = total_ref[...]
        hat = hat1_ref[...].astype(F32)
        dvec_ref[1:2, :] = column_sum(grad * hat)
        dvec_ref[2:3, :] = column_sum(grad)
        back = norm_back(grad, hat, inv1_ref[:, :1], vec_ref[1:2, :])
        dsum_ref[...] = back
        attn_low = back.astype(BF)
        dvec_ref[0:1, :] = column_sum(attn_low.astype(F32))
        for part in range(parts):
            here = slice(part * width, (part + 1) * width)
            dwo_ref[here, :] = dot_tn(att_ref[part], attn_low).astype(BF)
            datt_ref[part] = dot_nt(attn_low, wo_ref[here, :]).astype(BF)
        out_copy.start()
        vector_copy.wait()
        for place in range(2):
            up_copy(steps - 2 + place, place).wait()
            down_copy(steps - 2 + place, place).wait()
        out_copy.wait()


def rows_backward(dproj, enc, hat2, inv2, packed, act, slope, low1, hat1, inv1, att, vectors):
    rows, hidden = act.shape
    keep = lambda shape: pl.BlockSpec(shape, lambda step: (0,) * len(shape))
    columns = pl.BlockSpec((rows, CHUNK), lambda step: (0, step))
    bias = pl.BlockSpec((1, CHUNK), lambda step: (0, step))
    weights = packed_specs()
    operands = (
        (dproj, None),
        (enc, None),
        (hat2, None),
        (inv2, None),
        (packed, weights["vector"]),
        (act, columns),
        (slope, columns),
        (packed, weights["up"]),
        (packed, weights["down"]),
        (low1, None),
        (hat1, None),
        (inv1, None),
        (att, None),
        (packed, weights["out"]),
        (vectors, None),
    )
    return pl.pallas_call(
        rows_back_kernel,
        grid=(hidden // CHUNK,),
        in_specs=[keep(entry.shape) if spec is None else spec for entry, spec in operands],
        out_specs=[
            pl.BlockSpec(memory_space=pl.ANY),
            bias,
            keep(att.shape),
            keep((rows, D)),
            keep((8, D)),
        ],
        out_shape=[
            jax.ShapeDtypeStruct(packed.shape, BF),
            jax.ShapeDtypeStruct((1, hidden), F32),
            jax.ShapeDtypeStruct(att.shape, BF),
            jax.ShapeDtypeStruct((rows, D), F32),
            jax.ShapeDtypeStruct((8, D), F32),
        ],
        scratch_shapes=[
            pltpu.VMEM((rows, D), BF),
            pltpu.VMEM((rows, D), F32),
            pltpu.VMEM((D, LANES), BF),
            pltpu.VMEM((D, D), BF),
            pltpu.VMEM((2, CHUNK // GROUPS, hidden), BF),
            pltpu.VMEM((2, D, CHUNK), BF),
            pltpu.SemaphoreType.DMA((2,)),
            pltpu.SemaphoreType.DMA((2,)),
            pltpu.SemaphoreType.DMA((2,)),
        ],
        compiler_params=params(),
        cost_estimate=pl.CostEstimate(
            flops=4 * rows * D * (D + 2 * hidden), bytes_accessed=1 << 26, transcendentals=0
        ),
        name="rows_backward",
    )(*(entry for entry, _ in operands))


class Exchange:
    def __init__(self, axis, size, send, recv):
        self.axis, self.size, self.send, self.recv = axis, size, send, recv
        self.me = lax.axis_index(axis)
        self.going = []

    def to(self, offset):
        return lax.rem(self.me + offset, self.size)

    def source(self, offset):
        return lax.rem(self.me - offset + self.size, self.size)

    def start(self, source_of, target_of):
        for offset in range(1, self.size):
            partner = self.to(offset)
            copy = pltpu.make_async_remote_copy(
                src_ref=source_of(partner),
                dst_ref=target_of(offset),
                send_sem=self.send.at[offset - 1],
                recv_sem=self.recv.at[offset - 1],
                device_id={self.axis: partner},
                device_id_type=pl.DeviceIdType.MESH,
            )
            copy.start()
            self.going.append(copy)

    def arrived(self):
        for copy in self.going:
            copy.wait_recv()

    def sent(self):
        for copy in self.going:
            copy.wait_send()


def greet(sizes):
    barrier = pltpu.get_barrier_semaphore()
    for axis, size in sizes.items():
        for offset in range(1, size):
            partner = lax.rem(lax.axis_index(axis) + offset, size)
            pl.semaphore_signal(
                barrier,
                inc=1,
                device_id={axis: partner},
                device_id_type=pl.DeviceIdType.MESH,
            )
    pl.semaphore_wait(barrier, sum(size - 1 for size in sizes.values()))


class Sent:
    def __init__(self, source, target, axis, index, send, recv):
        self.copy = pltpu.make_async_remote_copy(
            src_ref=source,
            dst_ref=target,
            send_sem=send,
            recv_sem=recv,
            device_id={axis: index},
            device_id_type=pl.DeviceIdType.MESH,
        )

    def start(self):
        self.copy.start()
        return self


pieces_along_y = 5


def heads_back_kernel(n_dp, n_fs, pairs, *refs):
    x_ref, w_ref, dsum_ref, vec_ref = refs[:4]
    grad_refs = refs[4 : 4 + 3 * pairs]
    dx_ref, dw_ref, dvec_ref = refs[4 + 3 * pairs : 7 + 3 * pairs]
    (
        first_out,
        second_out,
        first_in,
        second_in,
        chip_out,
        chip_in,
        kept_ref,
        dw_out,
        dw_in,
        dw_sum,
        vec_in,
        vec_sum,
        vec_last,
        core_send,
        core_recv,
        chip_send,
        chip_recv,
        *sems,
    ) = refs[7 + 3 * pairs :]
    me, my_dp = lax.axis_index("fsdp"), lax.axis_index("dp")
    core, chip = lax.rem(me, 2), me // 2
    other_core = chip * 2 + 1 - core
    other_chip = (1 - chip) * 2 + core
    over = [
        Exchange(axis, n_dp if axis == "dp" else n_fs, sems[2 * i], sems[2 * i + 1])
        for i, axis in enumerate(("fsdp", "dp", "dp", "fsdp"))
    ]
    greet({"dp": n_dp, "fsdp": n_fs})
    width = w_ref.shape[1] // 3
    rows = x_ref.shape[1]
    piece = rows // pieces_along_y

    over[0].start(lambda partner: vec_ref.at[partner], lambda offset: vec_in.at[offset - 1])

    def back(part):
        total = jnp.zeros((rows, D), F32)
        for index in range(3):
            for pair in range(pairs):
                here = index * width + pair * LANES
                total += dot_nt(
                    grad_refs[pair * 3 + index][part], w_ref[:, here : here + LANES]
                )
        return total

    def to_core(source, target, at):
        return Sent(source, target, "fsdp", other_core, core_send.at[at], core_recv.at[at]).start()

    first_out[...] = back((1 - chip) * 2 + 1 - core).astype(BF)
    first = to_core(first_out, first_in, 0)
    away = back(other_chip)
    first.copy.wait_recv()
    chip_out[...] = (away + first_in[...].astype(F32)).astype(BF)
    along_y = []
    for at in range(pieces_along_y):
        here = pl.ds(at * piece, piece)
        along_y.append(
            Sent(
                chip_out.at[here],
                chip_in.at[here],
                "fsdp",
                other_chip,
                chip_send.at[at],
                chip_recv.at[at],
            ).start()
        )

    block = D // n_dp
    for index in range(3):
        for pair in range(pairs):
            here = index * width + pair * LANES
            total = jnp.zeros((D, LANES), F32)
            for part in range(n_fs):
                total += dot_tn(x_ref[part], grad_refs[pair * 3 + index][part])
            dw_out[:, :, here : here + LANES] = total.astype(BF).reshape(n_dp, block, LANES)
    over[1].start(lambda partner: dw_out.at[partner], lambda offset: dw_in.at[offset - 1])

    over[0].arrived()
    vec_total = vec_ref[me]
    for offset in range(n_fs - 1):
        vec_total = vec_total + vec_in[offset]
    vec_sum[...] = vec_total
    over[2].start(lambda partner: vec_sum.at[partner], lambda offset: vec_last.at[offset - 1])

    second_out[...] = back(other_core).astype(BF)
    second = to_core(second_out, second_in, 1)
    kept_ref[...] = back(me) + dsum_ref[...]
    second.copy.wait_recv()
    kept_ref[...] += second_in[...].astype(F32)

    over[2].arrived()
    vec_total = vec_sum[my_dp]
    for offset in range(n_dp - 1):
        vec_total = vec_total + vec_last[offset]
    dvec_ref[...] = vec_total

    over[1].arrived()
    dw_total = dw_out[my_dp].astype(F32)
    for offset in range(n_dp - 1):
        dw_total = dw_total + dw_in[offset].astype(F32)
    each = block // n_fs
    dw_sum[...] = dw_total.reshape(n_fs, each, 3 * width)
    mine = dw_ref.at[me]
    dw_ref[me] = dw_sum[me]
    over[3].start(lambda partner: dw_sum.at[partner], lambda offset: mine)
    for at in range(pieces_along_y):
        here = slice(at * piece, (at + 1) * piece)
        along_y[at].copy.wait_recv()
        dx_ref[here, :] = (kept_ref[here, :] + chip_in[here, :].astype(F32)).astype(BF)
    over[3].arrived()
    for exchange in over:
        exchange.sent()
    for one in [first, second] + along_y:
        one.copy.wait_send()


def heads_backward(x_all, w_heads, dsum, vector_grads, grads):
    n_dp, n_fs = lax.axis_size("dp"), lax.axis_size("fsdp")
    _, rows, _ = x_all.shape
    pairs = len(grads) // 3
    whole = pl.BlockSpec(memory_space=pltpu.VMEM)
    block = D // n_dp
    columns = w_heads.shape[1]
    tile = vector_grads.shape[2:]
    line = pltpu.VMEM((rows, D), BF)
    dma = lambda axis: [pltpu.SemaphoreType.DMA(((n_dp if axis == "dp" else n_fs) - 1,))] * 2
    return pl.pallas_call(
        functools.partial(heads_back_kernel, n_dp, n_fs, pairs),
        in_specs=[whole] * (4 + 3 * pairs),
        out_specs=[whole] * 3,
        out_shape=[
            jax.ShapeDtypeStruct((rows, D), BF),
            jax.ShapeDtypeStruct((n_fs, block // n_fs, columns), F32),
            jax.ShapeDtypeStruct(tile, F32),
        ],
        scratch_shapes=[line] * 6
        + [
            pltpu.VMEM((rows, D), F32),
            pltpu.VMEM((n_dp, block, columns), BF),
            pltpu.VMEM((n_dp - 1, block, columns), BF),
            pltpu.VMEM((n_fs, block // n_fs, columns), F32),
            pltpu.VMEM((n_fs - 1, n_dp) + tile, F32),
            pltpu.VMEM((n_dp,) + tile, F32),
            pltpu.VMEM((n_dp - 1,) + tile, F32),
            pltpu.SemaphoreType.DMA((2,)),
            pltpu.SemaphoreType.DMA((2,)),
            pltpu.SemaphoreType.DMA((pieces_along_y,)),
            pltpu.SemaphoreType.DMA((pieces_along_y,)),
        ]
        + [sem for axis in ("fsdp", "dp", "dp", "fsdp") for sem in dma(axis)],
        compiler_params=params(collective_id=2, has_side_effects=True),
        name="heads_backward",
    )(x_all, w_heads, dsum, vector_grads, *grads)


widths = (PROJ, PROJ * 3 // 4, PROJ // 2)
token_block = 1024


def unit(projected, columns):
    leading = jnp.where(lanes_of(projected.shape) < columns, projected, 0.0)
    inverse = lax.rsqrt(jnp.sum(leading * leading, axis=-1, keepdims=True) + vector_eps)
    return leading, inverse, (leading * inverse).astype(BF)


def unit_back(leading, inverse, grad):
    along = jnp.sum(leading * grad, axis=-1, keepdims=True)
    return grad * inverse - leading * (along * (inverse * inverse * inverse))


def exact(left, right):
    return lax.dot_general(
        left,
        right,
        (((1,), (0,)), ((), ())),
        precision=lax.Precision.HIGHEST,
        preferred_element_type=F32,
    )


def maxsim_kernel(
    n_dp,
    n_fs,
    pq_ref,
    pd_ref,
    mask_ref,
    label_ref,
    loss_ref,
    dq_ref,
    dd_ref,
    all_ref,
    power_ref,
    part_ref,
    score_ref,
    grad_ref,
    first_ref,
    total_ref,
    second_ref,
    *sems,
):
    tokens = n_dp * n_fs * QLEN
    blocks = tokens // token_block
    spots = label_ref.shape[1]
    my_dp, my_fs = lax.axis_index("dp"), lax.axis_index("fsdp")
    over = [
        Exchange(axis, n_dp if axis == "dp" else n_fs, sems[2 * i], sems[2 * i + 1])
        for i, axis in enumerate(("dp", "fsdp", "fsdp", "dp", "fsdp", "dp"))
    ]
    greet({"dp": n_dp, "fsdp": n_fs})

    own = all_ref.at[my_fs, my_dp]
    all_ref[my_fs, my_dp] = pq_ref[...]
    over[0].start(lambda partner: own, lambda offset: own)
    docs = [unit(pd_ref[...], columns) for columns in widths]
    over[0].arrived()
    over[1].start(lambda partner: all_ref.at[my_fs], lambda offset: all_ref.at[my_fs])
    over[1].arrived()

    def queries(block):
        every = all_ref[...].reshape(tokens, PROJ)
        return every[block * token_block : (block + 1) * token_block]

    def powers(index, block):
        similar = dot_nt(docs[index][2], unit(queries(block), widths[index])[2])
        return jnp.exp2(similar * (log2e / smooth_temp)) * mask_ref[:, :1]

    mine = part_ref.at[my_fs]
    part_ref[my_fs] = jnp.ones((8, tokens), F32)
    for block in range(blocks):
        here = slice(block * token_block, (block + 1) * token_block)
        for index in range(3):
            power = powers(index, block)
            if blocks == 1:
                power_ref[index] = power
            part_ref[my_fs, index : index + 1, here] = column_sum(power)
    over[2].start(lambda partner: mine, lambda offset: mine)
    over[2].arrived()
    total = part_ref[0]
    for source in range(1, n_fs):
        total = total + part_ref[source]

    token_of = lax.broadcasted_iota(jnp.int32, (tokens, spots), 0) // QLEN
    pool = jnp.where(token_of == lanes_of((tokens, spots)), 1.0, 0.0)
    score = exact(jnp.log(total), pool) * (smooth_temp / QLEN)
    score_ref[my_dp] = score
    row = score_ref.at[my_dp]
    over[3].start(lambda partner: row, lambda offset: row)
    over[3].arrived()
    logits = score_ref[...] * (1.0 / loss_temp)
    largest = jnp.max(logits, axis=0)
    log_sum = largest + jnp.log(jnp.sum(jnp.exp(logits - largest[None]), axis=0))
    label = label_ref[...]
    picked = jnp.zeros_like(log_sum)
    for index in range(n_dp):
        picked += jnp.where(label == index, logits[index], 0.0)
    loss_ref[...] = log_sum - picked
    dscore = jnp.exp(score * (1.0 / loss_temp) - log_sum) - jnp.where(label == my_dp, 1.0, 0.0)
    query_of = lax.broadcasted_iota(jnp.int32, (spots, tokens), 0)
    spread = jnp.where(lanes_of((spots, tokens)) // QLEN == query_of, 1.0, 0.0)
    factor = exact(dscore * (1.0 / (loss_temp * QLEN)), spread) / total

    grad_doc = [jnp.zeros(pd_ref.shape, F32)] * 3
    for block in range(blocks):
        here = slice(block * token_block, (block + 1) * token_block)
        grad_query = jnp.zeros((token_block, PROJ), F32)
        for index, columns in enumerate(widths):
            leading, inverse, vector = unit(queries(block), columns)
            power = power_ref[index] if blocks == 1 else powers(index, block)
            dsim = (power * factor[index : index + 1, here]).astype(BF)
            grad_query += unit_back(leading, inverse, dot_tn(dsim, docs[index][2]))
            grad_doc[index] += dot_nn(dsim, vector)
        if blocks == 1:
            grad_ref[...] = grad_query.reshape(grad_ref.shape)
        else:
            flat = block * token_block // QLEN
            count = token_block // QLEN
            grad_ref[flat // n_dp, flat % n_dp : flat % n_dp + count] = grad_query.reshape(
                count, QLEN, PROJ
            )
    over[4].start(lambda partner: grad_ref.at[partner], lambda offset: first_ref.at[offset - 1])
    dd = jnp.zeros(pd_ref.shape, F32)
    for index in range(3):
        dd += unit_back(docs[index][0], docs[index][1], grad_doc[index])
    dd_ref[...] = dd.astype(BF)
    over[4].arrived()
    summed = grad_ref[my_fs]
    for offset in range(n_fs - 1):
        summed = summed + first_ref[offset]
    total_ref[...] = summed
    over[5].start(lambda partner: total_ref.at[partner], lambda offset: second_ref.at[offset - 1])
    over[5].arrived()
    dq = total_ref[my_dp]
    for offset in range(n_dp - 1):
        dq = dq + second_ref[offset]
    dq_ref[...] = dq.astype(BF)
    for exchange in over:
        exchange.sent()


def maxsim(proj_query, proj_doc, doc_allowed, labels):
    n_dp, n_fs = lax.axis_size("dp"), lax.axis_size("fsdp")
    query_total = n_dp * n_fs
    tokens = query_total * QLEN
    blocks = tokens // token_block
    spots = -(-query_total // LANES) * LANES
    doc_rows = proj_doc.shape[0]
    ordered = jnp.transpose(labels).reshape(1, query_total)
    ordered = jnp.pad(ordered, ((0, 0), (0, spots - query_total)), constant_values=-1)
    mask = jnp.broadcast_to(doc_allowed[:, None], (doc_rows, LANES)).astype(F32)
    dma = lambda axis: [pltpu.SemaphoreType.DMA(((n_dp if axis == "dp" else n_fs) - 1,))] * 2
    whole = pl.BlockSpec(memory_space=pltpu.VMEM)
    loss, grad_query, grad_doc = pl.pallas_call(
        functools.partial(maxsim_kernel, n_dp, n_fs),
        in_specs=[whole] * 4,
        out_specs=[whole] * 3,
        out_shape=[
            jax.ShapeDtypeStruct((8, spots), F32),
            jax.ShapeDtypeStruct((QLEN, PROJ), BF),
            jax.ShapeDtypeStruct((doc_rows, PROJ), BF),
        ],
        scratch_shapes=[
            pltpu.VMEM((n_fs, n_dp, QLEN, PROJ), F32),
            pltpu.VMEM((3, doc_rows, token_block) if blocks == 1 else (3, 8, LANES), F32),
            pltpu.VMEM((n_fs, 8, tokens), F32),
            pltpu.VMEM((n_dp, 8, spots), F32),
            pltpu.VMEM((n_fs, n_dp, QLEN, PROJ), F32),
            pltpu.VMEM((n_fs - 1, n_dp, QLEN, PROJ), F32),
            pltpu.VMEM((n_dp, QLEN, PROJ), F32),
            pltpu.VMEM((n_dp - 1, QLEN, PROJ), F32),
        ]
        + [sem for axis in ("dp", "fsdp", "fsdp", "dp", "fsdp", "dp") for sem in dma(axis)],
        compiler_params=params(collective_id=1, has_side_effects=True),
        name="maxsim",
    )(proj_query, proj_doc, mask, jnp.broadcast_to(ordered, (8, spots)))
    losses = loss[:3, :query_total].reshape(3, n_fs, n_dp).transpose(0, 2, 1)
    return losses.reshape(3, query_total), grad_query, grad_doc


def other_core(parts):
    return [(part, part ^ 1) for part in range(parts)]


def other_chip(parts):
    return [(part, part ^ 2) for part in range(parts)]


def shards(
    doc_tokens,
    query_tokens,
    doc_lengths,
    labels,
    query_weight,
    query_bias,
    key_weight,
    key_bias,
    value_weight,
    value_bias,
    out_weight,
    out_bias,
    first_gain,
    first_shift,
    inner_weight,
    inner_bias,
    outer_weight,
    outer_bias,
    second_gain,
    second_shift,
    vector_weight,
):
    parts = lax.axis_size("fsdp")
    mine = lax.axis_index("fsdp")
    doc_rows = doc_tokens.shape[1]
    rows = doc_rows + QLEN
    width = D // parts
    split = query_weight.shape[0]

    w_split = jnp.concatenate(
        [
            entry[:, part * width : (part + 1) * width]
            for part in range(parts)
            for entry in (query_weight, key_weight, value_weight)
        ],
        axis=1,
    )
    w_split = lax.all_to_all(w_split, "fsdp", 1, 0, tiled=True)
    w_heads = lax.all_gather(w_split, "dp", axis=0, tiled=True)
    small = [
        query_bias,
        key_bias,
        value_bias,
        out_bias,
        first_gain,
        first_shift,
        outer_bias,
        second_gain,
        second_shift,
    ]
    hidden_split = inner_bias.shape[0]
    packed = lax.all_gather(jnp.concatenate(small + [inner_bias]), AXES, axis=0, tiled=False)
    packed = packed.astype(F32)

    def vector(index):
        return packed[:, index * split : (index + 1) * split].reshape(-1)

    inner_vec = packed[:, len(small) * split :].reshape(1, -1)
    vectors = jnp.stack([vector(i) for i in (3, 4, 5, 6, 7, 8)] + [jnp.zeros((D,), F32)] * 2)
    b_heads = jnp.concatenate(
        [lax.dynamic_slice(vector(i), (mine * width,), (width,)) for i in range(3)]
    ).reshape(1, -1)

    rows_in = jnp.concatenate([doc_tokens.reshape(doc_rows, D), query_tokens.reshape(QLEN, D)])
    x_all = lax.all_gather(rows_in, "fsdp")
    own_up = [outer_weight[group * split : (group + 1) * split] for group in range(GROUPS)]
    packed_own = jnp.concatenate(own_up + [inner_weight, out_weight, vector_weight], axis=1)
    packed_w = lax.all_gather(packed_own, AXES, axis=0, tiled=True)

    tables = rope_tables(parts, doc_rows)
    cosine, sine = jnp.asarray(tables[0]), jnp.asarray(tables[1])
    query, key, value = project_heads(
        doc_lengths, x_all, w_heads, b_heads, cosine, sine, doc_rows
    )
    mixed, mixed_full, query_log = attend(query, key, value, parts, doc_rows)
    att = lax.all_to_all(mixed, "fsdp", 0, 0, tiled=True)
    hat1, inv1, low1, act, slope, hat2, inv2, enc, proj = rows_forward(
        att, rows_in, packed_w, inner_vec, vectors
    )

    positions = mine * doc_rows + jnp.arange(doc_rows, dtype=jnp.int32)
    losses, grad_query, grad_doc = maxsim(
        proj[doc_rows:], proj[:doc_rows], positions < doc_lengths[0], labels
    )
    dproj = jnp.concatenate([grad_doc, grad_query])

    grads, dbi, datt, dsum, dvec = rows_backward(
        dproj, enc, hat2, inv2, packed_w, act, slope, low1, hat1, inv1, att, vectors
    )
    grad_mixed = lax.all_to_all(datt, "fsdp", 0, 0, tiled=True)
    pair_args = (query_log, key, value, grad_mixed, mixed_full, cosine, sine)

    n_dp = lax.axis_size("dp")
    z, x = lax.axis_index("dp") // 2, lax.axis_index("dp") % 2
    core, y = mine % 2, mine // 2
    pick = lambda value, index, axis: lax.dynamic_index_in_dim(value, index, axis, False)
    middle = grads.shape[1] // 2 // LANES * LANES
    by_device = grads.reshape(n_dp // 2, 2, 2, 2, split, -1)
    across = [(d, d ^ 1) for d in range(n_dp)]
    add = lambda one, two: one.astype(F32) + two.astype(F32)
    from_core = lax.ppermute(pick(by_device, 1 - core, 3), "fsdp", other_core(parts))
    own = lambda columns: pick(by_device, core, 3)[..., columns]
    left, right = slice(0, middle), slice(middle, None)
    sum_left = add(own(left), from_core[..., left])
    sum_right = add(own(right), from_core[..., right])
    out_x = pick(sum_left, 1 - x, 1).astype(BF)
    out_y = pick(sum_right, 1 - y, 2).astype(BF)
    out_x, out_y, *pair_args = lax.optimization_barrier((out_x, out_y) + pair_args)
    left_x = lax.ppermute(out_x, "dp", across)
    right_y = lax.ppermute(out_y, "fsdp", other_chip(parts))
    grads_pair = list(attend_back(0, *pair_args, doc_rows))
    left_x, right_y, grads_pair[0] = lax.optimization_barrier((left_x, right_y, grads_pair[0]))
    sum_left = add(pick(sum_left, x, 1), left_x)
    sum_right = add(pick(sum_right, y, 2), right_y)
    out_y = pick(sum_left, 1 - y, 1).astype(BF)
    out_x = pick(sum_right, 1 - x, 1).astype(BF)
    out_x, out_y, grads_pair[0], *pair_args = lax.optimization_barrier(
        (out_x, out_y, grads_pair[0], *pair_args)
    )
    left_y = lax.ppermute(out_y, "fsdp", other_chip(parts))
    right_x = lax.ppermute(out_x, "dp", across)
    pairs = [grads_pair, list(attend_back(1, *pair_args, doc_rows))]
    left_y, right_x, pairs[1][0] = lax.optimization_barrier((left_y, right_x, pairs[1][0]))
    by_z = jnp.concatenate(
        [add(pick(sum_left, y, 1), left_y), add(pick(sum_right, x, 1), right_x)], axis=-1
    ).astype(BF)
    n_z = n_dp // 2
    grads_own = pick(by_z, z, 0).astype(F32)
    for shift in range(1, n_z):
        along = [(d, (d + 2 * shift) % n_dp) for d in range(n_dp)]
        grads_own += lax.ppermute(pick(by_z, (z + shift) % n_z, 0), "dp", along).astype(F32)

    place = jnp.arange(parts, dtype=jnp.int32)[None, :, None] == mine
    db = jnp.stack([jnp.concatenate([pair[3][i] for pair in pairs]) for i in range(3)])
    db_all = jnp.where(place, db[:, None, :], 0.0).reshape(3, D)
    vector_grads = jnp.concatenate([db_all, dvec[:6]]).reshape(9, -1, split).transpose(1, 0, 2)
    vector_grads = jnp.concatenate(
        [vector_grads.reshape(-1, 9 * split), dbi.reshape(-1, hidden_split)], axis=1
    )
    used = vector_grads.shape[1]
    vector_grads = jnp.pad(vector_grads, ((0, 0), (0, -used % (8 * LANES))))
    vector_grads = vector_grads.reshape(n_dp, parts, 8, -1).transpose(1, 0, 2, 3)
    grad_low, dw, summed = heads_backward(
        x_all, w_heads, dsum, vector_grads, [entry for pair in pairs for entry in pair[:3]]
    )
    dw_own = dw.reshape(parts, split, 3, width).transpose(2, 1, 0, 3).reshape(3, split, D)
    summed = summed.reshape(-1)
    up_own = jnp.concatenate([grads_own[:, i * D : (i + 1) * D] for i in range(GROUPS)])
    hidden = GROUPS * D
    dwi_own = grads_own[:, hidden : 2 * hidden]
    dwo_own = grads_own[:, 2 * hidden : 2 * hidden + D]
    dwv_own = grads_own[:, 2 * hidden + D :]
    vec_own = [summed[index * split : (index + 1) * split] for index in range(9)]
    dbi_own = summed[9 * split : 9 * split + hidden_split]
    return (
        losses,
        enc[:doc_rows].reshape(1, doc_rows, D),
        enc[doc_rows:].reshape(1, 1, QLEN, D),
        grad_low[:doc_rows].reshape(1, doc_rows, D),
        grad_low[doc_rows:].reshape(1, 1, QLEN, D),
        dw_own[0],
        vec_own[0],
        dw_own[1],
        vec_own[1],
        dw_own[2],
        vec_own[2],
        dwo_own,
        vec_own[3],
        vec_own[4],
        vec_own[5],
        dwi_own,
        dbi_own,
        up_own,
        vec_own[6],
        vec_own[7],
        vec_own[8],
        dwv_own,
    )


def solution(mesh):
    rows = P(AXES, None)
    line = P(AXES)
    doc = P("dp", "fsdp", None)
    query = P("dp", "fsdp", None, None)
    weights = (rows, line) * 4 + (line, line, rows, line, rows, line, line, line, rows)
    return jax.shard_map(
        shards,
        mesh=mesh,
        in_specs=(doc, query, P("dp"), P()) + weights,
        out_specs=(P(), doc, query, doc, query) + weights,
        check_vma=False,
    )
```

```python
import functools
import math

import jax
import jax.numpy as jnp
import numpy as np
from jax import lax
from jax.experimental import pallas as pl
from jax.experimental.pallas import tpu as pltpu
from jax.sharding import PartitionSpec as P

D = 1024
HEAD_DIM = 64
PROJ = 128
QLEN = 32
LANES = 128

norm_eps = 1e-05
vector_eps = 1e-06
rope_base = 10000.0
smooth_temp = 0.05
loss_temp = 0.02
masked_score = -1e30
log2e = math.log2(math.e)
AXES = ("dp", "fsdp")
BF = jnp.bfloat16
F32 = jnp.float32
VMEM_MOST = 60 << 20


def dot_nn(left, right):
    return lax.dot_general(left, right, (((1,), (0,)), ((), ())), preferred_element_type=F32)


def dot_nt(left, right):
    return lax.dot_general(left, right, (((1,), (1,)), ((), ())), preferred_element_type=F32)


def dot_tn(left, right):
    return lax.dot_general(left, right, (((0,), (0,)), ((), ())), preferred_element_type=F32)


def lanes_of(shape):
    return lax.broadcasted_iota(jnp.int32, shape, len(shape) - 1)


def split_three(value):
    high = value.astype(BF)
    rest = value - high.astype(F32)
    middle = rest.astype(BF)
    return high, middle, (rest - middle.astype(F32)).astype(BF)


def params(**more):
    return pltpu.CompilerParams(vmem_limit_bytes=VMEM_MOST, **more)


def rope_tables(parts, doc_rows):
    half_dim = HEAD_DIM // 2
    frequency = rope_base ** (-np.arange(half_dim, dtype=np.float64) / half_dim)
    own = [
        np.concatenate([part * doc_rows + np.arange(doc_rows), np.arange(QLEN)])
        for part in range(parts)
    ]
    angles = np.concatenate(own)[:, None] * frequency[None, :]
    cosine, sine = np.cos(angles), np.sin(angles)
    shape = (parts, doc_rows + QLEN, LANES)
    return (
        np.concatenate([cosine] * 4, axis=1).astype(np.float32).reshape(shape),
        np.concatenate([-sine, sine, -sine, sine], axis=1).astype(np.float32).reshape(shape),
    )


def turn(tile, cosine, sine):
    first = lanes_of(tile.shape) % HEAD_DIM < HEAD_DIM // 2
    partner = jnp.where(first, pltpu.roll(tile, LANES - 32, 1), pltpu.roll(tile, 32, 1))
    return tile * cosine + partner * sine


class Exchange:
    def __init__(self, axis, size, send, recv):
        self.axis, self.size, self.send, self.recv = axis, size, send, recv
        self.me = lax.axis_index(axis)
        self.going = []

    def to(self, offset):
        return lax.rem(self.me + offset, self.size)

    def source(self, offset):
        return lax.rem(self.me - offset + self.size, self.size)

    def start(self, source_of, target_of):
        for offset in range(1, self.size):
            partner = self.to(offset)
            copy = pltpu.make_async_remote_copy(
                src_ref=source_of(partner),
                dst_ref=target_of(offset),
                send_sem=self.send.at[offset - 1],
                recv_sem=self.recv.at[offset - 1],
                device_id={self.axis: partner},
                device_id_type=pl.DeviceIdType.MESH,
            )
            copy.start()
            self.going.append(copy)

    def arrived(self):
        for copy in self.going:
            copy.wait_recv()

    def sent(self):
        for copy in self.going:
            copy.wait_send()


def greet(sizes):
    barrier = pltpu.get_barrier_semaphore()
    for axis, size in sizes.items():
        for offset in range(1, size):
            partner = lax.rem(lax.axis_index(axis) + offset, size)
            pl.semaphore_signal(
                barrier,
                inc=1,
                device_id={axis: partner},
                device_id_type=pl.DeviceIdType.MESH,
            )
    pl.semaphore_wait(barrier, sum(size - 1 for size in sizes.values()))


class Sent:
    def __init__(self, source, target, axis, index, send, recv):
        self.copy = pltpu.make_async_remote_copy(
            src_ref=source,
            dst_ref=target,
            send_sem=send,
            recv_sem=recv,
            device_id={axis: index},
            device_id_type=pl.DeviceIdType.MESH,
        )

    def start(self):
        self.copy.start()
        return self


pieces_along_y = 5


def start_kernel(n_dp, n_fs, x_ref, w_ref, v_ref, x_all, w_all, v_all, *sems):
    (
        chip_send,
        chip_recv,
        core_send,
        core_recv,
        own_sem,
        *sems,
    ) = sems
    me, my_dp = lax.axis_index("fsdp"), lax.axis_index("dp")
    core, chip = lax.rem(me, 2), me // 2
    other_core = chip * 2 + 1 - core
    other_chip = (1 - chip) * 2 + core
    over = [
        Exchange(axis, n_dp if axis == "dp" else n_fs, sems[2 * i], sems[2 * i + 1])
        for i, axis in enumerate(("fsdp", "fsdp", "dp", "dp"))
    ]
    greet({"dp": n_dp, "fsdp": n_fs})
    over[0].start(lambda partner: w_ref.at[partner], lambda offset: w_all.at[my_dp, me])
    over[1].start(lambda partner: v_ref, lambda offset: v_all.at[my_dp, me])
    piece = x_ref.shape[0] // pieces_along_y
    spans = [pl.ds(at * piece, piece) for at in range(pieces_along_y)]
    along_y = [
        Sent(
            x_ref.at[span],
            x_all.at[me, span],
            "fsdp",
            other_chip,
            chip_send.at[at],
            chip_recv.at[at],
        ).start()
        for at, span in enumerate(spans)
    ]
    own = [
        pltpu.make_async_copy(w_ref.at[me], w_all.at[my_dp, me], own_sem.at[0]),
        pltpu.make_async_copy(v_ref, v_all.at[my_dp, me], own_sem.at[1]),
        pltpu.make_async_copy(x_ref, x_all.at[me], own_sem.at[2]),
    ]
    for copy in own:
        copy.start()
    last = pieces_along_y
    to_core = [
        Sent(
            x_ref, x_all.at[me], "fsdp", other_core, core_send.at[last], core_recv.at[last]
        ).start()
    ]
    own[0].wait()
    own[1].wait()
    over[0].arrived()
    over[1].arrived()
    over[2].start(lambda partner: w_all.at[my_dp], lambda offset: w_all.at[my_dp])
    over[3].start(lambda partner: v_all.at[my_dp], lambda offset: v_all.at[my_dp])
    for at, span in enumerate(spans):
        along_y[at].copy.wait_recv()
        to_core.append(
            Sent(
                x_all.at[other_chip, span],
                x_all.at[other_chip, span],
                "fsdp",
                other_core,
                core_send.at[at],
                core_recv.at[at],
            ).start()
        )
    for one in to_core:
        one.copy.wait_recv()
    over[2].arrived()
    over[3].arrived()
    own[2].wait()
    for exchange in over:
        exchange.sent()
    for one in along_y + to_core:
        one.copy.wait_send()


def gather_start(rows_in, w_split, vector_tile):
    n_dp, n_fs = lax.axis_size("dp"), lax.axis_size("fsdp")
    anywhere = pl.BlockSpec(memory_space=pl.ANY)
    dma = lambda axis: [pltpu.SemaphoreType.DMA(((n_dp if axis == "dp" else n_fs) - 1,))] * 2
    return pl.pallas_call(
        functools.partial(start_kernel, n_dp, n_fs),
        in_specs=[anywhere] * 3,
        out_specs=[anywhere] * 3,
        out_shape=[
            jax.ShapeDtypeStruct((n_fs,) + rows_in.shape, BF),
            jax.ShapeDtypeStruct((n_dp,) + w_split.shape, BF),
            jax.ShapeDtypeStruct((n_dp, n_fs) + vector_tile.shape, F32),
        ],
        scratch_shapes=[
            pltpu.SemaphoreType.DMA((pieces_along_y,)),
            pltpu.SemaphoreType.DMA((pieces_along_y,)),
            pltpu.SemaphoreType.DMA((pieces_along_y + 1,)),
            pltpu.SemaphoreType.DMA((pieces_along_y + 1,)),
            pltpu.SemaphoreType.DMA((3,)),
        ]
        + [sem for axis in ("fsdp", "fsdp", "dp", "dp") for sem in dma(axis)],
        compiler_params=params(collective_id=3, has_side_effects=True),
        name="gather_start",
    )(rows_in, w_split, vector_tile)


def heads_kernel(doc_rows, len_ref, x_ref, w_ref, b_ref, cos_ref, sin_ref, q_ref, k_ref, v_ref):
    part = pl.program_id(0)
    rows = x_ref.shape[1]
    cosine, sine = cos_ref[0], sin_ref[0]
    lane = lanes_of((rows, LANES))
    row = lax.broadcasted_iota(jnp.int32, (rows, LANES), 0)
    allowed = (row >= doc_rows) | (part * doc_rows + row < len_ref[0])
    mask = jnp.where(allowed, 0.0, masked_score)
    width = w_ref.shape[1] // 3
    line = dot_nn(x_ref[0], w_ref[...]) + b_ref[...]
    for pair in range(width // LANES):
        here = pair * LANES
        query = turn(line[:, here : here + LANES], cosine, sine) * (log2e * HEAD_DIM**-0.5)
        key = turn(line[:, width + here : width + here + LANES], cosine, sine)
        value = line[:, 2 * width + here : 2 * width + here + LANES]
        for half in range(2):
            if half:
                query, key, value = (pltpu.roll(entry, 64, 1) for entry in (query, key, value))
            q_ref[2 * pair + half] = jnp.where(
                lane < 64, query, jnp.where(lane == 64, 1.0, 0.0)
            ).astype(BF)
            k_ref[2 * pair + half] = jnp.where(
                lane < 64, key, jnp.where(lane == 64, mask, jnp.where(lane < 68, 1.0, 0.0))
            ).astype(BF)
            v_ref[2 * pair + half] = jnp.where(
                lane < 64, value, jnp.where(lane < 67, 1.0, 0.0)
            ).astype(BF)


def project_heads(length, x_all, w_heads, b_heads, cosine, sine, doc_rows):
    parts, rows, _ = x_all.shape
    heads = w_heads.shape[1] // 3 // HEAD_DIM
    block = pl.BlockSpec((heads, rows, LANES), lambda part: (0, part, 0))
    shape = jax.ShapeDtypeStruct((heads, parts * rows, LANES), BF)
    table = pl.BlockSpec((1, rows, LANES), lambda part: (part, 0, 0))
    return pl.pallas_call(
        functools.partial(heads_kernel, doc_rows),
        grid=(parts,),
        in_specs=[
            pl.BlockSpec(memory_space=pltpu.SMEM),
            pl.BlockSpec((1, rows, D), lambda part: (part, 0, 0)),
            pl.BlockSpec(w_heads.shape, lambda part: (0, 0)),
            pl.BlockSpec(b_heads.shape, lambda part: (0, 0)),
            table,
            table,
        ],
        out_specs=[block] * 3,
        out_shape=[shape] * 3,
        compiler_params=params(),
        name="project_heads",
    )(length, x_all, w_heads, b_heads, cosine, sine)


def attend_rows(query, chunks):
    largest = jnp.full((query.shape[0], 1), -1e38, F32)
    total = jnp.zeros((query.shape[0], LANES), F32)
    for key, value in chunks:
        scores = dot_nt(query, key())
        newest = jnp.maximum(largest, jnp.max(scores, axis=1, keepdims=True))
        powers = jnp.exp2(scores - newest).astype(BF)
        total = total * jnp.exp2(largest - newest) + dot_nn(powers, value())
        largest = newest
    row_sum = total[:, 64:65]
    return total / row_sum, largest + jnp.log2(row_sum)


def attend_kernel(
    doc_rows, parts, q_ref, k_ref, v_ref, ko_ref, vo_ref, o_ref, full_ref, qa_ref
):
    rows = doc_rows + QLEN
    for span, own in ((slice(0, doc_rows), False), (slice(doc_rows, rows), True)):
        mixed = []
        for head in range(2):
            query = q_ref[head, span, :]
            lane = lanes_of(query.shape)
            if own:
                chunks = [(lambda: ko_ref[head], lambda: vo_ref[head])]
            else:
                chunks = [
                    (
                        lambda part=part: k_ref[head, part * rows : part * rows + doc_rows, :],
                        lambda part=part: v_ref[head, part * rows : part * rows + doc_rows, :],
                    )
                    for part in range(parts)
                ]
            out, log_sum = attend_rows(query, chunks)
            mixed.append(out)
            high, middle, low = split_three(-log_sum)
            qa_ref[head, span, :] = jnp.where(
                lane == 65,
                high,
                jnp.where(lane == 66, middle, jnp.where(lane == 67, low, query)),
            )
        joined = jnp.where(lanes_of(mixed[0].shape) < 64, mixed[0], pltpu.roll(mixed[1], 64, 1))
        full_ref[0, span, :] = joined
        o_ref[0, span, :] = joined.astype(BF)


def attend(query, key, value, parts, doc_rows):
    heads, total, _ = query.shape
    rows = total // parts
    own_at = rows // QLEN
    mine = pl.BlockSpec((2, rows, LANES), lambda pair, part: (pair, part, 0))
    whole = pl.BlockSpec((2, total, LANES), lambda pair, part: (pair, 0, 0))
    own = pl.BlockSpec((2, QLEN, LANES), lambda pair, part: (pair, part * own_at + own_at - 1, 0))
    flat = pl.BlockSpec((1, rows, LANES), lambda pair, part: (part, 0, pair))
    flops = 4 * heads * total * total * 256
    return pl.pallas_call(
        functools.partial(attend_kernel, doc_rows, parts),
        grid=(heads // 2, parts),
        in_specs=[mine, whole, whole, own, own],
        out_specs=[flat, flat, mine],
        out_shape=[
            jax.ShapeDtypeStruct((parts, rows, heads * HEAD_DIM), BF),
            jax.ShapeDtypeStruct((parts, rows, heads * HEAD_DIM), F32),
            jax.ShapeDtypeStruct(query.shape, BF),
        ],
        compiler_params=params(),
        cost_estimate=pl.CostEstimate(flops=flops, bytes_accessed=1 << 24, transcendentals=0),
        name="attend",
    )(query, key, value, key, value)


def attend_back_kernel(
    halves,
    doc_rows,
    parts,
    q_ref,
    k_ref,
    v_ref,
    ko_ref,
    vo_ref,
    do_ref,
    o_ref,
    cos_ref,
    sin_ref,
    dq_ref,
    dk_ref,
    dv_ref,
    sums_ref,
    dk_doc,
    dv_doc,
    dk_own,
    dv_own,
):
    rows = doc_rows + QLEN
    at = pl.program_id(0)

    @pl.when(at == 0)
    def _():
        dk_doc[...] = jnp.zeros_like(dk_doc)
        dv_doc[...] = jnp.zeros_like(dv_doc)
        sums_ref[...] = jnp.zeros_like(sums_ref)

    for span, own in ((slice(0, doc_rows), False), (slice(doc_rows, rows), True)):
        grad_pair = do_ref[0, span, :]
        lane = lanes_of(grad_pair.shape)
        product = grad_pair.astype(F32) * o_ref[0, span, :]
        turned = pltpu.roll(grad_pair.astype(F32), 64, 1).astype(BF)
        joined = jnp.zeros(grad_pair.shape, F32)
        for head in halves:
            query = q_ref[head, span, :]
            inside = lane < 64 if head == 0 else lane >= 64
            row_dot = jnp.sum(jnp.where(inside, product, 0.0), axis=1, keepdims=True)
            high, middle, low = split_three(-row_dot)
            grad = jnp.where(
                lane < 64,
                turned if head else grad_pair,
                jnp.where(
                    lane == 64,
                    high,
                    jnp.where(
                        lane == 65, middle, jnp.where(lane == 66, low, jnp.zeros_like(grad_pair))
                    ),
                ),
            )
            query_t, grad_t = query.T, grad.T
            grad_query = jnp.zeros(query.shape, F32)
            for part in range(1 if own else parts):
                if own:
                    key, value = ko_ref[head], vo_ref[head]
                else:
                    key = k_ref[head, part * rows : part * rows + doc_rows, :]
                    value = v_ref[head, part * rows : part * rows + doc_rows, :]
                powers = jnp.exp2(dot_nt(query, key))
                grad_scores = (powers * dot_nt(grad, value)).astype(BF)
                if own:
                    dv_own[head, at] = dot_nn(grad_t, powers.astype(BF))
                    dk_own[head, at] = dot_nn(query_t, grad_scores)
                else:
                    dv_doc[head, part] += dot_nn(grad_t, powers.astype(BF))
                    dk_doc[head, part] += dot_nn(query_t, grad_scores)
                grad_query += dot_nn(grad_scores, key)
            joined = jnp.where(inside, pltpu.roll(grad_query, 64, 1) if head else grad_query, joined)
        joined = joined * HEAD_DIM**-0.5
        low = turn(joined, cos_ref[at, span, :], -sin_ref[at, span, :]).astype(BF)
        dq_ref[0, span, :] = low
        sums_ref[0:1, :] += column_sum(low.astype(F32))

    @pl.when(at == parts - 1)
    def _():
        def both(kept, part):
            sides = [kept[head, part].T for head in halves]
            lane = lanes_of(sides[0].shape)
            if len(halves) == 2:
                return jnp.where(lane < 64, sides[0], pltpu.roll(sides[1], 64, 1))
            if halves[0]:
                return jnp.where(lane < 64, 0.0, pltpu.roll(sides[0], 64, 1))
            return jnp.where(lane < 64, sides[0], 0.0)

        for part in range(parts):
            for span, keys, values in (
                (slice(0, doc_rows), dk_doc, dv_doc),
                (slice(doc_rows, rows), dk_own, dv_own),
            ):
                grad_key = both(keys, part) * (1.0 / log2e)
                low = turn(grad_key, cos_ref[part, span, :], -sin_ref[part, span, :]).astype(BF)
                dk_ref[part, span, :] = low
                sums_ref[1:2, :] += column_sum(low.astype(F32))
                low = both(values, part).astype(BF)
                dv_ref[part, span, :] = low
                sums_ref[2:3, :] += column_sum(low.astype(F32))


def attend_back(pair, halves, query, key, value, grad, mixed, cosine, sine, doc_rows):
    heads, total, _ = query.shape
    parts, rows, width = grad.shape
    own_at = rows // QLEN
    mine = pl.BlockSpec((2, rows, LANES), lambda part: (pair, part, 0))
    whole = pl.BlockSpec((2, total, LANES), lambda part: (pair, 0, 0))
    own = pl.BlockSpec((2, QLEN, LANES), lambda part: (pair, part * own_at + own_at - 1, 0))
    flat = pl.BlockSpec((1, rows, LANES), lambda part: (part, 0, pair))
    table = pl.BlockSpec((parts, rows, LANES), lambda part: (0, 0, 0))
    full = pl.BlockSpec((parts, rows, LANES), lambda part: (0, 0, 0))
    shape = jax.ShapeDtypeStruct((parts, rows, LANES), BF)
    return pl.pallas_call(
        functools.partial(attend_back_kernel, halves, doc_rows, parts),
        grid=(parts,),
        in_specs=[mine, whole, whole, own, own, flat, flat, table, table],
        out_specs=[
            pl.BlockSpec((1, rows, LANES), lambda part: (part, 0, 0)),
            full,
            full,
            pl.BlockSpec((8, LANES), lambda part: (0, 0)),
        ],
        out_shape=[shape] * 3 + [jax.ShapeDtypeStruct((8, LANES), F32)],
        scratch_shapes=[
            pltpu.VMEM((2, parts, LANES, doc_rows), F32),
            pltpu.VMEM((2, parts, LANES, doc_rows), F32),
            pltpu.VMEM((2, parts, LANES, QLEN), F32),
            pltpu.VMEM((2, parts, LANES, QLEN), F32),
        ],
        compiler_params=params(),
        cost_estimate=pl.CostEstimate(
            flops=10 * len(halves) * total * total * 256, bytes_accessed=1 << 24, transcendentals=0
        ),
        name="attend_back",
    )(query, key, value, key, value, grad, mixed, cosine, sine)


def normed(summed):
    centered = summed - jnp.mean(summed, axis=-1, keepdims=True)
    variance = jnp.mean(centered * centered, axis=-1, keepdims=True)
    inverse = lax.rsqrt(variance + norm_eps)
    return centered * inverse, inverse


GROUPS = 4
CHUNK = 512
OWN_ROWS = 32


def joined_up(up_ref):
    size = OWN_ROWS
    pieces = [
        up_ref[at : at + size, group * D : (group + 1) * D]
        for at in range(0, up_ref.shape[0], size)
        for group in range(GROUPS)
    ]
    return jnp.concatenate(pieces, axis=0)


def packed_specs():
    hidden = GROUPS * D
    return {
        "up": pl.BlockSpec((CHUNK // GROUPS, hidden), lambda step: (step, 0)),
        "down": pl.BlockSpec((D, CHUNK), lambda step: (0, hidden // CHUNK + step)),
        "out": pl.BlockSpec((D, D), lambda step: (0, 2 * hidden // D)),
        "vector": pl.BlockSpec((D, LANES), lambda step: (0, (2 * hidden + D) // LANES)),
    }


def rows_kernel(
    att_ref,
    x_ref,
    wo_ref,
    wi_ref,
    wu_ref,
    wv_ref,
    bi_ref,
    vec_ref,
    hat1_ref,
    inv1_ref,
    low1_ref,
    act_ref,
    slope_ref,
    hat2_ref,
    inv2_ref,
    enc_ref,
    proj_ref,
    sum_ref,
):
    step = pl.program_id(0)
    parts, _, width = att_ref.shape

    @pl.when(step == 0)
    def _():
        summed = x_ref[...].astype(F32) + vec_ref[0:1, :]
        for part in range(parts):
            summed += dot_nn(att_ref[part], wo_ref[part * width : (part + 1) * width, :])
        hat, inverse = normed(summed)
        hat1_ref[...] = hat.astype(BF)
        inv1_ref[...] = jnp.broadcast_to(inverse, inv1_ref.shape)
        out = hat * vec_ref[1:2, :] + vec_ref[2:3, :]
        low1_ref[...] = out.astype(BF)
        sum_ref[...] = out + vec_ref[3:4, :]

    up = joined_up(wu_ref)
    inner = dot_nn(low1_ref[...], wi_ref[...]) + bi_ref[...]
    share = 0.5 * lax.erf(inner * math.sqrt(0.5)) + 0.5
    act = (inner * share).astype(BF)
    act_ref[...] = act
    density = jnp.exp(inner * inner * -0.5) * (1.0 / math.sqrt(2.0 * math.pi))
    slope_ref[...] = (share + inner * density).astype(BF)
    sum_ref[...] += dot_nn(act, up)

    @pl.when(step == pl.num_programs(0) - 1)
    def _():
        hat, inverse = normed(sum_ref[...])
        hat2_ref[...] = hat.astype(BF)
        inv2_ref[...] = jnp.broadcast_to(inverse, inv2_ref.shape)
        low = (hat * vec_ref[4:5, :] + vec_ref[5:6, :]).astype(BF)
        enc_ref[...] = low
        proj_ref[...] = dot_nn(low, wv_ref[...])


def rows_forward(att, rows_in, packed, inner_bias, vectors):
    rows = rows_in.shape[0]
    hidden = inner_bias.shape[1]
    chunk = CHUNK
    weights = packed_specs()
    keep = lambda shape: pl.BlockSpec(shape, lambda step: (0,) * len(shape))
    columns = pl.BlockSpec((rows, chunk), lambda step: (0, step))
    wide = jax.ShapeDtypeStruct((rows, D), BF)
    thin = jax.ShapeDtypeStruct((rows, LANES), F32)
    big = jax.ShapeDtypeStruct((rows, hidden), BF)
    return pl.pallas_call(
        rows_kernel,
        grid=(hidden // chunk,),
        in_specs=[
            keep(att.shape),
            keep(rows_in.shape),
            weights["out"],
            weights["down"],
            weights["up"],
            weights["vector"],
            pl.BlockSpec((1, chunk), lambda step: (0, step)),
            keep(vectors.shape),
        ],
        out_specs=[
            keep((rows, D)),
            keep((rows, LANES)),
            keep((rows, D)),
            columns,
            columns,
            keep((rows, D)),
            keep((rows, LANES)),
            keep((rows, D)),
            keep((rows, LANES)),
        ],
        out_shape=[wide, thin, wide, big, big, wide, thin, wide, thin],
        scratch_shapes=[pltpu.VMEM((rows, D), F32)],
        compiler_params=params(),
        cost_estimate=pl.CostEstimate(
            flops=2 * rows * D * (D + 2 * hidden), bytes_accessed=1 << 25, transcendentals=0
        ),
        name="rows_forward",
    )(att, rows_in, packed, packed, packed, packed, inner_bias, vectors)


def norm_back(grad, hat, inverse, gain):
    scaled = grad * gain
    first = jnp.mean(scaled, axis=-1, keepdims=True)
    second = jnp.mean(scaled * hat, axis=-1, keepdims=True)
    return (scaled - first - hat * second) * inverse


def column_sum(value):
    return jnp.sum(value, axis=0, keepdims=True)


def rows_back_kernel(
    dproj_ref,
    enc_ref,
    hat2_ref,
    inv2_ref,
    wv_ref,
    act_ref,
    slope_ref,
    wu_ref,
    wi_ref,
    low1_ref,
    hat1_ref,
    inv1_ref,
    att_ref,
    wo_ref,
    vec_ref,
    keep_ref,
    send_ref,
    dbi_ref,
    datt_ref,
    dsum_ref,
    dvec_ref,
    low_ref,
    total_ref,
    dwv_ref,
    dwo_ref,
    dwu_ref,
    dwi_ref,
    once_sem,
    up_sem,
    down_sem,
):
    step = pl.program_id(0)
    steps = pl.num_programs(0)
    parts, _, width = att_ref.shape
    hidden = GROUPS * D
    slot = lax.rem(step, 2)

    core = lax.rem(lax.axis_index("fsdp"), 2)

    def both(source, rows_at, columns, sem):
        return [
            pltpu.make_async_copy(
                source.at[:, which], target.at[rows_at, :, columns], sem.at[index]
            )
            for index, (which, target) in enumerate(((1 - core, send_ref), (core, keep_ref)))
        ]

    count = dwu_ref.shape[1]
    every = pl.ds(0, keep_ref.shape[0])

    def up_copy(at, place):
        return both(
            dwu_ref.at[place], pl.ds(at * count, count), pl.ds(0, hidden), up_sem.at[place]
        )

    def down_copy(at, place):
        here = pl.ds(pl.multiple_of(hidden + at * CHUNK, CHUNK), CHUNK)
        return both(dwi_ref.at[place], every, here, down_sem.at[place])

    def vector_copy():
        return both(dwv_ref, every, pl.ds(2 * hidden + D, LANES), once_sem.at[0])

    def out_copy():
        return both(dwo_ref, every, pl.ds(2 * hidden, D), once_sem.at[1])

    def start(copies):
        for copy in copies:
            copy.start()

    def wait(copies):
        for copy in copies:
            copy.wait()

    def by_device(value):
        return value.astype(BF).reshape(-1, 2, OWN_ROWS, value.shape[1])

    @pl.when(step == 0)
    def _():
        dproj = dproj_ref[...]
        dwv_ref[...] = by_device(dot_tn(enc_ref[...], dproj))
        start(vector_copy())
        grad = dot_nt(dproj, wv_ref[...])
        hat = hat2_ref[...].astype(F32)
        dvec_ref[4:5, :] = column_sum(grad * hat)
        dvec_ref[5:6, :] = column_sum(grad)
        back = norm_back(grad, hat, inv2_ref[:, :1], vec_ref[4:5, :])
        low = back.astype(BF)
        low_ref[...] = low
        total_ref[...] = back
        dvec_ref[3:4, :] = column_sum(low.astype(F32))

    @pl.when(step >= 2)
    def _():
        wait(up_copy(step - 2, slot))
        wait(down_copy(step - 2, slot))

    low = low_ref[...]
    dinner = (dot_nt(low, joined_up(wu_ref)) * slope_ref[...].astype(F32)).astype(BF)
    dbi_ref[...] = column_sum(dinner.astype(F32))
    up_grad = dot_tn(act_ref[...], low).astype(BF)
    for at in range(0, CHUNK, OWN_ROWS):
        own, group = at // (OWN_ROWS * GROUPS), at // OWN_ROWS % GROUPS
        dwu_ref[slot, own // 2, own % 2, :, group * D : (group + 1) * D] = up_grad[at : at + OWN_ROWS]
    start(up_copy(step, slot))
    dwi_ref[slot] = by_device(dot_tn(low1_ref[...], dinner))
    start(down_copy(step, slot))
    total_ref[...] += dot_nt(dinner, wi_ref[...])

    @pl.when(step == pl.num_programs(0) - 1)
    def _():
        grad = total_ref[...]
        hat = hat1_ref[...].astype(F32)
        dvec_ref[1:2, :] = column_sum(grad * hat)
        dvec_ref[2:3, :] = column_sum(grad)
        back = norm_back(grad, hat, inv1_ref[:, :1], vec_ref[1:2, :])
        dsum_ref[...] = back
        attn_low = back.astype(BF)
        dvec_ref[0:1, :] = column_sum(attn_low.astype(F32))
        for part in range(parts):
            here = slice(part * width, (part + 1) * width)
            size = width // (2 * OWN_ROWS)
            dwo_ref[part * size : (part + 1) * size] = by_device(dot_tn(att_ref[part], attn_low))
            datt_ref[part] = dot_nt(attn_low, wo_ref[here, :]).astype(BF)
        start(out_copy())
        wait(vector_copy())
        for place in range(2):
            wait(up_copy(steps - 2 + place, place))
            wait(down_copy(steps - 2 + place, place))
        wait(out_copy())


def rows_backward(dproj, enc, hat2, inv2, packed, act, slope, low1, hat1, inv1, att, vectors):
    rows, hidden = act.shape
    keep = lambda shape: pl.BlockSpec(shape, lambda step: (0,) * len(shape))
    columns = pl.BlockSpec((rows, CHUNK), lambda step: (0, step))
    bias = pl.BlockSpec((1, CHUNK), lambda step: (0, step))
    weights = packed_specs()
    pairs = packed.shape[0] // (2 * OWN_ROWS)
    half = jax.ShapeDtypeStruct((pairs, OWN_ROWS, packed.shape[1]), BF)
    operands = (
        (dproj, None),
        (enc, None),
        (hat2, None),
        (inv2, None),
        (packed, weights["vector"]),
        (act, columns),
        (slope, columns),
        (packed, weights["up"]),
        (packed, weights["down"]),
        (low1, None),
        (hat1, None),
        (inv1, None),
        (att, None),
        (packed, weights["out"]),
        (vectors, None),
    )
    return pl.pallas_call(
        rows_back_kernel,
        grid=(hidden // CHUNK,),
        in_specs=[keep(entry.shape) if spec is None else spec for entry, spec in operands],
        out_specs=[
            pl.BlockSpec(memory_space=pl.ANY),
            pl.BlockSpec(memory_space=pl.ANY),
            bias,
            keep(att.shape),
            keep((rows, D)),
            keep((8, D)),
        ],
        out_shape=[
            half,
            half,
            jax.ShapeDtypeStruct((1, hidden), F32),
            jax.ShapeDtypeStruct(att.shape, BF),
            jax.ShapeDtypeStruct((rows, D), F32),
            jax.ShapeDtypeStruct((8, D), F32),
        ],
        scratch_shapes=[
            pltpu.VMEM((rows, D), BF),
            pltpu.VMEM((rows, D), F32),
            pltpu.VMEM((pairs, 2, OWN_ROWS, LANES), BF),
            pltpu.VMEM((pairs, 2, OWN_ROWS, D), BF),
            pltpu.VMEM((2, CHUNK // (2 * GROUPS * OWN_ROWS), 2, OWN_ROWS, hidden), BF),
            pltpu.VMEM((2, pairs, 2, OWN_ROWS, CHUNK), BF),
            pltpu.SemaphoreType.DMA((2, 2)),
            pltpu.SemaphoreType.DMA((2, 2)),
            pltpu.SemaphoreType.DMA((2, 2)),
        ],
        compiler_params=params(),
        cost_estimate=pl.CostEstimate(
            flops=4 * rows * D * (D + 2 * hidden), bytes_accessed=1 << 26, transcendentals=0
        ),
        name="rows_backward",
    )(*(entry for entry, _ in operands))


def heads_back_kernel(n_dp, n_fs, pair_of, *refs):
    calls, pairs = len(pair_of), max(pair_of) + 1
    x_ref, w_ref, dsum_ref, vec_ref = refs[:4]
    call_refs = refs[4 : 4 + 3 * calls]
    dx_ref, dw_ref, dvec_ref = refs[4 + 3 * calls : 7 + 3 * calls]
    (
        first_out,
        second_out,
        first_in,
        second_in,
        chip_out,
        chip_in,
        kept_ref,
        dw_out,
        dw_across,
        dw_line,
        dw_in,
        dw_sum,
        vec_in,
        vec_sum,
        vec_last,
        core_send,
        core_recv,
        chip_send,
        chip_recv,
        across_send,
        across_recv,
        along_send,
        along_recv,
        *sems,
    ) = refs[7 + 3 * calls :]
    me, my_dp = lax.axis_index("fsdp"), lax.axis_index("dp")
    core, chip = lax.rem(me, 2), me // 2
    other_core = chip * 2 + 1 - core
    other_chip = (1 - chip) * 2 + core
    over = [
        Exchange(axis, n_dp if axis == "dp" else n_fs, sems[2 * i], sems[2 * i + 1])
        for i, axis in enumerate(("fsdp", "dp", "fsdp"))
    ]
    greet({"dp": n_dp, "fsdp": n_fs})
    width = w_ref.shape[1] // 3
    rows = x_ref.shape[1]
    piece = rows // pieces_along_y

    over[0].start(lambda partner: vec_ref.at[partner], lambda offset: vec_in.at[offset - 1])

    def gradient(index, pair, part):
        found = [
            call_refs[call * 3 + index][part] for call in range(calls) if pair_of[call] == pair
        ]
        return functools.reduce(lambda one, two: one + two, found)

    def back(part):
        total = jnp.zeros((rows, D), F32)
        for index in range(3):
            for pair in range(pairs):
                here = index * width + pair * LANES
                total += dot_nt(gradient(index, pair, part), w_ref[:, here : here + LANES])
        return total

    def to_core(source, target, at):
        return Sent(source, target, "fsdp", other_core, core_send.at[at], core_recv.at[at]).start()

    first_out[...] = back((1 - chip) * 2 + 1 - core).astype(BF)
    first = to_core(first_out, first_in, 0)
    away = back(other_chip)
    first.copy.wait_recv()
    chip_out[...] = (away + first_in[...].astype(F32)).astype(BF)
    along_y = []
    for at in range(pieces_along_y):
        here = pl.ds(at * piece, piece)
        along_y.append(
            Sent(
                chip_out.at[here],
                chip_in.at[here],
                "fsdp",
                other_chip,
                chip_send.at[at],
                chip_recv.at[at],
            ).start()
        )

    block = D // n_dp
    n_z, z, x = n_dp // 2, my_dp // 2, lax.rem(my_dp, 2)
    across, along_z = [], []
    for index in range(3):
        for pair in range(pairs):
            here = slice(pair * LANES, (pair + 1) * LANES)
            total = jnp.zeros((D, LANES), F32)
            for part in range(n_fs):
                total += dot_tn(x_ref[part], gradient(index, pair, part))
            dw_out[index, :, :, :, here] = total.astype(BF).reshape(n_z, 2, block, LANES)
        across.append(
            Sent(
                dw_out.at[index, :, 1 - x],
                dw_across.at[index],
                "dp",
                z * 2 + 1 - x,
                across_send.at[index],
                across_recv.at[index],
            ).start()
        )

    def send_along_z(index):
        across[index].copy.wait_recv()
        dw_line[index] = (dw_out[index, :, x].astype(F32) + dw_across[index].astype(F32)).astype(BF)
        for offset in range(1, n_z):
            partner = lax.rem(z + offset, n_z)
            along_z.append(
                Sent(
                    dw_line.at[index, partner],
                    dw_in.at[index, offset - 1],
                    "dp",
                    partner * 2 + x,
                    along_send.at[index, offset - 1],
                    along_recv.at[index, offset - 1],
                ).start()
            )

    over[0].arrived()
    vec_total = vec_ref[me]
    for offset in range(n_fs - 1):
        vec_total = vec_total + vec_in[offset]
    vec_sum[...] = vec_total
    over[1].start(lambda partner: vec_sum.at[partner], lambda offset: vec_last.at[offset - 1])

    send_along_z(0)
    second_out[...] = back(other_core).astype(BF)
    second = to_core(second_out, second_in, 1)
    send_along_z(1)
    kept_ref[...] = back(me) + dsum_ref[...]
    send_along_z(2)
    second.copy.wait_recv()
    kept_ref[...] += second_in[...].astype(F32)

    over[1].arrived()
    vec_total = vec_sum[my_dp]
    for offset in range(n_dp - 1):
        vec_total = vec_total + vec_last[offset]
    dvec_ref[...] = vec_total

    each = block // n_fs
    mine = dw_ref.at[me]
    for index in range(3):
        total = dw_out[index, z, x].astype(F32) + dw_across[index, z].astype(F32)
        for offset in range(n_z - 1):
            along_z[index * (n_z - 1) + offset].copy.wait_recv()
            total = total + dw_in[index, offset].astype(F32)
        dw_sum[:, :, index * width : (index + 1) * width] = total.reshape(n_fs, each, width)
    dw_ref[me] = dw_sum[me]
    over[2].start(lambda partner: dw_sum.at[partner], lambda offset: mine)
    for at in range(pieces_along_y):
        here = slice(at * piece, (at + 1) * piece)
        along_y[at].copy.wait_recv()
        dx_ref[here, :] = (kept_ref[here, :] + chip_in[here, :].astype(F32)).astype(BF)
    over[2].arrived()
    for exchange in over:
        exchange.sent()
    for one in [first, second] + across + along_y + along_z:
        one.copy.wait_send()


def heads_backward(x_all, w_heads, dsum, vector_grads, pair_of, grads):
    n_dp, n_fs = lax.axis_size("dp"), lax.axis_size("fsdp")
    _, rows, _ = x_all.shape
    whole = pl.BlockSpec(memory_space=pltpu.VMEM)
    block = D // n_dp
    columns = w_heads.shape[1]
    tile = vector_grads.shape[2:]
    line = pltpu.VMEM((rows, D), BF)
    dma = lambda axis: [pltpu.SemaphoreType.DMA(((n_dp if axis == "dp" else n_fs) - 1,))] * 2
    return pl.pallas_call(
        functools.partial(heads_back_kernel, n_dp, n_fs, pair_of),
        in_specs=[whole] * (4 + len(grads)),
        out_specs=[whole] * 3,
        out_shape=[
            jax.ShapeDtypeStruct((rows, D), BF),
            jax.ShapeDtypeStruct((n_fs, block // n_fs, columns), F32),
            jax.ShapeDtypeStruct(tile, F32),
        ],
        scratch_shapes=[line] * 6
        + [
            pltpu.VMEM((rows, D), F32),
            pltpu.VMEM((3, n_dp // 2, 2, block, columns // 3), BF),
            pltpu.VMEM((3, n_dp // 2, block, columns // 3), BF),
            pltpu.VMEM((3, n_dp // 2, block, columns // 3), BF),
            pltpu.VMEM((3, n_dp // 2 - 1, block, columns // 3), BF),
            pltpu.VMEM((n_fs, block // n_fs, columns), F32),
            pltpu.VMEM((n_fs - 1, n_dp) + tile, F32),
            pltpu.VMEM((n_dp,) + tile, F32),
            pltpu.VMEM((n_dp - 1,) + tile, F32),
            pltpu.SemaphoreType.DMA((2,)),
            pltpu.SemaphoreType.DMA((2,)),
            pltpu.SemaphoreType.DMA((pieces_along_y,)),
            pltpu.SemaphoreType.DMA((pieces_along_y,)),
            pltpu.SemaphoreType.DMA((3,)),
            pltpu.SemaphoreType.DMA((3,)),
            pltpu.SemaphoreType.DMA((3, n_dp // 2 - 1)),
            pltpu.SemaphoreType.DMA((3, n_dp // 2 - 1)),
        ]
        + [sem for axis in ("fsdp", "dp", "fsdp") for sem in dma(axis)],
        compiler_params=params(collective_id=2, has_side_effects=True),
        name="heads_backward",
    )(x_all, w_heads, dsum, vector_grads, *grads)


widths = (PROJ, PROJ * 3 // 4, PROJ // 2)
token_block = 1024


def unit(projected, columns):
    leading = jnp.where(lanes_of(projected.shape) < columns, projected, 0.0)
    inverse = lax.rsqrt(jnp.sum(leading * leading, axis=-1, keepdims=True) + vector_eps)
    return leading, inverse, (leading * inverse).astype(BF)


def unit_back(leading, inverse, grad):
    along = jnp.sum(leading * grad, axis=-1, keepdims=True)
    return grad * inverse - leading * (along * (inverse * inverse * inverse))


def exact(left, right):
    return lax.dot_general(
        left,
        right,
        (((1,), (0,)), ((), ())),
        precision=lax.Precision.HIGHEST,
        preferred_element_type=F32,
    )


def maxsim_kernel(
    n_dp,
    n_fs,
    pq_ref,
    pd_ref,
    mask_ref,
    label_ref,
    loss_ref,
    dq_ref,
    dd_ref,
    all_ref,
    power_ref,
    part_ref,
    score_ref,
    grad_ref,
    first_ref,
    total_ref,
    second_ref,
    *sems,
):
    tokens = n_dp * n_fs * QLEN
    blocks = tokens // token_block
    spots = label_ref.shape[1]
    my_dp, my_fs = lax.axis_index("dp"), lax.axis_index("fsdp")
    over = [
        Exchange(axis, n_dp if axis == "dp" else n_fs, sems[2 * i], sems[2 * i + 1])
        for i, axis in enumerate(("dp", "fsdp", "fsdp", "dp", "fsdp", "dp"))
    ]
    greet({"dp": n_dp, "fsdp": n_fs})

    own = all_ref.at[my_fs, my_dp]
    all_ref[my_fs, my_dp] = pq_ref[...]
    over[0].start(lambda partner: own, lambda offset: own)
    docs = [unit(pd_ref[...], columns) for columns in widths]
    over[0].arrived()
    over[1].start(lambda partner: all_ref.at[my_fs], lambda offset: all_ref.at[my_fs])
    over[1].arrived()

    def queries(block):
        every = all_ref[...].reshape(tokens, PROJ)
        return every[block * token_block : (block + 1) * token_block]

    def powers(index, block):
        similar = dot_nt(docs[index][2], unit(queries(block), widths[index])[2])
        return jnp.exp2(similar * (log2e / smooth_temp)) * mask_ref[:, :1]

    mine = part_ref.at[my_fs]
    part_ref[my_fs] = jnp.ones((8, tokens), F32)
    for block in range(blocks):
        here = slice(block * token_block, (block + 1) * token_block)
        for index in range(3):
            power = powers(index, block)
            if blocks == 1:
                power_ref[index] = power
            part_ref[my_fs, index : index + 1, here] = column_sum(power)
    over[2].start(lambda partner: mine, lambda offset: mine)
    over[2].arrived()
    total = part_ref[0]
    for source in range(1, n_fs):
        total = total + part_ref[source]

    token_of = lax.broadcasted_iota(jnp.int32, (tokens, spots), 0) // QLEN
    pool = jnp.where(token_of == lanes_of((tokens, spots)), 1.0, 0.0)
    score = exact(jnp.log(total), pool) * (smooth_temp / QLEN)
    score_ref[my_dp] = score
    row = score_ref.at[my_dp]
    over[3].start(lambda partner: row, lambda offset: row)
    over[3].arrived()
    logits = score_ref[...] * (1.0 / loss_temp)
    largest = jnp.max(logits, axis=0)
    log_sum = largest + jnp.log(jnp.sum(jnp.exp(logits - largest[None]), axis=0))
    label = label_ref[...]
    picked = jnp.zeros_like(log_sum)
    for index in range(n_dp):
        picked += jnp.where(label == index, logits[index], 0.0)
    loss_ref[...] = log_sum - picked
    dscore = jnp.exp(score * (1.0 / loss_temp) - log_sum) - jnp.where(label == my_dp, 1.0, 0.0)
    query_of = lax.broadcasted_iota(jnp.int32, (spots, tokens), 0)
    spread = jnp.where(lanes_of((spots, tokens)) // QLEN == query_of, 1.0, 0.0)
    factor = exact(dscore * (1.0 / (loss_temp * QLEN)), spread) / total

    grad_doc = [jnp.zeros(pd_ref.shape, F32)] * 3
    for block in range(blocks):
        here = slice(block * token_block, (block + 1) * token_block)
        grad_query = jnp.zeros((token_block, PROJ), F32)
        for index, columns in enumerate(widths):
            leading, inverse, vector = unit(queries(block), columns)
            power = power_ref[index] if blocks == 1 else powers(index, block)
            dsim = (power * factor[index : index + 1, here]).astype(BF)
            grad_query += unit_back(leading, inverse, dot_tn(dsim, docs[index][2]))
            grad_doc[index] += dot_nn(dsim, vector)
        if blocks == 1:
            grad_ref[...] = grad_query.reshape(grad_ref.shape)
        else:
            flat = block * token_block // QLEN
            count = token_block // QLEN
            grad_ref[flat // n_dp, flat % n_dp : flat % n_dp + count] = grad_query.reshape(
                count, QLEN, PROJ
            )
    over[4].start(lambda partner: grad_ref.at[partner], lambda offset: first_ref.at[offset - 1])
    dd = jnp.zeros(pd_ref.shape, F32)
    for index in range(3):
        dd += unit_back(docs[index][0], docs[index][1], grad_doc[index])
    dd_ref[...] = dd.astype(BF)
    over[4].arrived()
    summed = grad_ref[my_fs]
    for offset in range(n_fs - 1):
        summed = summed + first_ref[offset]
    total_ref[...] = summed
    over[5].start(lambda partner: total_ref.at[partner], lambda offset: second_ref.at[offset - 1])
    over[5].arrived()
    dq = total_ref[my_dp]
    for offset in range(n_dp - 1):
        dq = dq + second_ref[offset]
    dq_ref[...] = dq.astype(BF)
    for exchange in over:
        exchange.sent()


def maxsim(proj_query, proj_doc, doc_allowed, labels):
    n_dp, n_fs = lax.axis_size("dp"), lax.axis_size("fsdp")
    query_total = n_dp * n_fs
    tokens = query_total * QLEN
    blocks = tokens // token_block
    spots = -(-query_total // LANES) * LANES
    doc_rows = proj_doc.shape[0]
    ordered = jnp.transpose(labels).reshape(1, query_total)
    ordered = jnp.pad(ordered, ((0, 0), (0, spots - query_total)), constant_values=-1)
    mask = jnp.broadcast_to(doc_allowed[:, None], (doc_rows, LANES)).astype(F32)
    dma = lambda axis: [pltpu.SemaphoreType.DMA(((n_dp if axis == "dp" else n_fs) - 1,))] * 2
    whole = pl.BlockSpec(memory_space=pltpu.VMEM)
    loss, grad_query, grad_doc = pl.pallas_call(
        functools.partial(maxsim_kernel, n_dp, n_fs),
        in_specs=[whole] * 4,
        out_specs=[whole] * 3,
        out_shape=[
            jax.ShapeDtypeStruct((8, spots), F32),
            jax.ShapeDtypeStruct((QLEN, PROJ), BF),
            jax.ShapeDtypeStruct((doc_rows, PROJ), BF),
        ],
        scratch_shapes=[
            pltpu.VMEM((n_fs, n_dp, QLEN, PROJ), F32),
            pltpu.VMEM((3, doc_rows, token_block) if blocks == 1 else (3, 8, LANES), F32),
            pltpu.VMEM((n_fs, 8, tokens), F32),
            pltpu.VMEM((n_dp, 8, spots), F32),
            pltpu.VMEM((n_fs, n_dp, QLEN, PROJ), F32),
            pltpu.VMEM((n_fs - 1, n_dp, QLEN, PROJ), F32),
            pltpu.VMEM((n_dp, QLEN, PROJ), F32),
            pltpu.VMEM((n_dp - 1, QLEN, PROJ), F32),
        ]
        + [sem for axis in ("dp", "fsdp", "fsdp", "dp", "fsdp", "dp") for sem in dma(axis)],
        compiler_params=params(collective_id=1, has_side_effects=True),
        name="maxsim",
    )(proj_query, proj_doc, mask, jnp.broadcast_to(ordered, (8, spots)))
    losses = loss[:3, :query_total].reshape(3, n_fs, n_dp).transpose(0, 2, 1)
    return losses.reshape(3, query_total), grad_query, grad_doc


def other_core(parts):
    return [(part, part ^ 1) for part in range(parts)]


def other_chip(parts):
    return [(part, part ^ 2) for part in range(parts)]


def shards(
    doc_tokens,
    query_tokens,
    doc_lengths,
    labels,
    query_weight,
    query_bias,
    key_weight,
    key_bias,
    value_weight,
    value_bias,
    out_weight,
    out_bias,
    first_gain,
    first_shift,
    inner_weight,
    inner_bias,
    outer_weight,
    outer_bias,
    second_gain,
    second_shift,
    vector_weight,
):
    parts = lax.axis_size("fsdp")
    mine = lax.axis_index("fsdp")
    doc_rows = doc_tokens.shape[1]
    rows = doc_rows + QLEN
    width = D // parts
    split = query_weight.shape[0]

    w_split = jnp.stack(
        [
            jnp.concatenate(
                [
                    entry[:, part * width : (part + 1) * width]
                    for entry in (query_weight, key_weight, value_weight)
                ],
                axis=1,
            )
            for part in range(parts)
        ]
    )
    small = [
        query_bias,
        key_bias,
        value_bias,
        out_bias,
        first_gain,
        first_shift,
        outer_bias,
        second_gain,
        second_shift,
    ]
    hidden_split = inner_bias.shape[0]
    line = jnp.concatenate(small + [inner_bias]).astype(F32)
    line = jnp.pad(line, (0, -line.shape[0] % (8 * LANES))).reshape(8, -1)
    rows_in = jnp.concatenate([doc_tokens.reshape(doc_rows, D), query_tokens.reshape(QLEN, D)])
    own_up = [outer_weight[group * split : (group + 1) * split] for group in range(GROUPS)]
    packed_own = jnp.concatenate(own_up + [inner_weight, out_weight, vector_weight], axis=1)
    x_all, w_heads, packed = gather_start(rows_in, w_split, line)
    packed_own, x_all = lax.optimization_barrier((packed_own, x_all))
    packed_w = lax.all_gather(packed_own, AXES, axis=0, tiled=True)
    w_heads = w_heads.reshape(D, 3 * width)
    packed = packed.reshape(lax.axis_size("dp") * parts, -1)

    def vector(index):
        return packed[:, index * split : (index + 1) * split].reshape(-1)

    inner_at = len(small) * split
    inner_vec = packed[:, inner_at : inner_at + hidden_split].reshape(1, -1)
    vectors = jnp.stack([vector(i) for i in (3, 4, 5, 6, 7, 8)] + [jnp.zeros((D,), F32)] * 2)
    b_heads = jnp.concatenate(
        [lax.dynamic_slice(vector(i), (mine * width,), (width,)) for i in range(3)]
    ).reshape(1, -1)

    tables = rope_tables(parts, doc_rows)
    cosine, sine = jnp.asarray(tables[0]), jnp.asarray(tables[1])
    query, key, value = project_heads(
        doc_lengths, x_all, w_heads, b_heads, cosine, sine, doc_rows
    )
    mixed, mixed_full, query_log = attend(query, key, value, parts, doc_rows)
    att = lax.all_to_all(mixed, "fsdp", 0, 0, tiled=True)
    hat1, inv1, low1, act, slope, hat2, inv2, enc, proj = rows_forward(
        att, rows_in, packed_w, inner_vec, vectors
    )

    positions = mine * doc_rows + jnp.arange(doc_rows, dtype=jnp.int32)
    losses, grad_query, grad_doc = maxsim(
        proj[doc_rows:], proj[:doc_rows], positions < doc_lengths[0], labels
    )
    dproj = jnp.concatenate([grad_doc, grad_query])

    keep, send, dbi, datt, dsum, dvec = rows_backward(
        dproj, enc, hat2, inv2, packed_w, act, slope, low1, hat1, inv1, att, vectors
    )
    grad_mixed = lax.all_to_all(datt, "fsdp", 0, 0, tiled=True)
    pair_args = (query_log, key, value, grad_mixed, mixed_full, cosine, sine)

    n_dp = lax.axis_size("dp")
    z, x = lax.axis_index("dp") // 2, lax.axis_index("dp") % 2
    core, y = mine % 2, mine // 2
    pick = lambda value, index, axis: lax.dynamic_index_in_dim(value, index, axis, False)
    middle = keep.shape[2] // 2 // LANES * LANES
    n_z = n_dp // 2
    whole = (n_z, 2, 2, split, keep.shape[2])
    across = [(d, d ^ 1) for d in range(n_dp)]
    add = lambda one, two: one.astype(F32) + two.astype(F32)
    keep = keep.reshape(whole)
    from_core = lax.ppermute(send, "fsdp", other_core(parts)).reshape(whole)
    left, right = slice(0, middle), slice(middle, None)
    sum_left = add(keep[..., left], from_core[..., left])
    sum_right = add(keep[..., right], from_core[..., right])
    out_x = pick(sum_left, 1 - x, 1).astype(BF)
    out_y = pick(sum_right, 1 - y, 2).astype(BF)
    out_x, out_y, *pair_args = lax.optimization_barrier((out_x, out_y) + pair_args)
    left_x = lax.ppermute(out_x, "dp", across)
    right_y = lax.ppermute(out_y, "fsdp", other_chip(parts))
    calls = [list(attend_back(0, (0, 1), *pair_args, doc_rows))]
    left_x, right_y, calls[0][0] = lax.optimization_barrier((left_x, right_y, calls[0][0]))
    sum_left = add(pick(sum_left, x, 1), left_x)
    sum_right = add(pick(sum_right, y, 2), right_y)
    out_y = pick(sum_left, 1 - y, 1).astype(BF)
    out_x = pick(sum_right, 1 - x, 1).astype(BF)
    out_x, out_y, calls[0][0], *pair_args = lax.optimization_barrier(
        (out_x, out_y, calls[0][0], *pair_args)
    )
    left_y = lax.ppermute(out_y, "fsdp", other_chip(parts))
    right_x = lax.ppermute(out_x, "dp", across)
    calls.append(list(attend_back(1, (0,), *pair_args, doc_rows)))
    left_y, right_x, calls[1][0] = lax.optimization_barrier((left_y, right_x, calls[1][0]))
    grads_own = jnp.concatenate(
        [add(pick(sum_left, y, 1), left_y), add(pick(sum_right, x, 1), right_x)], axis=-1
    )
    bits = n_z.bit_length() - 1
    for bit in range(bits):
        grads_own = grads_own.reshape(-1, 2, split, grads_own.shape[-1])
        mine_bit = z // 2**bit % 2
        out_z = pick(grads_own, 1 - mine_bit, 1).astype(BF)
        if bit == 0:
            out_z, calls[1][0], *pair_args = lax.optimization_barrier(
                (out_z, calls[1][0], *pair_args)
            )
        along = [(d, d ^ (2 << bit)) for d in range(n_dp)]
        from_z = lax.ppermute(out_z, "dp", along)
        if bit == 0:
            calls.append(list(attend_back(1, (1,), *pair_args, doc_rows)))
            from_z, calls[2][0] = lax.optimization_barrier((from_z, calls[2][0]))
        grads_own = add(pick(grads_own, mine_bit, 1), from_z)
    grads_own = grads_own.reshape(split, -1)

    place = jnp.arange(parts, dtype=jnp.int32)[None, :, None] == mine
    db = jnp.stack(
        [jnp.concatenate([calls[0][3][i], calls[1][3][i] + calls[2][3][i]]) for i in range(3)]
    )
    db_all = jnp.where(place, db[:, None, :], 0.0).reshape(3, D)
    vector_grads = jnp.concatenate([db_all, dvec[:6]]).reshape(9, -1, split).transpose(1, 0, 2)
    vector_grads = jnp.concatenate(
        [vector_grads.reshape(-1, 9 * split), dbi.reshape(-1, hidden_split)], axis=1
    )
    used = vector_grads.shape[1]
    vector_grads = jnp.pad(vector_grads, ((0, 0), (0, -used % (8 * LANES))))
    vector_grads = vector_grads.reshape(n_dp, parts, 8, -1).transpose(1, 0, 2, 3)
    grad_low, dw, summed = heads_backward(
        x_all,
        w_heads,
        dsum,
        vector_grads,
        (0, 1, 1),
        [entry for call in calls for entry in call[:3]],
    )
    dw_own = dw.reshape(parts, split, 3, width).transpose(2, 1, 0, 3).reshape(3, split, D)
    summed = summed.reshape(-1)
    up_own = jnp.concatenate([grads_own[:, i * D : (i + 1) * D] for i in range(GROUPS)])
    hidden = GROUPS * D
    dwi_own = grads_own[:, hidden : 2 * hidden]
    dwo_own = grads_own[:, 2 * hidden : 2 * hidden + D]
    dwv_own = grads_own[:, 2 * hidden + D :]
    vec_own = [summed[index * split : (index + 1) * split] for index in range(9)]
    dbi_own = summed[9 * split : 9 * split + hidden_split]
    return (
        losses,
        enc[:doc_rows].reshape(1, doc_rows, D),
        enc[doc_rows:].reshape(1, 1, QLEN, D),
        grad_low[:doc_rows].reshape(1, doc_rows, D),
        grad_low[doc_rows:].reshape(1, 1, QLEN, D),
        dw_own[0],
        vec_own[0],
        dw_own[1],
        vec_own[1],
        dw_own[2],
        vec_own[2],
        dwo_own,
        vec_own[3],
        vec_own[4],
        vec_own[5],
        dwi_own,
        dbi_own,
        up_own,
        vec_own[6],
        vec_own[7],
        vec_own[8],
        dwv_own,
    )


def solution(mesh):
    rows = P(AXES, None)
    line = P(AXES)
    doc = P("dp", "fsdp", None)
    query = P("dp", "fsdp", None, None)
    weights = (rows, line) * 4 + (line, line, rows, line, rows, line, line, line, rows)
    return jax.shard_map(
        shards,
        mesh=mesh,
        in_specs=(doc, query, P("dp"), P()) + weights,
        out_specs=(P(), doc, query, doc, query) + weights,
        check_vma=False,
    )
```

```python
import functools
import math

import jax
import jax.numpy as jnp
import numpy as np
from jax import lax
from jax.experimental import pallas as pl
from jax.experimental.pallas import tpu as pltpu
from jax.sharding import PartitionSpec as P

D = 1024
HEAD_DIM = 64
PROJ = 128
QLEN = 32
LANES = 128
GROUPS = 4
CHUNK = 512
OWN_ROWS = 32

norm_eps = 1e-05
vector_eps = 1e-06
rope_base = 10000.0
smooth_temp = 0.05
loss_temp = 0.02
masked_score = -1e30
log2e = math.log2(math.e)
AXES = ("dp", "fsdp")
BF = jnp.bfloat16
F32 = jnp.float32
VMEM_MOST = 60 << 20


def dot_nn(left, right):
    return lax.dot_general(left, right, (((1,), (0,)), ((), ())), preferred_element_type=F32)


def dot_nt(left, right):
    return lax.dot_general(left, right, (((1,), (1,)), ((), ())), preferred_element_type=F32)


def dot_tn(left, right):
    return lax.dot_general(left, right, (((0,), (0,)), ((), ())), preferred_element_type=F32)


def lanes_of(shape):
    return lax.broadcasted_iota(jnp.int32, shape, len(shape) - 1)


def split_three(value):
    high = value.astype(BF)
    rest = value - high.astype(F32)
    middle = rest.astype(BF)
    return high, middle, (rest - middle.astype(F32)).astype(BF)


def params(**more):
    return pltpu.CompilerParams(vmem_limit_bytes=VMEM_MOST, **more)


def rope_tables(parts, doc_rows):
    half_dim = HEAD_DIM // 2
    frequency = rope_base ** (-np.arange(half_dim, dtype=np.float64) / half_dim)
    own = [
        np.concatenate([part * doc_rows + np.arange(doc_rows), np.arange(QLEN)])
        for part in range(parts)
    ]
    angles = np.concatenate(own)[:, None] * frequency[None, :]
    cosine, sine = np.cos(angles), np.sin(angles)
    shape = (parts, doc_rows + QLEN, LANES)
    return (
        np.concatenate([cosine] * 4, axis=1).astype(np.float32).reshape(shape),
        np.concatenate([-sine, sine, -sine, sine], axis=1).astype(np.float32).reshape(shape),
    )


def turn(tile, cosine, sine):
    first = lanes_of(tile.shape) % HEAD_DIM < HEAD_DIM // 2
    partner = jnp.where(first, pltpu.roll(tile, LANES - 32, 1), pltpu.roll(tile, 32, 1))
    return tile * cosine + partner * sine


class Exchange:
    def __init__(self, axis, size, send, recv):
        self.axis, self.size, self.send, self.recv = axis, size, send, recv
        self.me = lax.axis_index(axis)
        self.going = []

    def to(self, offset):
        return lax.rem(self.me + offset, self.size)

    def source(self, offset):
        return lax.rem(self.me - offset + self.size, self.size)

    def start(self, source_of, target_of):
        for offset in range(1, self.size):
            partner = self.to(offset)
            copy = pltpu.make_async_remote_copy(
                src_ref=source_of(partner),
                dst_ref=target_of(offset),
                send_sem=self.send.at[offset - 1],
                recv_sem=self.recv.at[offset - 1],
                device_id={self.axis: partner},
                device_id_type=pl.DeviceIdType.MESH,
            )
            copy.start()
            self.going.append(copy)

    def arrived(self):
        for copy in self.going:
            copy.wait_recv()

    def sent(self):
        for copy in self.going:
            copy.wait_send()


def greet(sizes):
    barrier = pltpu.get_barrier_semaphore()
    for axis, size in sizes.items():
        for offset in range(1, size):
            partner = lax.rem(lax.axis_index(axis) + offset, size)
            pl.semaphore_signal(
                barrier,
                inc=1,
                device_id={axis: partner},
                device_id_type=pl.DeviceIdType.MESH,
            )
    pl.semaphore_wait(barrier, sum(size - 1 for size in sizes.values()))


class Sent:
    def __init__(self, source, target, axis, index, send, recv):
        self.copy = pltpu.make_async_remote_copy(
            src_ref=source,
            dst_ref=target,
            send_sem=send,
            recv_sem=recv,
            device_id={axis: index},
            device_id_type=pl.DeviceIdType.MESH,
        )

    def start(self):
        self.copy.start()
        return self


pieces_along_y = 5
doc_pieces = 4


class Rows:
    def __init__(self, doc_ref, query_ref, x_all, chosen, sems):
        me = lax.axis_index("fsdp")
        core, chip = lax.rem(me, 2), me // 2
        self.other_core = chip * 2 + 1 - core
        self.other_chip = (1 - chip) * 2 + core
        self.sems, self.x_all, self.going = sems, x_all, []
        piece = doc_ref.shape[0] // doc_pieces
        self.moved = []
        for slot, at in enumerate(chosen):
            if at < doc_pieces:
                span = pl.ds(at * piece, piece)
                source = doc_ref.at[span]
            else:
                span = pl.ds(doc_ref.shape[0], QLEN)
                source = query_ref
            self.moved.append((slot, span, source, x_all.at[me, span]))

    def send(self, source, target, partner, kind, slot):
        one = Sent(
            source,
            target,
            "fsdp",
            partner,
            self.sems[2 * kind].at[slot],
            self.sems[2 * kind + 1].at[slot],
        ).start()
        self.going.append(one)
        return one

    def start(self):
        self.along_y = [
            self.send(source, target, self.other_chip, 0, slot)
            for slot, span, source, target in self.moved
        ]
        self.own = [
            self.send(source, target, self.other_core, 1, slot)
            for slot, span, source, target in self.moved
        ]
        self.local = []
        for slot, span, source, target in self.moved:
            copy = pltpu.make_async_copy(source, target, self.sems[6].at[slot])
            copy.start()
            self.local.append(copy)

    def finish(self):
        passed = []
        for slot, span, source, target in self.moved:
            self.along_y[slot].copy.wait_recv()
            block = self.x_all.at[self.other_chip, span]
            passed.append(self.send(block, block, self.other_core, 2, slot))
        for one in self.own + passed:
            one.copy.wait_recv()
        for copy in self.local:
            copy.wait()
        for one in self.going:
            one.copy.wait_send()


def rows_sems(chosen):
    return [pltpu.SemaphoreType.DMA((len(chosen),))] * 7


def start_kernel(n_dp, n_fs, chosen, *refs):
    (
        doc_ref,
        query_ref,
        w_ref,
        v_ref,
        x_all,
        w_all,
        v_all,
        *sems,
    ) = refs
    moving, (own_sem, line_send, line_recv, cross_send, cross_recv, *sems) = sems[:7], sems[7:]
    me, my_dp = lax.axis_index("fsdp"), lax.axis_index("dp")
    n_z, z, x = n_dp // 2, my_dp // 2, lax.rem(my_dp, 2)
    over = [
        Exchange(axis, n_dp if axis == "dp" else n_fs, sems[2 * i], sems[2 * i + 1])
        for i, axis in enumerate(("fsdp", "fsdp", "dp"))
    ]
    rows = Rows(doc_ref, query_ref, x_all, chosen, moving)
    greet({"dp": n_dp, "fsdp": n_fs})
    over[0].start(lambda partner: w_ref.at[partner], lambda offset: w_all.at[my_dp, me])
    over[1].start(lambda partner: v_ref, lambda offset: v_all.at[my_dp, me])
    rows.start()

    moves = [(w_ref.at[me], w_all.at[my_dp, me]), (v_ref, v_all.at[my_dp, me])]
    local = [
        pltpu.make_async_copy(source, target, own_sem.at[at])
        for at, (source, target) in enumerate(moves)
    ]
    for copy in local:
        copy.start()
    local[0].wait()
    local[1].wait()
    over[0].arrived()
    over[1].arrived()

    block = w_all.at[my_dp]
    along = []
    for offset in range(1, n_z):
        partner = lax.rem(z + offset, n_z) * 2 + x
        along.append(
            Sent(
                block, block, "dp", partner, line_send.at[offset - 1], line_recv.at[offset - 1]
            ).start()
        )
    other = z * 2 + 1 - x
    cross = [Sent(block, block, "dp", other, cross_send.at[0], cross_recv.at[0]).start()]
    over[2].start(lambda partner: v_all.at[my_dp], lambda offset: v_all.at[my_dp])
    for offset in range(1, n_z):
        along[offset - 1].copy.wait_recv()
        block = w_all.at[lax.rem(z - offset + n_z, n_z) * 2 + x]
        cross.append(
            Sent(block, block, "dp", other, cross_send.at[offset], cross_recv.at[offset]).start()
        )
    rows.finish()
    for one in cross:
        one.copy.wait_recv()
    over[2].arrived()
    for exchange in over:
        exchange.sent()
    for one in along + cross:
        one.copy.wait_send()


def gather_start(doc, query, w_split, vector_tile):
    n_dp, n_fs = lax.axis_size("dp"), lax.axis_size("fsdp")
    chosen = tuple(range(doc_pieces - 1))
    rows = doc.shape[0] + query.shape[0]
    anywhere = pl.BlockSpec(memory_space=pl.ANY)
    many = lambda count: [pltpu.SemaphoreType.DMA((count,))] * 2
    dma = lambda axis: many((n_dp if axis == "dp" else n_fs) - 1)
    return pl.pallas_call(
        functools.partial(start_kernel, n_dp, n_fs, chosen),
        in_specs=[pl.BlockSpec(memory_space=pltpu.VMEM)] * 4,
        out_specs=[anywhere] * 3,
        out_shape=[
            jax.ShapeDtypeStruct((n_fs, rows, D), BF),
            jax.ShapeDtypeStruct((n_dp,) + w_split.shape, BF),
            jax.ShapeDtypeStruct((n_dp, n_fs) + vector_tile.shape, F32),
        ],
        scratch_shapes=rows_sems(chosen)
        + [pltpu.SemaphoreType.DMA((2,))]
        + many(n_dp // 2 - 1)
        + many(n_dp // 2)
        + [sem for axis in ("fsdp", "fsdp", "dp") for sem in dma(axis)],
        compiler_params=params(collective_id=3, has_side_effects=True),
        name="gather_start",
    )(doc, query, w_split, vector_tile)


def rest_kernel(n_fs, chosen, doc_ref, query_ref, given_ref, x_all, *sems):
    rows = Rows(doc_ref, query_ref, x_all, chosen, sems)
    greet({"fsdp": n_fs})
    rows.start()
    rows.finish()


def gather_rest(doc, query, x_all):
    chosen = tuple(range(doc_pieces - 1, pieces_along_y))
    anywhere = pl.BlockSpec(memory_space=pl.ANY)
    return pl.pallas_call(
        functools.partial(rest_kernel, lax.axis_size("fsdp"), chosen),
        in_specs=[pl.BlockSpec(memory_space=pltpu.VMEM)] * 2 + [anywhere],
        out_specs=anywhere,
        out_shape=jax.ShapeDtypeStruct(x_all.shape, BF),
        scratch_shapes=rows_sems(chosen),
        input_output_aliases={2: 0},
        compiler_params=params(collective_id=4, has_side_effects=True),
        name="gather_rest",
    )(doc, query, x_all)


def heads_kernel(doc_rows, len_ref, x_ref, w_ref, b_ref, cos_ref, sin_ref, q_ref, k_ref, v_ref):
    part = pl.program_id(0)
    rows = x_ref.shape[1]
    cosine, sine = cos_ref[0], sin_ref[0]
    lane = lanes_of((rows, LANES))
    row = lax.broadcasted_iota(jnp.int32, (rows, LANES), 0)
    allowed = (row >= doc_rows) | (part * doc_rows + row < len_ref[0])
    mask = jnp.where(allowed, 0.0, masked_score)
    width = w_ref.shape[1] // 3
    line = dot_nn(x_ref[0], w_ref[...]) + b_ref[...]
    for pair in range(width // LANES):
        here = pair * LANES
        query = turn(line[:, here : here + LANES], cosine, sine) * (log2e * HEAD_DIM**-0.5)
        key = turn(line[:, width + here : width + here + LANES], cosine, sine)
        value = line[:, 2 * width + here : 2 * width + here + LANES]
        for half in range(2):
            if half:
                query, key, value = (pltpu.roll(entry, 64, 1) for entry in (query, key, value))
            q_ref[2 * pair + half] = jnp.where(
                lane < 64, query, jnp.where(lane == 64, 1.0, 0.0)
            ).astype(BF)
            k_ref[2 * pair + half] = jnp.where(
                lane < 64, key, jnp.where(lane == 64, mask, jnp.where(lane < 68, 1.0, 0.0))
            ).astype(BF)
            v_ref[2 * pair + half] = jnp.where(
                lane < 64, value, jnp.where(lane < 67, 1.0, 0.0)
            ).astype(BF)


def project_heads(length, x_all, w_heads, b_heads, cosine, sine, doc_rows):
    parts, rows, _ = x_all.shape
    heads = w_heads.shape[1] // 3 // HEAD_DIM
    block = pl.BlockSpec((heads, rows, LANES), lambda part: (0, part, 0))
    shape = jax.ShapeDtypeStruct((heads, parts * rows, LANES), BF)
    table = pl.BlockSpec((1, rows, LANES), lambda part: (part, 0, 0))
    return pl.pallas_call(
        functools.partial(heads_kernel, doc_rows),
        grid=(parts,),
        in_specs=[
            pl.BlockSpec(memory_space=pltpu.SMEM),
            pl.BlockSpec((1, rows, D), lambda part: (part, 0, 0)),
            pl.BlockSpec(w_heads.shape, lambda part: (0, 0)),
            pl.BlockSpec(b_heads.shape, lambda part: (0, 0)),
            table,
            table,
        ],
        out_specs=[block] * 3,
        out_shape=[shape] * 3,
        compiler_params=params(),
        name="project_heads",
    )(length, x_all, w_heads, b_heads, cosine, sine)


def attend_rows(query, chunks):
    largest = jnp.full((query.shape[0], 1), -1e38, F32)
    total = jnp.zeros((query.shape[0], LANES), F32)
    for key, value in chunks:
        scores = dot_nt(query, key())
        newest = jnp.maximum(largest, jnp.max(scores, axis=1, keepdims=True))
        powers = jnp.exp2(scores - newest).astype(BF)
        total = total * jnp.exp2(largest - newest) + dot_nn(powers, value())
        largest = newest
    row_sum = total[:, 64:65]
    return total / row_sum, largest + jnp.log2(row_sum)


def attend_kernel(
    doc_rows, parts, q_ref, k_ref, v_ref, ko_ref, vo_ref, o_ref, full_ref, qa_ref
):
    rows = doc_rows + QLEN
    for span, own in ((slice(0, doc_rows), False), (slice(doc_rows, rows), True)):
        mixed = []
        for head in range(2):
            query = q_ref[head, span, :]
            lane = lanes_of(query.shape)
            if own:
                chunks = [(lambda: ko_ref[head], lambda: vo_ref[head])]
            else:
                chunks = [
                    (
                        lambda part=part: k_ref[head, part * rows : part * rows + doc_rows, :],
                        lambda part=part: v_ref[head, part * rows : part * rows + doc_rows, :],
                    )
                    for part in range(parts)
                ]
            out, log_sum = attend_rows(query, chunks)
            mixed.append(out)
            high, middle, low = split_three(-log_sum)
            qa_ref[head, span, :] = jnp.where(
                lane == 65,
                high,
                jnp.where(lane == 66, middle, jnp.where(lane == 67, low, query)),
            )
        joined = jnp.where(lanes_of(mixed[0].shape) < 64, mixed[0], pltpu.roll(mixed[1], 64, 1))
        full_ref[0, span, :] = joined
        o_ref[0, span, :] = joined.astype(BF)


def attend(query, key, value, parts, doc_rows):
    heads, total, _ = query.shape
    rows = total // parts
    own_at = rows // QLEN
    mine = pl.BlockSpec((2, rows, LANES), lambda pair, part: (pair, part, 0))
    whole = pl.BlockSpec((2, total, LANES), lambda pair, part: (pair, 0, 0))
    own = pl.BlockSpec((2, QLEN, LANES), lambda pair, part: (pair, part * own_at + own_at - 1, 0))
    flat = pl.BlockSpec((1, rows, LANES), lambda pair, part: (part, 0, pair))
    flops = 4 * heads * total * total * 256
    return pl.pallas_call(
        functools.partial(attend_kernel, doc_rows, parts),
        grid=(heads // 2, parts),
        in_specs=[mine, whole, whole, own, own],
        out_specs=[flat, flat, mine],
        out_shape=[
            jax.ShapeDtypeStruct((parts, rows, heads * HEAD_DIM), BF),
            jax.ShapeDtypeStruct((parts, rows, heads * HEAD_DIM), F32),
            jax.ShapeDtypeStruct(query.shape, BF),
        ],
        compiler_params=params(),
        cost_estimate=pl.CostEstimate(flops=flops, bytes_accessed=1 << 24, transcendentals=0),
        name="attend",
    )(query, key, value, key, value)


def attend_back_kernel(
    halves,
    doc_rows,
    parts,
    q_ref,
    k_ref,
    v_ref,
    ko_ref,
    vo_ref,
    do_ref,
    o_ref,
    cos_ref,
    sin_ref,
    dq_ref,
    dk_ref,
    dv_ref,
    sums_ref,
    dk_doc,
    dv_doc,
    dk_own,
    dv_own,
):
    rows = doc_rows + QLEN
    at = pl.program_id(0)

    @pl.when(at == 0)
    def _():
        dk_doc[...] = jnp.zeros_like(dk_doc)
        dv_doc[...] = jnp.zeros_like(dv_doc)
        sums_ref[...] = jnp.zeros_like(sums_ref)

    for span, own in ((slice(0, doc_rows), False), (slice(doc_rows, rows), True)):
        grad_pair = do_ref[0, span, :]
        lane = lanes_of(grad_pair.shape)
        product = grad_pair.astype(F32) * o_ref[0, span, :]
        turned = pltpu.roll(grad_pair.astype(F32), 64, 1).astype(BF)
        joined = jnp.zeros(grad_pair.shape, F32)
        for head in halves:
            query = q_ref[head, span, :]
            inside = lane < 64 if head == 0 else lane >= 64
            row_dot = jnp.sum(jnp.where(inside, product, 0.0), axis=1, keepdims=True)
            high, middle, low = split_three(-row_dot)
            grad = jnp.where(
                lane < 64,
                turned if head else grad_pair,
                jnp.where(
                    lane == 64,
                    high,
                    jnp.where(
                        lane == 65, middle, jnp.where(lane == 66, low, jnp.zeros_like(grad_pair))
                    ),
                ),
            )
            query_t, grad_t = query.T, grad.T
            grad_query = jnp.zeros(query.shape, F32)
            for part in range(1 if own else parts):
                if own:
                    key, value = ko_ref[head], vo_ref[head]
                else:
                    key = k_ref[head, part * rows : part * rows + doc_rows, :]
                    value = v_ref[head, part * rows : part * rows + doc_rows, :]
                powers = jnp.exp2(dot_nt(query, key))
                grad_scores = (powers * dot_nt(grad, value)).astype(BF)
                if own:
                    dv_own[head, at] = dot_nn(grad_t, powers.astype(BF))
                    dk_own[head, at] = dot_nn(query_t, grad_scores)
                else:
                    dv_doc[head, part] += dot_nn(grad_t, powers.astype(BF))
                    dk_doc[head, part] += dot_nn(query_t, grad_scores)
                grad_query += dot_nn(grad_scores, key)
            joined = jnp.where(inside, pltpu.roll(grad_query, 64, 1) if head else grad_query, joined)
        joined = joined * HEAD_DIM**-0.5
        low = turn(joined, cos_ref[at, span, :], -sin_ref[at, span, :]).astype(BF)
        dq_ref[0, span, :] = low
        sums_ref[0:1, :] += column_sum(low.astype(F32))

    @pl.when(at == parts - 1)
    def _():
        def both(kept, part):
            sides = [kept[head, part].T for head in halves]
            lane = lanes_of(sides[0].shape)
            if len(halves) == 2:
                return jnp.where(lane < 64, sides[0], pltpu.roll(sides[1], 64, 1))
            if halves[0]:
                return jnp.where(lane < 64, 0.0, pltpu.roll(sides[0], 64, 1))
            return jnp.where(lane < 64, sides[0], 0.0)

        for part in range(parts):
            for span, keys, values in (
                (slice(0, doc_rows), dk_doc, dv_doc),
                (slice(doc_rows, rows), dk_own, dv_own),
            ):
                grad_key = both(keys, part) * (1.0 / log2e)
                low = turn(grad_key, cos_ref[part, span, :], -sin_ref[part, span, :]).astype(BF)
                dk_ref[part, span, :] = low
                sums_ref[1:2, :] += column_sum(low.astype(F32))
                low = both(values, part).astype(BF)
                dv_ref[part, span, :] = low
                sums_ref[2:3, :] += column_sum(low.astype(F32))


def attend_back(pair, halves, query, key, value, grad, mixed, cosine, sine, doc_rows):
    heads, total, _ = query.shape
    parts, rows, width = grad.shape
    own_at = rows // QLEN
    mine = pl.BlockSpec((2, rows, LANES), lambda part: (pair, part, 0))
    whole = pl.BlockSpec((2, total, LANES), lambda part: (pair, 0, 0))
    own = pl.BlockSpec((2, QLEN, LANES), lambda part: (pair, part * own_at + own_at - 1, 0))
    flat = pl.BlockSpec((1, rows, LANES), lambda part: (part, 0, pair))
    table = pl.BlockSpec((parts, rows, LANES), lambda part: (0, 0, 0))
    full = pl.BlockSpec((parts, rows, LANES), lambda part: (0, 0, 0))
    shape = jax.ShapeDtypeStruct((parts, rows, LANES), BF)
    return pl.pallas_call(
        functools.partial(attend_back_kernel, halves, doc_rows, parts),
        grid=(parts,),
        in_specs=[mine, whole, whole, own, own, flat, flat, table, table],
        out_specs=[
            pl.BlockSpec((1, rows, LANES), lambda part: (part, 0, 0)),
            full,
            full,
            pl.BlockSpec((8, LANES), lambda part: (0, 0)),
        ],
        out_shape=[shape] * 3 + [jax.ShapeDtypeStruct((8, LANES), F32)],
        scratch_shapes=[
            pltpu.VMEM((2, parts, LANES, doc_rows), F32),
            pltpu.VMEM((2, parts, LANES, doc_rows), F32),
            pltpu.VMEM((2, parts, LANES, QLEN), F32),
            pltpu.VMEM((2, parts, LANES, QLEN), F32),
        ],
        compiler_params=params(),
        cost_estimate=pl.CostEstimate(
            flops=10 * len(halves) * total * total * 256, bytes_accessed=1 << 24, transcendentals=0
        ),
        name="attend_back",
    )(query, key, value, key, value, grad, mixed, cosine, sine)


def normed(summed):
    centered = summed - jnp.mean(summed, axis=-1, keepdims=True)
    variance = jnp.mean(centered * centered, axis=-1, keepdims=True)
    inverse = lax.rsqrt(variance + norm_eps)
    return centered * inverse, inverse


def joined_up(up_ref):
    size = OWN_ROWS
    pieces = [
        up_ref[at : at + size, group * D : (group + 1) * D]
        for at in range(0, up_ref.shape[0], size)
        for group in range(GROUPS)
    ]
    return jnp.concatenate(pieces, axis=0)


def regrouped(packed, old, new):
    if old == new:
        return packed
    hidden = GROUPS * D
    rows = packed[:, :hidden].reshape(-1, old, GROUPS, D).transpose(0, 2, 1, 3)
    rows = rows.reshape(-1, GROUPS, new, D).transpose(0, 2, 1, 3).reshape(-1, hidden)
    return jnp.concatenate([rows, packed[:, hidden:]], axis=1)


def packed_specs():
    hidden = GROUPS * D
    return {
        "up": pl.BlockSpec((CHUNK // GROUPS, hidden), lambda step: (step, 0)),
        "down": pl.BlockSpec((D, CHUNK), lambda step: (0, hidden // CHUNK + step)),
        "out": pl.BlockSpec((D, D), lambda step: (0, 2 * hidden // D)),
        "vector": pl.BlockSpec((D, LANES), lambda step: (0, (2 * hidden + D) // LANES)),
    }


def rows_kernel(
    att_ref,
    x_ref,
    wo_ref,
    wi_ref,
    wu_ref,
    wv_ref,
    bi_ref,
    vec_ref,
    hat1_ref,
    inv1_ref,
    low1_ref,
    act_ref,
    slope_ref,
    hat2_ref,
    inv2_ref,
    enc_ref,
    proj_ref,
    sum_ref,
):
    step = pl.program_id(0)
    parts, _, width = att_ref.shape

    @pl.when(step == 0)
    def _():
        summed = x_ref[...].astype(F32) + vec_ref[0:1, :]
        for part in range(parts):
            summed += dot_nn(att_ref[part], wo_ref[part * width : (part + 1) * width, :])
        hat, inverse = normed(summed)
        hat1_ref[...] = hat.astype(BF)
        inv1_ref[...] = jnp.broadcast_to(inverse, inv1_ref.shape)
        out = hat * vec_ref[1:2, :] + vec_ref[2:3, :]
        low1_ref[...] = out.astype(BF)
        sum_ref[...] = out + vec_ref[3:4, :]

    up = joined_up(wu_ref)
    inner = dot_nn(low1_ref[...], wi_ref[...]) + bi_ref[...]
    share = 0.5 * lax.erf(inner * math.sqrt(0.5)) + 0.5
    act = (inner * share).astype(BF)
    act_ref[...] = act
    density = jnp.exp(inner * inner * -0.5) * (1.0 / math.sqrt(2.0 * math.pi))
    slope_ref[...] = (share + inner * density).astype(BF)
    sum_ref[...] += dot_nn(act, up)

    @pl.when(step == pl.num_programs(0) - 1)
    def _():
        hat, inverse = normed(sum_ref[...])
        hat2_ref[...] = hat.astype(BF)
        inv2_ref[...] = jnp.broadcast_to(inverse, inv2_ref.shape)
        low = (hat * vec_ref[4:5, :] + vec_ref[5:6, :]).astype(BF)
        enc_ref[...] = low
        proj_ref[...] = dot_nn(low, wv_ref[...])


def rows_forward(att, rows_in, packed, inner_bias, vectors):
    rows = rows_in.shape[0]
    hidden = inner_bias.shape[1]
    chunk = CHUNK
    weights = packed_specs()
    keep = lambda shape: pl.BlockSpec(shape, lambda step: (0,) * len(shape))
    columns = pl.BlockSpec((rows, chunk), lambda step: (0, step))
    wide = jax.ShapeDtypeStruct((rows, D), BF)
    thin = jax.ShapeDtypeStruct((rows, LANES), F32)
    big = jax.ShapeDtypeStruct((rows, hidden), BF)
    return pl.pallas_call(
        rows_kernel,
        grid=(hidden // chunk,),
        in_specs=[
            keep(att.shape),
            keep(rows_in.shape),
            weights["out"],
            weights["down"],
            weights["up"],
            weights["vector"],
            pl.BlockSpec((1, chunk), lambda step: (0, step)),
            keep(vectors.shape),
        ],
        out_specs=[
            keep((rows, D)),
            keep((rows, LANES)),
            keep((rows, D)),
            columns,
            columns,
            keep((rows, D)),
            keep((rows, LANES)),
            keep((rows, D)),
            keep((rows, LANES)),
        ],
        out_shape=[wide, thin, wide, big, big, wide, thin, wide, thin],
        scratch_shapes=[pltpu.VMEM((rows, D), F32)],
        compiler_params=params(),
        cost_estimate=pl.CostEstimate(
            flops=2 * rows * D * (D + 2 * hidden), bytes_accessed=1 << 25, transcendentals=0
        ),
        name="rows_forward",
    )(att, rows_in, packed, packed, packed, packed, inner_bias, vectors)


def norm_back(grad, hat, inverse, gain):
    scaled = grad * gain
    first = jnp.mean(scaled, axis=-1, keepdims=True)
    second = jnp.mean(scaled * hat, axis=-1, keepdims=True)
    return (scaled - first - hat * second) * inverse


def column_sum(value):
    return jnp.sum(value, axis=0, keepdims=True)


def rows_back_kernel(
    by_core,
    dproj_ref,
    enc_ref,
    hat2_ref,
    inv2_ref,
    wv_ref,
    act_ref,
    slope_ref,
    wu_ref,
    wi_ref,
    low1_ref,
    hat1_ref,
    inv1_ref,
    att_ref,
    wo_ref,
    vec_ref,
    keep_ref,
    send_ref,
    dbi_ref,
    datt_ref,
    dsum_ref,
    dvec_ref,
    low_ref,
    total_ref,
    dwv_ref,
    dwo_ref,
    dwu_ref,
    dwi_ref,
    once_sem,
    up_sem,
    down_sem,
):
    step = pl.program_id(0)
    steps = pl.num_programs(0)
    parts, _, width = att_ref.shape
    hidden = GROUPS * D
    slot = lax.rem(step, 2)

    core = lax.rem(lax.axis_index("fsdp"), 2) if by_core else 0

    def both(source, rows_at, columns, sem):
        return [
            pltpu.make_async_copy(
                source.at[:, which], target.at[rows_at, :, columns], sem.at[index]
            )
            for index, (which, target) in enumerate(((1 - core, send_ref), (core, keep_ref)))
        ]

    count = dwu_ref.shape[1]
    every = pl.ds(0, keep_ref.shape[0])

    def up_copy(at, place):
        return both(
            dwu_ref.at[place], pl.ds(at * count, count), pl.ds(0, hidden), up_sem.at[place]
        )

    def down_copy(at, place):
        here = pl.ds(pl.multiple_of(hidden + at * CHUNK, CHUNK), CHUNK)
        return both(dwi_ref.at[place], every, here, down_sem.at[place])

    def vector_copy():
        return both(dwv_ref, every, pl.ds(2 * hidden + D, LANES), once_sem.at[0])

    def out_copy():
        return both(dwo_ref, every, pl.ds(2 * hidden, D), once_sem.at[1])

    def start(copies):
        for copy in copies:
            copy.start()

    def wait(copies):
        for copy in copies:
            copy.wait()

    def by_device(value):
        return value.astype(BF).reshape(-1, 2, OWN_ROWS, value.shape[1])

    @pl.when(step == 0)
    def _():
        dproj = dproj_ref[...]
        dwv_ref[...] = by_device(dot_tn(enc_ref[...], dproj))
        start(vector_copy())
        grad = dot_nt(dproj, wv_ref[...])
        hat = hat2_ref[...].astype(F32)
        dvec_ref[4:5, :] = column_sum(grad * hat)
        dvec_ref[5:6, :] = column_sum(grad)
        back = norm_back(grad, hat, inv2_ref[:, :1], vec_ref[4:5, :])
        low = back.astype(BF)
        low_ref[...] = low
        total_ref[...] = back
        dvec_ref[3:4, :] = column_sum(low.astype(F32))

    @pl.when(step >= 2)
    def _():
        wait(up_copy(step - 2, slot))
        wait(down_copy(step - 2, slot))

    low = low_ref[...]
    dinner = (dot_nt(low, joined_up(wu_ref)) * slope_ref[...].astype(F32)).astype(BF)
    dbi_ref[...] = column_sum(dinner.astype(F32))
    up_grad = dot_tn(act_ref[...], low).astype(BF)
    for at in range(0, CHUNK, OWN_ROWS):
        own, group = at // (OWN_ROWS * GROUPS), at // OWN_ROWS % GROUPS
        dwu_ref[slot, own // 2, own % 2, :, group * D : (group + 1) * D] = up_grad[at : at + OWN_ROWS]
    start(up_copy(step, slot))
    dwi_ref[slot] = by_device(dot_tn(low1_ref[...], dinner))
    start(down_copy(step, slot))
    total_ref[...] += dot_nt(dinner, wi_ref[...])

    @pl.when(step == pl.num_programs(0) - 1)
    def _():
        grad = total_ref[...]
        hat = hat1_ref[...].astype(F32)
        dvec_ref[1:2, :] = column_sum(grad * hat)
        dvec_ref[2:3, :] = column_sum(grad)
        back = norm_back(grad, hat, inv1_ref[:, :1], vec_ref[1:2, :])
        dsum_ref[...] = back
        attn_low = back.astype(BF)
        dvec_ref[0:1, :] = column_sum(attn_low.astype(F32))
        for part in range(parts):
            here = slice(part * width, (part + 1) * width)
            size = width // (2 * OWN_ROWS)
            dwo_ref[part * size : (part + 1) * size] = by_device(dot_tn(att_ref[part], attn_low))
            datt_ref[part] = dot_nt(attn_low, wo_ref[here, :]).astype(BF)
        start(out_copy())
        wait(vector_copy())
        for place in range(2):
            wait(up_copy(steps - 2 + place, place))
            wait(down_copy(steps - 2 + place, place))
        wait(out_copy())


def rows_backward(by_core, dproj, enc, hat2, inv2, packed, act, slope, low1, hat1, inv1, att, vectors):
    rows, hidden = act.shape
    keep = lambda shape: pl.BlockSpec(shape, lambda step: (0,) * len(shape))
    columns = pl.BlockSpec((rows, CHUNK), lambda step: (0, step))
    bias = pl.BlockSpec((1, CHUNK), lambda step: (0, step))
    weights = packed_specs()
    pairs = packed.shape[0] // (2 * OWN_ROWS)
    half = jax.ShapeDtypeStruct((pairs, OWN_ROWS, packed.shape[1]), BF)
    operands = (
        (dproj, None),
        (enc, None),
        (hat2, None),
        (inv2, None),
        (packed, weights["vector"]),
        (act, columns),
        (slope, columns),
        (packed, weights["up"]),
        (packed, weights["down"]),
        (low1, None),
        (hat1, None),
        (inv1, None),
        (att, None),
        (packed, weights["out"]),
        (vectors, None),
    )
    return pl.pallas_call(
        functools.partial(rows_back_kernel, by_core),
        grid=(hidden // CHUNK,),
        in_specs=[keep(entry.shape) if spec is None else spec for entry, spec in operands],
        out_specs=[
            pl.BlockSpec(memory_space=pl.ANY),
            pl.BlockSpec(memory_space=pl.ANY),
            bias,
            keep(att.shape),
            keep((rows, D)),
            keep((8, D)),
        ],
        out_shape=[
            half,
            half,
            jax.ShapeDtypeStruct((1, hidden), F32),
            jax.ShapeDtypeStruct(att.shape, BF),
            jax.ShapeDtypeStruct((rows, D), F32),
            jax.ShapeDtypeStruct((8, D), F32),
        ],
        scratch_shapes=[
            pltpu.VMEM((rows, D), BF),
            pltpu.VMEM((rows, D), F32),
            pltpu.VMEM((pairs, 2, OWN_ROWS, LANES), BF),
            pltpu.VMEM((pairs, 2, OWN_ROWS, D), BF),
            pltpu.VMEM((2, CHUNK // (2 * GROUPS * OWN_ROWS), 2, OWN_ROWS, hidden), BF),
            pltpu.VMEM((2, pairs, 2, OWN_ROWS, CHUNK), BF),
            pltpu.SemaphoreType.DMA((2, 2)),
            pltpu.SemaphoreType.DMA((2, 2)),
            pltpu.SemaphoreType.DMA((2, 2)),
        ],
        compiler_params=params(),
        cost_estimate=pl.CostEstimate(
            flops=4 * rows * D * (D + 2 * hidden), bytes_accessed=1 << 26, transcendentals=0
        ),
        name="rows_backward",
    )(*(entry for entry, _ in operands))


def heads_back_kernel(n_dp, n_fs, pair_of, *refs):
    calls, pairs = len(pair_of), max(pair_of) + 1
    x_ref, w_ref, dsum_ref, vec_ref = refs[:4]
    call_refs = refs[4 : 4 + 3 * calls]
    dx_ref, dw_ref, dvec_ref = refs[4 + 3 * calls : 7 + 3 * calls]
    (
        first_out,
        second_out,
        first_in,
        second_in,
        chip_out,
        chip_in,
        kept_ref,
        dw_out,
        dw_across,
        dw_line,
        dw_in,
        dw_sum,
        vec_in,
        vec_sum,
        vec_last,
        core_send,
        core_recv,
        chip_send,
        chip_recv,
        across_send,
        across_recv,
        along_send,
        along_recv,
        *sems,
    ) = refs[7 + 3 * calls :]
    me, my_dp = lax.axis_index("fsdp"), lax.axis_index("dp")
    core, chip = lax.rem(me, 2), me // 2
    other_core = chip * 2 + 1 - core
    other_chip = (1 - chip) * 2 + core
    over = [
        Exchange(axis, n_dp if axis == "dp" else n_fs, sems[2 * i], sems[2 * i + 1])
        for i, axis in enumerate(("fsdp", "dp", "fsdp"))
    ]
    greet({"dp": n_dp, "fsdp": n_fs})
    width = w_ref.shape[1] // 3
    rows = x_ref.shape[1]
    piece = rows // pieces_along_y

    over[0].start(lambda partner: vec_ref.at[partner], lambda offset: vec_in.at[offset - 1])

    def gradient(index, pair, part):
        found = [
            call_refs[call * 3 + index][part] for call in range(calls) if pair_of[call] == pair
        ]
        return functools.reduce(lambda one, two: one + two, found)

    def back(part):
        total = jnp.zeros((rows, D), F32)
        for index in range(3):
            for pair in range(pairs):
                here = index * width + pair * LANES
                total += dot_nt(gradient(index, pair, part), w_ref[:, here : here + LANES])
        return total

    def to_core(source, target, at):
        return Sent(source, target, "fsdp", other_core, core_send.at[at], core_recv.at[at]).start()

    first_out[...] = back((1 - chip) * 2 + 1 - core).astype(BF)
    first = to_core(first_out, first_in, 0)
    away = back(other_chip)
    first.copy.wait_recv()
    chip_out[...] = (away + first_in[...].astype(F32)).astype(BF)
    along_y = []
    for at in range(pieces_along_y):
        here = pl.ds(at * piece, piece)
        along_y.append(
            Sent(
                chip_out.at[here],
                chip_in.at[here],
                "fsdp",
                other_chip,
                chip_send.at[at],
                chip_recv.at[at],
            ).start()
        )

    block = D // n_dp
    n_z, z, x = n_dp // 2, my_dp // 2, lax.rem(my_dp, 2)
    across, along_z = [], []
    for index in range(3):
        for pair in range(pairs):
            here = slice(pair * LANES, (pair + 1) * LANES)
            total = jnp.zeros((D, LANES), F32)
            for part in range(n_fs):
                total += dot_tn(x_ref[part], gradient(index, pair, part))
            dw_out[index, :, :, :, here] = total.astype(BF).reshape(n_z, 2, block, LANES)
        across.append(
            Sent(
                dw_out.at[index, :, 1 - x],
                dw_across.at[index],
                "dp",
                z * 2 + 1 - x,
                across_send.at[index],
                across_recv.at[index],
            ).start()
        )

    def send_along_z(index):
        across[index].copy.wait_recv()
        dw_line[index] = (dw_out[index, :, x].astype(F32) + dw_across[index].astype(F32)).astype(BF)
        for offset in range(1, n_z):
            partner = lax.rem(z + offset, n_z)
            along_z.append(
                Sent(
                    dw_line.at[index, partner],
                    dw_in.at[index, offset - 1],
                    "dp",
                    partner * 2 + x,
                    along_send.at[index, offset - 1],
                    along_recv.at[index, offset - 1],
                ).start()
            )

    over[0].arrived()
    vec_total = vec_ref[me]
    for offset in range(n_fs - 1):
        vec_total = vec_total + vec_in[offset]
    vec_sum[...] = vec_total
    over[1].start(lambda partner: vec_sum.at[partner], lambda offset: vec_last.at[offset - 1])

    send_along_z(0)
    second_out[...] = back(other_core).astype(BF)
    second = to_core(second_out, second_in, 1)
    send_along_z(1)
    kept_ref[...] = back(me) + dsum_ref[...]
    send_along_z(2)
    second.copy.wait_recv()
    kept_ref[...] += second_in[...].astype(F32)

    over[1].arrived()
    vec_total = vec_sum[my_dp]
    for offset in range(n_dp - 1):
        vec_total = vec_total + vec_last[offset]
    dvec_ref[...] = vec_total

    each = block // n_fs
    mine = dw_ref.at[me]
    for index in range(3):
        total = dw_out[index, z, x].astype(F32) + dw_across[index, z].astype(F32)
        for offset in range(n_z - 1):
            along_z[index * (n_z - 1) + offset].copy.wait_recv()
            total = total + dw_in[index, offset].astype(F32)
        dw_sum[:, :, index * width : (index + 1) * width] = total.reshape(n_fs, each, width)
    dw_ref[me] = dw_sum[me]
    over[2].start(lambda partner: dw_sum.at[partner], lambda offset: mine)
    for at in range(pieces_along_y):
        here = slice(at * piece, (at + 1) * piece)
        along_y[at].copy.wait_recv()
        dx_ref[here, :] = (kept_ref[here, :] + chip_in[here, :].astype(F32)).astype(BF)
    over[2].arrived()
    for exchange in over:
        exchange.sent()
    for one in [first, second] + across + along_y + along_z:
        one.copy.wait_send()


def heads_backward(x_all, w_heads, dsum, vector_grads, pair_of, grads):
    n_dp, n_fs = lax.axis_size("dp"), lax.axis_size("fsdp")
    _, rows, _ = x_all.shape
    whole = pl.BlockSpec(memory_space=pltpu.VMEM)
    block = D // n_dp
    columns = w_heads.shape[1]
    tile = vector_grads.shape[2:]
    line = pltpu.VMEM((rows, D), BF)
    dma = lambda axis: [pltpu.SemaphoreType.DMA(((n_dp if axis == "dp" else n_fs) - 1,))] * 2
    return pl.pallas_call(
        functools.partial(heads_back_kernel, n_dp, n_fs, pair_of),
        in_specs=[whole] * (4 + len(grads)),
        out_specs=[whole] * 3,
        out_shape=[
            jax.ShapeDtypeStruct((rows, D), BF),
            jax.ShapeDtypeStruct((n_fs, block // n_fs, columns), F32),
            jax.ShapeDtypeStruct(tile, F32),
        ],
        scratch_shapes=[line] * 6
        + [
            pltpu.VMEM((rows, D), F32),
            pltpu.VMEM((3, n_dp // 2, 2, block, columns // 3), BF),
            pltpu.VMEM((3, n_dp // 2, block, columns // 3), BF),
            pltpu.VMEM((3, n_dp // 2, block, columns // 3), BF),
            pltpu.VMEM((3, n_dp // 2 - 1, block, columns // 3), BF),
            pltpu.VMEM((n_fs, block // n_fs, columns), F32),
            pltpu.VMEM((n_fs - 1, n_dp) + tile, F32),
            pltpu.VMEM((n_dp,) + tile, F32),
            pltpu.VMEM((n_dp - 1,) + tile, F32),
            pltpu.SemaphoreType.DMA((2,)),
            pltpu.SemaphoreType.DMA((2,)),
            pltpu.SemaphoreType.DMA((pieces_along_y,)),
            pltpu.SemaphoreType.DMA((pieces_along_y,)),
            pltpu.SemaphoreType.DMA((3,)),
            pltpu.SemaphoreType.DMA((3,)),
            pltpu.SemaphoreType.DMA((3, n_dp // 2 - 1)),
            pltpu.SemaphoreType.DMA((3, n_dp // 2 - 1)),
        ]
        + [sem for axis in ("fsdp", "dp", "fsdp") for sem in dma(axis)],
        compiler_params=params(collective_id=2, has_side_effects=True),
        name="heads_backward",
    )(x_all, w_heads, dsum, vector_grads, *grads)


widths = (PROJ, PROJ * 3 // 4, PROJ // 2)
token_block = 1024


def unit(projected, columns):
    leading = jnp.where(lanes_of(projected.shape) < columns, projected, 0.0)
    inverse = lax.rsqrt(jnp.sum(leading * leading, axis=-1, keepdims=True) + vector_eps)
    return leading, inverse, (leading * inverse).astype(BF)


def unit_back(leading, inverse, grad):
    along = jnp.sum(leading * grad, axis=-1, keepdims=True)
    return grad * inverse - leading * (along * (inverse * inverse * inverse))


def exact(left, right):
    return lax.dot_general(
        left,
        right,
        (((1,), (0,)), ((), ())),
        precision=lax.Precision.HIGHEST,
        preferred_element_type=F32,
    )


def maxsim_kernel(
    n_dp,
    n_fs,
    pq_ref,
    pd_ref,
    mask_ref,
    label_ref,
    loss_ref,
    dq_ref,
    dd_ref,
    all_ref,
    power_ref,
    part_ref,
    score_ref,
    grad_ref,
    first_ref,
    total_ref,
    second_ref,
    *sems,
):
    tokens = n_dp * n_fs * QLEN
    blocks = tokens // token_block
    spots = label_ref.shape[1]
    my_dp, my_fs = lax.axis_index("dp"), lax.axis_index("fsdp")
    over = [
        Exchange(axis, n_dp if axis == "dp" else n_fs, sems[2 * i], sems[2 * i + 1])
        for i, axis in enumerate(("dp", "fsdp", "fsdp", "dp", "fsdp", "dp"))
    ]
    greet({"dp": n_dp, "fsdp": n_fs})

    own = all_ref.at[my_fs, my_dp]
    all_ref[my_fs, my_dp] = pq_ref[...]
    over[0].start(lambda partner: own, lambda offset: own)
    docs = [unit(pd_ref[...], columns) for columns in widths]
    over[0].arrived()
    over[1].start(lambda partner: all_ref.at[my_fs], lambda offset: all_ref.at[my_fs])
    over[1].arrived()

    def queries(block):
        every = all_ref[...].reshape(tokens, PROJ)
        return every[block * token_block : (block + 1) * token_block]

    def powers(index, block):
        similar = dot_nt(docs[index][2], unit(queries(block), widths[index])[2])
        return jnp.exp2(similar * (log2e / smooth_temp)) * mask_ref[:, :1]

    mine = part_ref.at[my_fs]
    part_ref[my_fs] = jnp.ones((8, tokens), F32)
    for block in range(blocks):
        here = slice(block * token_block, (block + 1) * token_block)
        for index in range(3):
            power = powers(index, block)
            if blocks == 1:
                power_ref[index] = power
            part_ref[my_fs, index : index + 1, here] = column_sum(power)
    over[2].start(lambda partner: mine, lambda offset: mine)
    over[2].arrived()
    total = part_ref[0]
    for source in range(1, n_fs):
        total = total + part_ref[source]

    token_of = lax.broadcasted_iota(jnp.int32, (tokens, spots), 0) // QLEN
    pool = jnp.where(token_of == lanes_of((tokens, spots)), 1.0, 0.0)
    score = exact(jnp.log(total), pool) * (smooth_temp / QLEN)
    score_ref[my_dp] = score
    row = score_ref.at[my_dp]
    over[3].start(lambda partner: row, lambda offset: row)
    over[3].arrived()
    logits = score_ref[...] * (1.0 / loss_temp)
    largest = jnp.max(logits, axis=0)
    log_sum = largest + jnp.log(jnp.sum(jnp.exp(logits - largest[None]), axis=0))
    label = label_ref[...]
    picked = jnp.zeros_like(log_sum)
    for index in range(n_dp):
        picked += jnp.where(label == index, logits[index], 0.0)
    loss_ref[...] = log_sum - picked
    dscore = jnp.exp(score * (1.0 / loss_temp) - log_sum) - jnp.where(label == my_dp, 1.0, 0.0)
    query_of = lax.broadcasted_iota(jnp.int32, (spots, tokens), 0)
    spread = jnp.where(lanes_of((spots, tokens)) // QLEN == query_of, 1.0, 0.0)
    factor = exact(dscore * (1.0 / (loss_temp * QLEN)), spread) / total

    grad_doc = [jnp.zeros(pd_ref.shape, F32)] * 3
    for block in range(blocks):
        here = slice(block * token_block, (block + 1) * token_block)
        grad_query = jnp.zeros((token_block, PROJ), F32)
        for index, columns in enumerate(widths):
            leading, inverse, vector = unit(queries(block), columns)
            power = power_ref[index] if blocks == 1 else powers(index, block)
            dsim = (power * factor[index : index + 1, here]).astype(BF)
            turned = dot_nn(docs[index][2].T, dsim).T
            grad_query += unit_back(leading, inverse, turned)
            grad_doc[index] += dot_nn(dsim, vector)
        if blocks == 1:
            grad_ref[...] = grad_query.reshape(grad_ref.shape)
        else:
            flat = block * token_block // QLEN
            count = token_block // QLEN
            grad_ref[flat // n_dp, flat % n_dp : flat % n_dp + count] = grad_query.reshape(
                count, QLEN, PROJ
            )
    over[4].start(lambda partner: grad_ref.at[partner], lambda offset: first_ref.at[offset - 1])
    dd = jnp.zeros(pd_ref.shape, F32)
    for index in range(3):
        dd += unit_back(docs[index][0], docs[index][1], grad_doc[index])
    dd_ref[...] = dd.astype(BF)
    over[4].arrived()
    summed = grad_ref[my_fs]
    for offset in range(n_fs - 1):
        summed = summed + first_ref[offset]
    total_ref[...] = summed
    over[5].start(lambda partner: total_ref.at[partner], lambda offset: second_ref.at[offset - 1])
    over[5].arrived()
    dq = total_ref[my_dp]
    for offset in range(n_dp - 1):
        dq = dq + second_ref[offset]
    dq_ref[...] = dq.astype(BF)
    for exchange in over:
        exchange.sent()


def maxsim(proj_query, proj_doc, doc_allowed, labels):
    n_dp, n_fs = lax.axis_size("dp"), lax.axis_size("fsdp")
    query_total = n_dp * n_fs
    tokens = query_total * QLEN
    blocks = tokens // token_block
    spots = -(-query_total // LANES) * LANES
    doc_rows = proj_doc.shape[0]
    ordered = jnp.transpose(labels).reshape(1, query_total)
    ordered = jnp.pad(ordered, ((0, 0), (0, spots - query_total)), constant_values=-1)
    mask = jnp.broadcast_to(doc_allowed[:, None], (doc_rows, LANES)).astype(F32)
    dma = lambda axis: [pltpu.SemaphoreType.DMA(((n_dp if axis == "dp" else n_fs) - 1,))] * 2
    whole = pl.BlockSpec(memory_space=pltpu.VMEM)
    loss, grad_query, grad_doc = pl.pallas_call(
        functools.partial(maxsim_kernel, n_dp, n_fs),
        in_specs=[whole] * 4,
        out_specs=[whole] * 3,
        out_shape=[
            jax.ShapeDtypeStruct((8, spots), F32),
            jax.ShapeDtypeStruct((QLEN, PROJ), BF),
            jax.ShapeDtypeStruct((doc_rows, PROJ), BF),
        ],
        scratch_shapes=[
            pltpu.VMEM((n_fs, n_dp, QLEN, PROJ), F32),
            pltpu.VMEM((3, doc_rows, token_block) if blocks == 1 else (3, 8, LANES), F32),
            pltpu.VMEM((n_fs, 8, tokens), F32),
            pltpu.VMEM((n_dp, 8, spots), F32),
            pltpu.VMEM((n_fs, n_dp, QLEN, PROJ), F32),
            pltpu.VMEM((n_fs - 1, n_dp, QLEN, PROJ), F32),
            pltpu.VMEM((n_dp, QLEN, PROJ), F32),
            pltpu.VMEM((n_dp - 1, QLEN, PROJ), F32),
        ]
        + [sem for axis in ("dp", "fsdp", "fsdp", "dp", "fsdp", "dp") for sem in dma(axis)],
        compiler_params=params(collective_id=1, has_side_effects=True),
        name="maxsim",
    )(proj_query, proj_doc, mask, jnp.broadcast_to(ordered, (8, spots)))
    losses = loss[:3, :query_total].reshape(3, n_fs, n_dp).transpose(0, 2, 1)
    return losses.reshape(3, query_total), grad_query, grad_doc


def other_core(parts):
    return [(part, part ^ 1) for part in range(parts)]


def other_chip(parts):
    return [(part, part ^ 2) for part in range(parts)]


def shards(
    doc_tokens,
    query_tokens,
    doc_lengths,
    labels,
    query_weight,
    query_bias,
    key_weight,
    key_bias,
    value_weight,
    value_bias,
    out_weight,
    out_bias,
    first_gain,
    first_shift,
    inner_weight,
    inner_bias,
    outer_weight,
    outer_bias,
    second_gain,
    second_shift,
    vector_weight,
):
    parts = lax.axis_size("fsdp")
    mine = lax.axis_index("fsdp")
    doc_rows = doc_tokens.shape[1]
    rows = doc_rows + QLEN
    width = D // parts
    split = query_weight.shape[0]

    w_split = jnp.stack(
        [
            jnp.concatenate(
                [
                    entry[:, part * width : (part + 1) * width]
                    for entry in (query_weight, key_weight, value_weight)
                ],
                axis=1,
            )
            for part in range(parts)
        ]
    )
    small = [
        query_bias,
        key_bias,
        value_bias,
        out_bias,
        first_gain,
        first_shift,
        outer_bias,
        second_gain,
        second_shift,
    ]
    hidden_split = inner_bias.shape[0]
    line = [jnp.pad(entry.astype(F32), (0, LANES - split)) for entry in small]
    inner_rows = -(-hidden_split // LANES)
    padded = jnp.pad(inner_bias.astype(F32), (0, inner_rows * LANES - hidden_split))
    line += list(padded.reshape(inner_rows, LANES))
    line += [jnp.zeros((LANES,), F32)] * (-len(line) % 8)
    line = jnp.stack(line)
    doc_in, query_in = doc_tokens.reshape(doc_rows, D), query_tokens.reshape(QLEN, D)
    x_all, w_heads, packed = gather_start(doc_in, query_in, w_split, line)
    own_up = [outer_weight[group * split : (group + 1) * split] for group in range(GROUPS)]
    packed_own = jnp.concatenate(own_up + [inner_weight, out_weight, vector_weight], axis=1)
    packed_own, w_heads = lax.optimization_barrier((packed_own, w_heads))
    packed_w = lax.all_gather(packed_own, AXES, axis=0, tiled=True)
    packed_w = regrouped(packed_w, split, OWN_ROWS)
    x_all = gather_rest(doc_in, query_in, x_all)
    rows_in = jnp.concatenate([doc_in, query_in])
    w_heads = w_heads.reshape(D, 3 * width)
    packed = packed.reshape((lax.axis_size("dp") * parts,) + line.shape)

    def vector(index):
        return packed[:, index, :split].reshape(-1)

    inner_vec = packed[:, len(small) : len(small) + inner_rows].reshape(packed.shape[0], -1)
    inner_vec = inner_vec[:, :hidden_split].reshape(1, -1)
    vectors = jnp.stack([vector(i) for i in (3, 4, 5, 6, 7, 8)] + [jnp.zeros((D,), F32)] * 2)
    b_heads = jnp.concatenate(
        [lax.dynamic_slice(vector(i), (mine * width,), (width,)) for i in range(3)]
    ).reshape(1, -1)

    tables = rope_tables(parts, doc_rows)
    cosine, sine = jnp.asarray(tables[0]), jnp.asarray(tables[1])
    query, key, value = project_heads(
        doc_lengths, x_all, w_heads, b_heads, cosine, sine, doc_rows
    )
    mixed, mixed_full, query_log = attend(query, key, value, parts, doc_rows)
    att = lax.all_to_all(mixed, "fsdp", 0, 0, tiled=True)
    hat1, inv1, low1, act, slope, hat2, inv2, enc, proj = rows_forward(
        att, rows_in, packed_w, inner_vec, vectors
    )

    positions = mine * doc_rows + jnp.arange(doc_rows, dtype=jnp.int32)
    losses, grad_query, grad_doc = maxsim(
        proj[doc_rows:], proj[:doc_rows], positions < doc_lengths[0], labels
    )
    dproj = jnp.concatenate([grad_doc, grad_query])

    keep, send, dbi, datt, dsum, dvec = rows_backward(
        split == OWN_ROWS, dproj, enc, hat2, inv2, packed_w, act, slope, low1, hat1, inv1, att, vectors
    )
    grad_mixed = lax.all_to_all(datt, "fsdp", 0, 0, tiled=True)
    pair_args = (query_log, key, value, grad_mixed, mixed_full, cosine, sine)

    n_dp = lax.axis_size("dp")
    z, x = lax.axis_index("dp") // 2, lax.axis_index("dp") % 2
    core, y = mine % 2, mine // 2
    pick = lambda value, index, axis: lax.dynamic_index_in_dim(value, index, axis, False)
    if split != OWN_ROWS:
        every = jnp.stack([keep, send], axis=1).reshape(D, -1)
        every = regrouped(every, OWN_ROWS, split).reshape(-1, 2, split, keep.shape[2])
        keep, send = pick(every, core, 1), pick(every, 1 - core, 1)
    middle = keep.shape[2] // 2 // LANES * LANES
    n_z = n_dp // 2
    whole = (n_z, 2, 2, split, keep.shape[2])
    across = [(d, d ^ 1) for d in range(n_dp)]
    add = lambda one, two: one.astype(F32) + two.astype(F32)
    keep = keep.reshape(whole)
    from_core = lax.ppermute(send, "fsdp", other_core(parts)).reshape(whole)
    left, right = slice(0, middle), slice(middle, None)
    sum_left = add(keep[..., left], from_core[..., left])
    sum_right = add(keep[..., right], from_core[..., right])
    out_x = pick(sum_left, 1 - x, 1).astype(BF)
    out_y = pick(sum_right, 1 - y, 2).astype(BF)
    out_x, out_y, *pair_args = lax.optimization_barrier((out_x, out_y) + pair_args)
    left_x = lax.ppermute(out_x, "dp", across)
    right_y = lax.ppermute(out_y, "fsdp", other_chip(parts))
    calls = [list(attend_back(0, (0, 1), *pair_args, doc_rows))]
    left_x, right_y, calls[0][0] = lax.optimization_barrier((left_x, right_y, calls[0][0]))
    sum_left = add(pick(sum_left, x, 1), left_x)
    sum_right = add(pick(sum_right, y, 2), right_y)
    out_y = pick(sum_left, 1 - y, 1).astype(BF)
    out_x = pick(sum_right, 1 - x, 1).astype(BF)
    out_x, out_y, calls[0][0], *pair_args = lax.optimization_barrier(
        (out_x, out_y, calls[0][0], *pair_args)
    )
    left_y = lax.ppermute(out_y, "fsdp", other_chip(parts))
    right_x = lax.ppermute(out_x, "dp", across)
    calls.append(list(attend_back(1, (0,), *pair_args, doc_rows)))
    left_y, right_x, calls[1][0] = lax.optimization_barrier((left_y, right_x, calls[1][0]))
    grads_own = jnp.concatenate(
        [add(pick(sum_left, y, 1), left_y), add(pick(sum_right, x, 1), right_x)], axis=-1
    )
    bits = n_z.bit_length() - 1
    for bit in range(bits):
        grads_own = grads_own.reshape(-1, 2, split, grads_own.shape[-1])
        mine_bit = z // 2**bit % 2
        out_z = pick(grads_own, 1 - mine_bit, 1).astype(BF)
        if bit == 0:
            out_z, calls[1][0], *pair_args = lax.optimization_barrier(
                (out_z, calls[1][0], *pair_args)
            )
        along = [(d, d ^ (2 << bit)) for d in range(n_dp)]
        from_z = lax.ppermute(out_z, "dp", along)
        if bit == 0:
            calls.append(list(attend_back(1, (1,), *pair_args, doc_rows)))
            from_z, calls[2][0] = lax.optimization_barrier((from_z, calls[2][0]))
        grads_own = add(pick(grads_own, mine_bit, 1), from_z)
    grads_own = grads_own.reshape(split, -1)

    place = jnp.arange(parts, dtype=jnp.int32)[None, :, None] == mine
    db = jnp.stack(
        [jnp.concatenate([calls[0][3][i], calls[1][3][i] + calls[2][3][i]]) for i in range(3)]
    )
    db_all = jnp.where(place, db[:, None, :], 0.0).reshape(3, D)
    vector_grads = jnp.concatenate([db_all, dvec[:6]]).reshape(9, -1, split).transpose(1, 0, 2)
    vector_grads = jnp.concatenate(
        [vector_grads.reshape(-1, 9 * split), dbi.reshape(-1, hidden_split)], axis=1
    )
    used = vector_grads.shape[1]
    vector_grads = jnp.pad(vector_grads, ((0, 0), (0, -used % (8 * LANES))))
    vector_grads = vector_grads.reshape(n_dp, parts, 8, -1).transpose(1, 0, 2, 3)
    grad_low, dw, summed = heads_backward(
        x_all,
        w_heads,
        dsum,
        vector_grads,
        (0, 1, 1),
        [entry for call in calls for entry in call[:3]],
    )
    dw_own = dw.reshape(parts, split, 3, width).transpose(2, 1, 0, 3).reshape(3, split, D)
    summed = summed.reshape(-1)
    up_own = jnp.concatenate([grads_own[:, i * D : (i + 1) * D] for i in range(GROUPS)])
    hidden = GROUPS * D
    dwi_own = grads_own[:, hidden : 2 * hidden]
    dwo_own = grads_own[:, 2 * hidden : 2 * hidden + D]
    dwv_own = grads_own[:, 2 * hidden + D :]
    vec_own = [summed[index * split : (index + 1) * split] for index in range(9)]
    dbi_own = summed[9 * split : 9 * split + hidden_split]
    return (
        losses,
        enc[:doc_rows].reshape(1, doc_rows, D),
        enc[doc_rows:].reshape(1, 1, QLEN, D),
        grad_low[:doc_rows].reshape(1, doc_rows, D),
        grad_low[doc_rows:].reshape(1, 1, QLEN, D),
        dw_own[0],
        vec_own[0],
        dw_own[1],
        vec_own[1],
        dw_own[2],
        vec_own[2],
        dwo_own,
        vec_own[3],
        vec_own[4],
        vec_own[5],
        dwi_own,
        dbi_own,
        up_own,
        vec_own[6],
        vec_own[7],
        vec_own[8],
        dwv_own,
    )


def solution(mesh):
    rows = P(AXES, None)
    line = P(AXES)
    doc = P("dp", "fsdp", None)
    query = P("dp", "fsdp", None, None)
    weights = (rows, line) * 4 + (line, line, rows, line, rows, line, line, line, rows)
    return jax.shard_map(
        shards,
        mesh=mesh,
        in_specs=(doc, query, P("dp"), P()) + weights,
        out_specs=(P(), doc, query, doc, query) + weights,
        check_vma=False,
    )
```
